32 devices in a mesh: gx: 4 (over z), gy: 8 (over y, x, core).
Axes of the slice: x: 2, y: 2, z: 4, core: 2. Of those that a mesh axis runs over, the one named last changes fastest.
Arguments:
- table: float32 [262144, 128], P(('gx', 'gy')), may hold values from -6 to 6
- accum: float32 [262144], P(('gx', 'gy')), may hold values from 0.05 to 1
- cache_values: float32 [131072, 128], P(('gx', 'gy')), may hold values from -6 to 6
- cache_rows: int32 [131072], P(('gx', 'gy')), may hold values from 0 to 262143, as said below
- pending: float32 [131072, 128], P(('gx', 'gy')), may hold values from -3 to 3
- batch_slots: int32 [3, 16384, 16], P(None, ('gx', 'gy')), may hold values from 0 to 4095
- targets: float32 [3, 16384, 128], P(None, ('gx', 'gy')), may hold values from -6 to 6
- dirty: int32 [3, 16384], P(None, ('gx', 'gy')), may hold values from 0 to 4095, as said below
Outputs:
- new_table: float32 [262144, 128], P(('gx', 'gy'))
- new_accum: float32 [262144], P(('gx', 'gy'))
- new_cache: float32 [131072, 128], P(('gx', 'gy'))
- new_pending: float32 [131072, 128], P(('gx', 'gy'))
The draws below stay inside these ranges and needn't reach their ends.
Inputs may be any that keep to these rules, and one draw needn't show every extreme that they name: `cache_rows`: each device's slots form 32 blocks of 128 consecutive slots; every block holds rows of one owner, and every owner has exactly one block on every device. `dirty`: in each step a device's 512 entries are distinct slots of that device; at most 32 of them hold rows of one owner, and in every step some owner gets exactly 32 from every device.
All inputs are finite; a program needn't handle non-finite values.
Results may differ from the reference program's by a relative error of at most 0.0001.
Values sent between devices are 32-bit elements; how exact they have to be, the bound alone decides.
No kernel may reach another device: no remote copies, remote signals or barrier semaphores. Data moves between devices by JAX's collectives and lax.ppermute only.
A program may use at most 128 MiB of HBM per device.

```python
import math
import jax
import jax.numpy as jnp
from jax import lax

W = 128
ROWS_DEV = 8192
CACHE = 4096
B_DEV = 512
BAG = 16
DIRTY = 512
STEPS = 3
DEVICES = 32


def owner_places(key):
    keys = jax.random.split(jax.random.fold_in(key, 101), DEVICES)
    return jax.vmap(lambda single: jax.random.permutation(single, DEVICES))(keys)


def draw_cache_rows(key, part):
    places = owner_places(key)
    per_block = CACHE // DEVICES
    block_owner = jnp.argsort(places, axis=1).astype(jnp.int32)
    local = jax.random.randint(jax.random.fold_in(key, 202), (DEVICES, DEVICES, per_block), 0, ROWS_DEV)
    holders = block_owner[:, :, None] * ROWS_DEV + local
    return holders.reshape(-1).astype(jnp.int32)


def dirty_step(key, places, step):
    per_block = CACHE // DEVICES
    capacity = 2 * DIRTY // DEVICES
    half = capacity // 2
    step_key = jax.random.fold_in(key, 300 + step)
    pairing = jax.random.permutation(jax.random.fold_in(step_key, 1), DEVICES)
    moves = jax.random.randint(jax.random.fold_in(step_key, 2), (DEVICES, DEVICES // 2), half // 2, half + 1)
    moves = moves.at[:, 0].set(half)
    counts = jnp.full((DEVICES, DEVICES), half, jnp.int32)
    counts = counts.at[:, pairing[0::2]].add(moves)
    counts = counts.at[:, pairing[1::2]].add(-moves)
    offsets = jax.random.randint(jax.random.fold_in(step_key, 3), (DEVICES, DEVICES), 0, per_block)
    within = jnp.arange(per_block, dtype=jnp.int32)
    chosen = within[None, None, :] < counts[:, :, None]
    slots = places[:, :, None] * per_block + (within[None, None, :] + offsets[:, :, None]) % per_block
    shuffle_keys = jax.random.split(jax.random.fold_in(step_key, 4), DEVICES)
    shuffles = jax.vmap(lambda single: jax.random.permutation(single, DEVICES * per_block))(shuffle_keys)
    scores = jnp.where(chosen.reshape(DEVICES, -1), 0, DEVICES * per_block) + shuffles
    order = jnp.argsort(scores, axis=1)[:, :DIRTY]
    return jnp.take_along_axis(slots.reshape(DEVICES, -1), order, axis=1)


def draw_dirty(key, part):
    places = owner_places(key)
    listed = jnp.stack([dirty_step(key, places, step) for step in range(STEPS)])
    return listed.reshape(STEPS, DEVICES * DIRTY).astype(jnp.int32)


def set_ends(values, stream_key, smallest, top_value):
    longest = values.shape.index(max(values.shape))
    spots = []
    for shift in (0, 1):
        where = [jax.random.randint(jax.random.fold_in(stream_key, axis), (), 0, length) for axis, length in enumerate(values.shape)]
        where[longest] = (where[longest] + shift) % values.shape[longest]
        spots.append(tuple(where))
    return values.at[spots[0]].set(smallest).at[spots[1]].set(top_value)


def steps_of(stream_key, shape, cuts, smallest, top_value):
    level = 1.0
    for position, shards_of in cuts:
        heights = jax.random.uniform(jax.random.fold_in(jax.random.fold_in(stream_key, 6), position), (shards_of,), jnp.float32, smallest / len(cuts), top_value / len(cuts))
        level = level * jnp.repeat(jnp.exp(heights), shape[position] // shards_of).reshape((-1,) + (1,) * (len(shape) - 1 - position))
    return level


def scatter_about(own_key, extent, deviation, most, cuts=(), kind=jnp.bfloat16):
    array = deviation * jax.random.normal(own_key, extent, jnp.float32)
    if cuts:
        array = array * steps_of(own_key, extent, cuts, -0.22, 0.18)
    return jnp.clip(array, -most, most).astype(kind)


def setup_inputs(seed: int = 0) -> dict:
    key_list = jax.random.split(jax.random.key(seed), 9)
    return {
        "table": scatter_about(key_list[0], (ROWS_DEV * DEVICES, W), 1.0, 6.0, ((0, 32),), jnp.float32),
        "accum": jnp.clip(jnp.exp(math.log(1.0) - 2.9957323 * jax.random.uniform(key_list[1], (ROWS_DEV * DEVICES,), jnp.float32) ** steps_of(key_list[1], (ROWS_DEV * DEVICES,), ((0, 32),), -0.2, 0.2)), 0.05, 1.0),
        "cache_values": scatter_about(key_list[2], (CACHE * DEVICES, W), 1.0, 6.0, ((0, 32),), jnp.float32),
        "cache_rows": draw_cache_rows(jax.random.fold_in(key_list[8], 71), 0),
        "pending": scatter_about(key_list[4], (CACHE * DEVICES, W), 0.3, 3.0, ((0, 32),), jnp.float32),
        "batch_slots": set_ends(jax.random.randint(key_list[5], (STEPS, B_DEV * DEVICES, BAG), 0, CACHE), jax.random.fold_in(key_list[5], 1), 0, CACHE - 1).astype(jnp.int32),
        "targets": scatter_about(key_list[6], (STEPS, B_DEV * DEVICES, W), 1.0, 6.0, ((1, 32),), jnp.float32),
        "dirty": draw_dirty(jax.random.fold_in(key_list[8], 71), 0),
    }


LEARN_RATE = 0.3

def local_grad(values, ids, goal):
    pooled = lax.optimization_barrier(jnp.mean(jnp.take(values, ids, axis=0), axis=1))
    bag_grad = (pooled - goal) / BAG
    spread = jnp.broadcast_to(bag_grad[:, None, :], (B_DEV, BAG, W)).reshape(-1, W)
    return jax.ops.segment_sum(spread, ids.reshape(-1), num_segments=CACHE)

def reference(table, accum, cache_values, cache_rows, pending, batch_slots, targets, dirty):
    cached = cache_values.reshape(DEVICES, CACHE, W)
    waiting = pending.reshape(DEVICES, CACHE, W)
    holders = cache_rows.reshape(DEVICES, CACHE)
    for step in range(STEPS):
        picks = batch_slots[step].reshape(DEVICES, B_DEV, BAG)
        wanted = targets[step].reshape(DEVICES, B_DEV, W)
        grads = lax.map(lambda item: local_grad(item[0], item[1], item[2]), (cached, picks, wanted))
        waiting = waiting + grads
        listed = dirty[step].reshape(DEVICES, DIRTY)
        flushed = jnp.take_along_axis(waiting, listed[:, :, None], axis=1)
        chosen_rows = jnp.take_along_axis(holders, listed, axis=1)
        table_grad = jnp.zeros_like(table).at[chosen_rows.reshape(-1)].add(flushed.reshape(-1, W))
        waiting = jax.vmap(lambda block, where: block.at[where].set(0.0))(waiting, listed)
        accum = accum + lax.optimization_barrier(jnp.mean(table_grad * table_grad, axis=1))
        table = table - LEARN_RATE * table_grad / jnp.sqrt(accum)[:, None]
        fresh = jnp.take(table, chosen_rows.reshape(-1), axis=0).reshape(DEVICES, DIRTY, W)
        cached = jax.vmap(lambda block, where, value: block.at[where].set(value))(cached, listed, fresh)
    return (table, accum, cached.reshape(-1, W), waiting.reshape(-1, W))
```

```python
import functools

import jax
import jax.numpy as jnp
from jax import lax
from jax.experimental import pallas as pl
from jax.experimental.pallas import tpu as pltpu
from jax.sharding import PartitionSpec as P

LEARN_RATE = 0.3
AXES = ("gx", "gy")
F32, BF16, I32 = jnp.float32, jnp.bfloat16, jnp.int32
LANES = 128
VMEM = pl.BlockSpec(memory_space=pltpu.VMEM)
SMEM = pl.BlockSpec(memory_space=pltpu.SMEM)


def call(body, outs, scratch=(), flops=0, nbytes=0, smem=(), n_in=0, vmem=40, aliases=None, name=None):
    return pl.pallas_call(
        body,
        out_shape=tuple(jax.ShapeDtypeStruct(shape, dtype) for shape, dtype in outs),
        in_specs=[SMEM if i in smem else VMEM for i in range(n_in)],
        out_specs=tuple(VMEM for _ in outs),
        scratch_shapes=list(scratch),
        input_output_aliases=aliases or {},
        compiler_params=pltpu.CompilerParams(vmem_limit_bytes=vmem * 2**20),
        cost_estimate=pl.CostEstimate(flops=flops, bytes_accessed=nbytes, transcendentals=0),
        name=name,
    )


def log2(value):
    assert value & (value - 1) == 0
    return value.bit_length() - 1


def iota(shape, dim):
    return lax.broadcasted_iota(I32, shape, dim)


def one(mask):
    return jnp.where(mask, 1.0, 0.0).astype(BF16)


def split2(x):
    top = x.astype(BF16)
    rest = (x - top.astype(F32)).astype(BF16)
    return jnp.concatenate([top, rest], axis=-1)


def split3(x):
    top = x.astype(BF16)
    rest = x - top.astype(F32)
    middle = rest.astype(BF16)
    last = (rest - middle.astype(F32)).astype(BF16)
    return jnp.concatenate([top, middle, last], axis=-1)


def dot(a, b):
    return lax.dot_general(a, b, (((1,), (0,)), ((), ())), preferred_element_type=F32)


def dot_nt(a, b):
    return lax.dot_general(a, b, (((1,), (1,)), ((), ())), preferred_element_type=F32)


def dot_tn(a, b):
    return lax.dot_general(a, b, (((0,), (0,)), ((), ())), preferred_element_type=F32)


def fold(x, parts):
    width = x.shape[-1] // parts
    total = x[..., (parts - 1) * width :]
    for part in reversed(range(parts - 1)):
        total = total + x[..., part * width : (part + 1) * width]
    return total


class Sizes:
    def __init__(self, devices, rows, slots, width, steps, bags, lookups, listed):
        self.devices, self.rows, self.slots, self.width = devices, rows, slots, width
        self.steps, self.bags, self.lookups, self.listed = steps, bags, lookups, listed
        self.cap = 2 * listed // devices
        self.places = devices * self.cap
        self.block = slots // devices
        self.chunks = self.places // LANES
        self.chunk = slots // self.chunks
        self.group = 256 // lookups
        self.groups = bags // self.group
        self.tiles = slots // LANES
        assert width == LANES and self.cap % 8 == 0 and self.chunk % self.block == 0
        assert self.groups * self.group == bags and self.group % 16 == 0


def place_kernel(z, dirty_ref, rows_ref, place_ref, index_ref):
    earlier = iota((z.chunk, z.chunk), 0)
    later = iota((z.chunk, z.chunk), 1)
    shift = log2(z.block)
    before = one((earlier < later) & ((earlier >> shift) == (later >> shift)))
    local = rows_ref[...] & (z.rows - 1)
    for t in range(z.steps):
        listed = dirty_ref[t : t + 1, :]
        high, low = listed >> log2(z.chunk), listed & (z.chunk - 1)
        chosen_high = one(iota((z.chunks, z.listed), 0) == high)
        chosen_low = one(iota((z.chunk, z.listed), 0) == low)
        chosen = dot_nt(chosen_high, chosen_low)
        rank = dot(chosen.astype(BF16), before)
        base = ((iota((z.chunks, z.chunk), 1) >> shift) * z.cap).astype(F32)
        place = jnp.where(chosen > 0.5, base + rank, -1.0)
        place_ref[t * z.chunks : (t + 1) * z.chunks, :] = place
        for c in range(z.chunks):
            pick = pick_of(z, place[c : c + 1, :])
            row = local[c : c + 1, :]
            parts = jnp.where(iota((8, z.chunk), 0) == 0, row >> 7, row & 127).astype(F32).astype(BF16)
            found = dot_nt(parts, pick)
            index = found[0:1, :] * 128.0 + found[1:2, :]
            index_ref[t * z.chunks + c : t * z.chunks + c + 1, :] = index.astype(I32)


def pick_of(z, place_row):
    return one(iota((LANES, z.chunk), 0).astype(F32) == place_row)


def count_into(z, ids, count_ref, key_ref, low_ref):
    lanes = z.group * z.lookups
    spread = one((iota((z.lookups, lanes), 1) & (z.lookups - 1)) == iota((z.lookups, lanes), 0))
    bag_of_lane = iota((z.bags, lanes), 1) >> log2(z.lookups)
    mine = bag_of_lane == (iota((z.bags, lanes), 0) & (z.group - 1))
    high = dot((ids >> 7).astype(F32).astype(BF16), spread)
    low = dot((ids & 127).astype(F32).astype(BF16), spread)
    key = high * z.group + bag_of_lane.astype(F32)
    key_ref[...] = jnp.sum(jnp.where(mine, key, 0.0).reshape(z.groups, z.group, lanes), axis=1)
    low_ref[...] = jnp.sum(jnp.where(mine, low, 0.0).reshape(z.groups, z.group, lanes), axis=1)

    def step(g, carry):
        key_row = key_ref[pl.ds(g, 1), :].astype(I32)
        low_row = low_ref[pl.ds(g, 1), :].astype(I32)
        left = one(iota((z.tiles * z.group, lanes), 0) == key_row)
        right = one(iota((LANES, lanes), 0) == low_row)
        counts = dot_nt(left, right).astype(BF16)
        start = pl.multiple_of(g * z.group, z.group)
        for h in range(z.tiles):
            count_ref[pl.ds(start, z.group), h * LANES : (h + 1) * LANES] = counts[
                h * z.group : (h + 1) * z.group, :
            ]
        return carry

    lax.fori_loop(0, z.groups, step, 0, unroll=2)


def count_scratch(z):
    lanes = z.group * z.lookups
    return [pltpu.VMEM((z.groups, lanes), F32), pltpu.VMEM((z.groups, lanes), F32)]


def to_owners(z, values_ref, owner_ref, out_ref):
    for b in range(z.devices):
        start = pl.multiple_of(owner_ref[b] * z.cap, z.cap)
        out_ref[pl.ds(start, z.cap), :] = values_ref[b * z.cap : (b + 1) * z.cap, :]


def from_owners(z, back_ref, owner_ref, out_ref):
    for b in range(z.devices):
        start = pl.multiple_of(owner_ref[b] * z.cap, z.cap)
        out_ref[b * z.cap : (b + 1) * z.cap, :] = back_ref[pl.ds(start, z.cap), :]


def pooled_total(z, count_ref, values_ref):
    total = jnp.zeros((z.bags, 2 * z.width), F32)
    for c in range(z.chunks):
        part = slice(c * z.chunk, (c + 1) * z.chunk)
        total = total + dot(count_ref[:, part], split2(values_ref[part, :]))
    return fold(total, 2)


def first_kernel(z, owner_ref, ids_ref, targets_ref, cache_ref, pending_ref, place_ref,
                 count_ref, grad_ref, out_ref, key_ref, low_ref, flush_ref):
    count_into(z, ids_ref[0], count_ref, key_ref, low_ref)
    pooled = pooled_total(z, count_ref, cache_ref) * (1.0 / z.lookups)
    grad = split2((pooled - targets_ref[0]) * (1.0 / z.lookups))
    grad_ref[...] = grad
    for c in range(z.chunks):
        part = slice(c * z.chunk, (c + 1) * z.chunk)
        pick = pick_of(z, place_ref[c : c + 1, :])
        lookups = dot_nt(pick, count_ref[:, part]).astype(BF16)
        flush_ref[c * LANES : (c + 1) * LANES, :] = fold(dot(pick, split3(pending_ref[part, :])), 3) + fold(
            dot(lookups, grad), 2
        )
    to_owners(z, flush_ref, owner_ref, out_ref)


def count_kernel(z, t, ids_ref, place_ref, count_ref, back_ref, flush_ref, key_ref, low_ref):
    count_into(z, ids_ref[t], count_ref, key_ref, low_ref)
    for c in range(z.chunks):
        part = slice(c * z.chunk, (c + 1) * z.chunk)
        counts = count_ref[:, part]
        before = (t - 1) * z.chunks + c
        back_ref[:, c * LANES : (c + 1) * LANES] = dot_nt(
            counts, pick_of(z, place_ref[before : before + 1, :])
        ).astype(BF16)
        now = t * z.chunks + c
        flush_ref[c * LANES : (c + 1) * LANES, :] = dot_nt(
            pick_of(z, place_ref[now : now + 1, :]), counts
        ).astype(BF16)


def keep_of(z, pick):
    return 1.0 - dot_tn(pick, jnp.ones((LANES, LANES), BF16))


def pending_kernel(z, t, last, count_ref, grad_ref, place_ref, pending_ref, *out_refs):
    new_ref = out_refs[0]
    for c in range(z.chunks):
        part = slice(c * z.chunk, (c + 1) * z.chunk)
        now = t * z.chunks + c
        pick = pick_of(z, place_ref[now : now + 1, :])
        added = fold(dot_tn(count_ref[:, part], grad_ref[...]), 2)
        value = (pending_ref[part, :] + added) * keep_of(z, pick)
        new_ref[part, :] = value
        if not last:
            pick = pick_of(z, place_ref[now + z.chunks : now + z.chunks + 1, :])
            out_refs[1][c * LANES : (c + 1) * LANES, :] = fold(dot(pick, split3(value)), 3)


def first_cache_kernel(z, count_ref, place_ref, cache_ref, total_ref):
    total = jnp.zeros((z.bags, 2 * z.width), F32)
    for c in range(z.chunks):
        part = slice(c * z.chunk, (c + 1) * z.chunk)
        pick = pick_of(z, place_ref[c : c + 1, :])
        total = total + dot(count_ref[:, part], split2(cache_ref[part, :] * keep_of(z, pick)))
    total_ref[...] = fold(total, 2)


def cache_kernel(z, t, masked, last, owner_ref, back_ref, place_ref, cache_ref, count_ref, new_ref, *rest):
    total_ref = None if last else rest[0]
    order_ref = rest[-1]
    from_owners(z, back_ref, owner_ref, order_ref)
    total = jnp.zeros((z.bags, 2 * z.width), F32)
    for c in range(z.chunks):
        part = slice(c * z.chunk, (c + 1) * z.chunk)
        now = t * z.chunks + c
        pick = pick_of(z, place_ref[now : now + 1, :])
        value = cache_ref[part, :]
        if not masked:
            value = value * keep_of(z, pick)
        value = value + fold(dot_tn(pick, split3(order_ref[c * LANES : (c + 1) * LANES, :])), 3)
        pick = pick_of(z, place_ref[now + z.chunks : now + z.chunks + 1, :])
        value = value * keep_of(z, pick)
        new_ref[part, :] = value
        if not last:
            total = total + dot(count_ref[:, part], split2(value))
    if not last:
        total_ref[...] = fold(total, 2)


def last_cache_kernel(z, owner_ref, back_ref, place_ref, cache_ref, new_ref, order_ref):
    t = z.steps - 1
    from_owners(z, back_ref, owner_ref, order_ref)
    for c in range(z.chunks):
        part = slice(c * z.chunk, (c + 1) * z.chunk)
        now = t * z.chunks + c
        pick = pick_of(z, place_ref[now : now + 1, :])
        new_ref[part, :] = cache_ref[part, :] + fold(
            dot_tn(pick, split3(order_ref[c * LANES : (c + 1) * LANES, :])), 3
        )


def step_kernel(z, t, owner_ref, back_ref, counts_ref, total_ref, targets_ref, flush_counts_ref, waiting_ref,
                grad_ref, out_ref, order_ref):
    from_owners(z, back_ref, owner_ref, order_ref)
    total = total_ref[...] + fold(dot(counts_ref[...], split2(order_ref[...])), 2)
    pooled = total * (1.0 / z.lookups)
    grad = split2((pooled - targets_ref[t]) * (1.0 / z.lookups))
    grad_ref[...] = grad
    order_ref[...] = waiting_ref[...] + fold(dot(flush_counts_ref[...], grad), 2)
    to_owners(z, order_ref, owner_ref, out_ref)


def column(row):
    return jnp.transpose(jnp.broadcast_to(row, (LANES, LANES)))


def same_kernel(z, index_ref, same_ref):
    pieces = z.places // LANES
    rows = [index_ref[c : c + 1, :].astype(F32) for c in range(pieces)]
    for i in range(pieces):
        col = column(rows[i])
        for j in range(pieces):
            same_ref[i * LANES : (i + 1) * LANES, j * LANES : (j + 1) * LANES] = one(col == rows[j])


def owner_kernel(z, got_ref, same_ref, old_ref, accum_ref, answer_ref, extra_ref):
    grad = fold(dot(same_ref[...], split2(got_ref[...])), 2)
    extra = jnp.mean(grad * grad, axis=1, keepdims=True)
    fresh = accum_ref[...] + extra
    extra_ref[...] = jnp.broadcast_to(extra, (z.places, LANES))
    answer_ref[...] = old_ref[...] - LEARN_RATE * grad / jnp.sqrt(fresh)


def gather_rows(z, index_ref, first, table_ref, out_ref):
    def step(g, carry):
        base = pl.multiple_of(g * 8, 8)
        for k in range(8):
            row = index_ref[first + base + k]
            out_ref[pl.ds(base + k, 1), :] = table_ref[pl.ds(row, 1), :]
        return carry

    lax.fori_loop(0, z.places // 8, step, 0, unroll=4)


def high_low(z, index_ref):
    highs, lows = [], []
    for c in range(z.places // LANES):
        col = column(index_ref[c : c + 1, :])
        lane = iota((LANES, LANES), 1)
        highs.append(col >> 7 == lane)
        lows.append(col & 127 == lane)
    return jnp.concatenate(highs, axis=0), jnp.concatenate(lows, axis=0)


def gather_accum(z, index_ref, accum_ref, out_ref):
    high, low = high_low(z, index_ref)
    tiles = fold(dot(one(high), split3(accum_ref[...])), 3)
    value = jnp.sum(jnp.where(low, tiles, 0.0), axis=1, keepdims=True)
    out_ref[...] = jnp.broadcast_to(value, (z.places, LANES))


def start_kernel(z, flat_ref, index_ref, table_ref, accum_ref, old_ref, old_accum_ref):
    gather_rows(z, flat_ref, 0, table_ref, old_ref)
    gather_accum(z, index_ref, accum_ref, old_accum_ref)


def table_kernel(z, t, last, flat_ref, index_ref, table_in, accum_in, answer_ref, extra_ref, *refs):
    table_ref, accum_ref = refs[0], refs[1]
    first = t * z.places
    table_ref[...] = table_in[...]

    def step(g, carry):
        base = pl.multiple_of(g * 8, 8)
        for k in range(8):
            row = flat_ref[first + base + k]
            table_ref[pl.ds(row, 1), :] = answer_ref[pl.ds(base + k, 1), :]
        return carry

    lax.fori_loop(0, z.places // 8, step, 0, unroll=4)
    pieces = z.places // LANES
    now = index_ref.at[t * pieces : (t + 1) * pieces]
    high, low = high_low(z, now)
    rows = [now[c : c + 1, :].astype(F32) for c in range(pieces)]
    total = accum_in[...]
    for i in range(pieces):
        part = slice(i * LANES, (i + 1) * LANES)
        col = column(rows[i])
        seen = jnp.zeros((LANES, LANES), F32)
        for j in range(i):
            seen = seen + jnp.where(col == rows[j], 1.0, 0.0)
        own = (col == rows[i]) & (iota((LANES, LANES), 1) < iota((LANES, LANES), 0))
        seen = seen + jnp.where(own, 1.0, 0.0)
        again = jnp.sum(seen, axis=1, keepdims=True)
        add = jnp.where(low[part] & (again < 0.5), extra_ref[part, :], 0.0)
        total = total + fold(dot_tn(one(high[part]), split3(add)), 3)
    accum_ref[...] = total
    if not last:
        gather_rows(z, flat_ref, first + z.places, table_ref, refs[2])
        gather_accum(z, index_ref.at[(t + 1) * pieces : (t + 2) * pieces], accum_ref, refs[3])


def body(table, accum, cache, cache_rows, pending, batch_slots, targets, dirty):
    z = Sizes(
        lax.axis_size(AXES), table.shape[0], cache.shape[0], cache.shape[1],
        batch_slots.shape[0], batch_slots.shape[1], batch_slots.shape[2], dirty.shape[1],
    )
    wide = (z.places, z.width)
    pieces = z.places // LANES
    owner = cache_rows.reshape(z.devices, z.block)[:, 0] >> log2(z.rows)
    place, index = call(
        functools.partial(place_kernel, z),
        [((z.steps * z.chunks, z.chunk), F32), ((z.steps * z.chunks, LANES), I32)],
        n_in=2, flops=10**9, nbytes=2**21, name="place",
    )(dirty, cache_rows.reshape(z.chunks, z.chunk))

    index = index.reshape(z.steps, z.devices, z.cap).transpose(1, 0, 2).reshape(z.devices, -1)
    to = owner[None, :] == jnp.arange(z.devices, dtype=I32)[:, None]
    index = jnp.sum(jnp.where(to[:, :, None], index[None], 0), axis=1)
    got_index = lax.all_to_all(index.reshape(z.devices, 1, -1), AXES, split_axis=0, concat_axis=0, tiled=True)
    got_index = got_index.reshape(z.devices, z.steps, z.cap).transpose(1, 0, 2)
    index = got_index.reshape(z.steps * pieces, LANES)
    flat = got_index.reshape(-1)

    def exchange(values):
        values = values.reshape(z.devices, z.cap, z.width)
        return lax.all_to_all(values, AXES, split_axis=0, concat_axis=0, tiled=True).reshape(wide)

    count_out = ((z.bags, z.slots), BF16)
    grad_out = ((z.bags, 2 * z.width), BF16)
    big = 2 * z.bags * z.slots * 2 * z.width
    rows = pltpu.VMEM(wide, F32)
    count, grad, outgoing = call(
        functools.partial(first_kernel, z), [count_out, grad_out, (wide, F32)],
        scratch=count_scratch(z) + [rows], smem=(0,), n_in=6, flops=6 * big, nbytes=2**24, name="first",
    )(owner, batch_slots, targets, cache, pending, place)

    old = old_accum = None
    accum = accum.reshape(z.rows // LANES, LANES)
    accum = jnp.pad(accum, ((0, LANES - z.rows // LANES), (0, 0))) if z.rows // LANES < LANES else accum
    masked = cache
    for t in range(z.steps):
        last = t == z.steps - 1
        got = exchange(outgoing)
        same = call(
            functools.partial(same_kernel, z), [((z.places, z.places), BF16)], n_in=1, flops=10**8, nbytes=2**21,
            name="same",
        )(index[t * pieces : (t + 1) * pieces])[0]
        if t == 0:
            old, old_accum = call(
                functools.partial(start_kernel, z), [(wide, F32), (wide, F32)], smem=(0,), n_in=4,
                flops=10**9, nbytes=2**23, name="start",
            )(flat, index, table, accum)
        outs = [((z.slots, z.width), F32)] + ([] if last else [(wide, F32)])
        done = call(
            functools.partial(pending_kernel, z, t, last), outs, n_in=4, flops=2 * big, nbytes=2**23, name="pending",
        )(count, grad, place, pending)
        pending = done[0]
        waiting = None if last else done[1]
        if not last:
            count, back_counts, flush_counts = call(
                functools.partial(count_kernel, z, t + 1),
                [count_out, ((z.bags, z.places), BF16), ((z.places, z.bags), BF16)],
                scratch=count_scratch(z), n_in=2, flops=4 * big, nbytes=2**23, name="count",
            )(batch_slots, place)
        if t == 0:
            total = call(
                functools.partial(first_cache_kernel, z), [((z.bags, z.width), F32)], n_in=3, flops=big,
                nbytes=2**23, name="first_cache",
            )(count, place, cache)[0]
        else:
            outs = [((z.slots, z.width), F32)] + ([] if last else [((z.bags, z.width), F32)])
            done = call(
                functools.partial(cache_kernel, z, t - 1, t > 1, last), outs, scratch=[rows], smem=(0,), n_in=5,
                flops=big, nbytes=2**23, name="cache",
            )(owner, back, place, masked, count)
            masked = done[0]
            total = None if last else done[1]
        answer, extra = call(
            functools.partial(owner_kernel, z), [(wide, F32), (wide, F32)], n_in=4, flops=10**9, nbytes=2**22,
            name="owner",
        )(got, same, old, old_accum)
        back = exchange(answer)
        outs = [(table.shape, F32), (accum.shape, F32)] + ([] if last else [(wide, F32), (wide, F32)])
        done = call(
            functools.partial(table_kernel, z, t, last), outs, smem=(0,), n_in=6, flops=10**9, nbytes=2**24,
            name="table",
        )(flat, index, table, accum, answer, extra)
        table, accum = done[0], done[1]
        if not last:
            old, old_accum = done[2], done[3]
            grad, outgoing = call(
                functools.partial(step_kernel, z, t + 1), [grad_out, (wide, F32)], scratch=[rows], smem=(0,), n_in=7,
                flops=10**9, nbytes=2**22, name="step",
            )(owner, back, back_counts, total, targets, flush_counts, waiting)
    cache = call(
        functools.partial(last_cache_kernel, z), [((z.slots, z.width), F32)], scratch=[rows], smem=(0,), n_in=4,
        flops=big, nbytes=2**23, name="last_cache",
    )(owner, back, place, masked)[0]
    return (table, accum[: z.rows // LANES].reshape(-1), cache, pending)


def solution(mesh):
    in_specs = (
        P(AXES, None),
        P(AXES),
        P(AXES, None),
        P(AXES),
        P(AXES, None),
        P(None, AXES, None),
        P(None, AXES, None),
        P(None, AXES),
    )
    out_specs = (P(AXES, None), P(AXES), P(AXES, None), P(AXES, None))
    return jax.shard_map(body, mesh=mesh, in_specs=in_specs, out_specs=out_specs, check_vma=False)
```

```python
import functools

import jax
import jax.numpy as jnp
from jax import lax
from jax.experimental import pallas as pl
from jax.experimental.pallas import tpu as pltpu
from jax.sharding import PartitionSpec as P

LEARN_RATE = 0.3
AXES = ("gx", "gy")
F32, BF16, I32 = jnp.float32, jnp.bfloat16, jnp.int32
LANES = 128
VMEM = pl.BlockSpec(memory_space=pltpu.VMEM)
SMEM = pl.BlockSpec(memory_space=pltpu.SMEM)
ANY = pl.BlockSpec(memory_space=pl.ANY)


def call(body, ins, outs, scratch=(), copies=0, flops=0, nbytes=0, vmem=40, name=None):
    kernel = pl.pallas_call(
        body,
        out_shape=tuple(pltpu.HBM(shape, dtype) if memory is ANY else jax.ShapeDtypeStruct(shape, dtype) for shape, dtype, memory in outs),
        in_specs=list(ins),
        out_specs=tuple(memory for _, _, memory in outs),
        scratch_shapes=list(scratch) + ([pltpu.SemaphoreType.DMA((copies,))] if copies else []),
        compiler_params=pltpu.CompilerParams(vmem_limit_bytes=vmem * 2**20),
        cost_estimate=pl.CostEstimate(flops=flops, bytes_accessed=nbytes, transcendentals=0),
        name=name,
    )

    def run(*operands):
        return kernel(*(
            pltpu.with_memory_space_constraint(x, pltpu.HBM) if memory is ANY else x
            for x, memory in zip(operands, ins)
        ))

    return run


def log2(value):
    assert value & (value - 1) == 0
    return value.bit_length() - 1


def iota(shape, dim):
    return lax.broadcasted_iota(I32, shape, dim)


def one(mask):
    return jnp.where(mask, 1.0, 0.0).astype(BF16)


def split2(x):
    top = x.astype(BF16)
    rest = (x - top.astype(F32)).astype(BF16)
    return jnp.concatenate([top, rest], axis=-1)


def split3(x):
    top = x.astype(BF16)
    rest = x - top.astype(F32)
    middle = rest.astype(BF16)
    last = (rest - middle.astype(F32)).astype(BF16)
    return jnp.concatenate([top, middle, last], axis=-1)


def dot(a, b):
    return lax.dot_general(a, b, (((1,), (0,)), ((), ())), preferred_element_type=F32)


def dot_nt(a, b):
    return lax.dot_general(a, b, (((1,), (1,)), ((), ())), preferred_element_type=F32)


def dot_tn(a, b):
    return lax.dot_general(a, b, (((0,), (0,)), ((), ())), preferred_element_type=F32)


def fold(x, parts):
    width = x.shape[-1] // parts
    total = x[..., (parts - 1) * width :]
    for part in reversed(range(parts - 1)):
        total = total + x[..., part * width : (part + 1) * width]
    return total


class Sizes:
    def __init__(self, devices, rows, slots, width, steps, bags, lookups, listed):
        self.devices, self.rows, self.slots, self.width = devices, rows, slots, width
        self.steps, self.bags, self.lookups, self.listed = steps, bags, lookups, listed
        self.cap = 2 * listed // devices
        self.places = devices * self.cap
        self.block = slots // devices
        self.chunks = self.places // LANES
        self.chunk = slots // self.chunks
        self.chunk_blocks = devices // self.chunks
        self.group = 256 // lookups
        self.groups = bags // self.group
        self.row_tiles = rows // LANES
        self.wide = (self.places, width)
        assert width == LANES and self.cap % 8 == 0 and self.chunk % self.block == 0
        assert self.groups * self.group == bags and self.group % 16 == 0
        assert slots // 256 * self.group <= 256 and self.row_tiles <= LANES

    def part(self, c):
        return slice(c * self.chunk, (c + 1) * self.chunk)


def lane_part(c):
    return slice(c * LANES, (c + 1) * LANES)


class Copies:
    def __init__(self, sems):
        self.sems, self.used, self.open = sems, 0, []

    def start(self, source, target):
        copy = pltpu.make_async_copy(source, target, self.sems.at[self.used])
        self.used += 1
        copy.start()
        return copy

    def send(self, source, target):
        self.open.append(self.start(source, target))

    def finish(self):
        for copy in self.open:
            copy.wait()


def place_of(z, dirty_ref, place_ref):
    earlier = iota((z.chunk, z.chunk), 0)
    later = iota((z.chunk, z.chunk), 1)
    shift = log2(z.block)
    before = one((earlier < later) & ((earlier >> shift) == (later >> shift)))
    base = ((iota((z.chunks, z.chunk), 1) >> shift) * z.cap).astype(F32)
    for t in range(z.steps):
        listed = dirty_ref[t : t + 1, :]
        high, low = listed >> log2(z.chunk), listed & (z.chunk - 1)
        chosen_high = one(iota((z.chunks, z.listed), 0) == high)
        chosen_low = one(iota((z.chunk, z.listed), 0) == low)
        chosen = dot_nt(chosen_high, chosen_low)
        rank = dot(chosen.astype(BF16), before)
        place_ref[t * z.chunks : (t + 1) * z.chunks, :] = jnp.where(chosen > 0.5, base + rank, -1.0)


def pick_of(z, place_ref, t, c):
    row = t * z.chunks + c
    return one(iota((LANES, z.chunk), 0).astype(F32) == place_ref[row : row + 1, :])


def keep_of(z, pick):
    return 1.0 - dot_tn(pick, jnp.ones((LANES, LANES), BF16))


def count_into(z, ids, count_ref, key_ref, low_ref):
    lanes = z.group * z.lookups
    spread = one((iota((z.lookups, lanes), 1) & (z.lookups - 1)) == iota((z.lookups, lanes), 0))
    bag_of_lane = iota((z.bags, lanes), 1) >> log2(z.lookups)
    mine = bag_of_lane == (iota((z.bags, lanes), 0) & (z.group - 1))
    high = dot_tn((ids >> 8).astype(F32).astype(BF16), spread)
    low = dot_tn((ids & 255).astype(F32).astype(BF16), spread)
    key = high * z.group + bag_of_lane.astype(F32)
    key_ref[...] = jnp.sum(jnp.where(mine, key, 0.0).reshape(z.groups, z.group, lanes), axis=1)
    low_ref[...] = jnp.sum(jnp.where(mine, low, 0.0).reshape(z.groups, z.group, lanes), axis=1)
    tiles = z.slots // 256
    for g in range(z.groups):
        key_row = key_ref[g : g + 1, :].astype(I32)
        low_row = low_ref[g : g + 1, :].astype(I32)
        left = one(iota((tiles * z.group, lanes), 0) == key_row)
        right = one(iota((256, lanes), 0) == low_row)
        counts = dot_nt(left, right).astype(BF16)
        for h in range(tiles):
            count_ref[g * z.group : (g + 1) * z.group, h * 256 : (h + 1) * 256] = counts[
                h * z.group : (h + 1) * z.group, :
            ]


def count_scratch(z):
    lanes = z.group * z.lookups
    return [pltpu.VMEM((z.groups, lanes), F32), pltpu.VMEM((z.groups, lanes), F32)]


def send_chunk(z, c, copies, owner, values_ref, out_ref):
    for b in range(c * z.chunk_blocks, (c + 1) * z.chunk_blocks):
        start = pl.multiple_of(owner(b) * z.cap, z.cap)
        copies.send(values_ref.at[b * z.cap : (b + 1) * z.cap, :], out_ref.at[pl.ds(start, z.cap), :])


def from_owners(z, back_ref, owner_ref, out_ref):
    for b in range(z.devices):
        start = pl.multiple_of(owner_ref[b] * z.cap, z.cap)
        out_ref[b * z.cap : (b + 1) * z.cap, :] = back_ref[pl.ds(start, z.cap), :]


def first_kernel(z, rows_ref, dirty_ref, ids_ref, targets_ref, cache_hbm, pending_hbm,
                 owner_ref, place_ref, grad_ref, count_hbm, out_hbm,
                 key_ref, low_ref, cache_ref, pending_ref, count_ref, flush_ref, sems):
    copies = Copies(sems)
    cache_in = copies.start(cache_hbm, cache_ref)
    pending_in = copies.start(pending_hbm, pending_ref)
    for b in range(z.devices):
        owner_ref[b] = rows_ref[b * z.block] >> log2(z.rows)
    place_of(z, dirty_ref, place_ref)
    count_into(z, ids_ref[0], count_ref, key_ref, low_ref)
    copies.send(count_ref, count_hbm)
    cache_in.wait()
    total = jnp.zeros((z.bags, 2 * z.width), F32)
    for c in range(z.chunks):
        total = total + dot(count_ref[:, z.part(c)], split2(cache_ref[z.part(c), :]))
    pooled = fold(total, 2) * (1.0 / z.lookups)
    grad = split2((pooled - targets_ref[0]) * (1.0 / z.lookups))
    grad_ref[...] = grad
    pending_in.wait()
    for c in range(z.chunks):
        pick = pick_of(z, place_ref, 0, c)
        lookups = dot_nt(pick, count_ref[:, z.part(c)]).astype(BF16)
        flush_ref[lane_part(c), :] = fold(dot(pick, split3(pending_ref[z.part(c), :])), 3) + fold(
            dot(lookups, grad), 2
        )
        send_chunk(z, c, copies, lambda b: owner_ref[b], flush_ref, out_hbm)
    copies.finish()


def index_kernel(z, rows_ref, place_ref, index_ref):
    local = rows_ref[...] & (z.rows - 1)
    for t in range(z.steps):
        for c in range(z.chunks):
            row = local[c : c + 1, :]
            parts = jnp.where(iota((8, z.chunk), 0) == 0, row >> 7, row & 127).astype(F32).astype(BF16)
            found = dot_nt(parts, pick_of(z, place_ref, t, c))
            index = found[0:1, :] * 128.0 + found[1:2, :]
            index_ref[t * z.chunks + c : t * z.chunks + c + 1, :] = index.astype(I32)


def next_kernel(z, t, place_ref, grad_ref, ids_ref, targets_ref, cache_hbm, pending_hbm, count_hbm,
                pending_out, waiting_hbm, new_count_hbm, back_hbm, flush_hbm, base_hbm,
                key_ref, low_ref, cache_ref, pending_ref, count_ref, new_ref, waiting_ref, back_ref, flush_ref,
                base_ref, sems):
    copies = Copies(sems)
    cache_in = copies.start(cache_hbm, cache_ref)
    pending_in = copies.start(pending_hbm, pending_ref)
    count_in = copies.start(count_hbm, count_ref)
    count_into(z, ids_ref[t + 1], new_ref, key_ref, low_ref)
    copies.send(new_ref, new_count_hbm)
    cache_in.wait()
    total = jnp.zeros((z.bags, 2 * z.width), F32)
    for c in range(z.chunks):
        counts = new_ref[:, z.part(c)]
        pick = pick_of(z, place_ref, t, c)
        value = cache_ref[z.part(c), :]
        if t == 0:
            value = value * keep_of(z, pick)
        total = total + dot(counts, split2(value))
        back_ref[:, lane_part(c)] = dot_nt(counts, pick).astype(BF16)
        flush_ref[lane_part(c), :] = dot_nt(pick_of(z, place_ref, t + 1, c), counts).astype(BF16)
    copies.send(back_ref, back_hbm)
    copies.send(flush_ref, flush_hbm)
    base_ref[...] = fold(total, 2) * (1.0 / z.lookups) - targets_ref[t + 1]
    copies.send(base_ref, base_hbm)
    pending_in.wait()
    count_in.wait()
    add_pending(z, t, place_ref, grad_ref, count_ref, pending_ref, waiting_ref)
    copies.send(pending_ref, pending_out)
    copies.send(waiting_ref, waiting_hbm)
    copies.finish()


def add_pending(z, t, place_ref, grad_ref, count_ref, pending_ref, waiting_ref):
    for c in range(z.chunks):
        added = fold(dot_tn(count_ref[:, z.part(c)], grad_ref[...]), 2)
        value = (pending_ref[z.part(c), :] + added) * keep_of(z, pick_of(z, place_ref, t, c))
        pending_ref[z.part(c), :] = value
        if waiting_ref is not None:
            waiting_ref[lane_part(c), :] = fold(dot(pick_of(z, place_ref, t + 1, c), split3(value)), 3)


def step_kernel(z, owner_ref, back_ref, counts_hbm, base_hbm, flush_counts_hbm, waiting_hbm,
                grad_ref, out_hbm, order_ref, counts_ref, base_ref, flush_counts_ref, waiting_ref, sems):
    copies = Copies(sems)
    counts_in = copies.start(counts_hbm, counts_ref)
    base_in = copies.start(base_hbm, base_ref)
    flush_in = copies.start(flush_counts_hbm, flush_counts_ref)
    waiting_in = copies.start(waiting_hbm, waiting_ref)
    from_owners(z, back_ref, owner_ref, order_ref)
    rows = split2(order_ref[...])
    counts_in.wait()
    total = fold(dot(counts_ref[...], rows), 2)
    base_in.wait()
    grad = split2((base_ref[...] + total * (1.0 / z.lookups)) * (1.0 / z.lookups))
    grad_ref[...] = grad
    flush_in.wait()
    waiting_in.wait()
    for c in range(z.chunks):
        part = lane_part(c)
        waiting_ref[part, :] = waiting_ref[part, :] + fold(dot(flush_counts_ref[part, :], grad), 2)
        send_chunk(z, c, copies, lambda b: owner_ref[b], waiting_ref, out_hbm)
    copies.finish()


def column(row):
    return jnp.transpose(jnp.broadcast_to(row, (LANES, LANES)))


def owner_kernel(z, t, got_ref, index_ref, accum_ref, old_hbm, answer_hbm, extra_hbm,
                 old_ref, answer_ref, extra_ref, sems):
    copies = Copies(sems)
    old_in = copies.start(old_hbm, old_ref)
    got = split2(got_ref[...])
    rows = [index_ref[t * z.chunks + c : t * z.chunks + c + 1, :].astype(F32) for c in range(z.chunks)]
    for c in range(z.chunks):
        part = lane_part(c)
        col = column(rows[c])
        same = jnp.concatenate([one(col == row) for row in rows], axis=1)
        grad = fold(dot(same, got), 2)
        extra = jnp.mean(grad * grad, axis=1, keepdims=True)
        fresh = column(accum_ref[c : c + 1, :]) + extra
        if c == 0:
            old_in.wait()
        answer_ref[part, :] = old_ref[part, :] - LEARN_RATE * grad / jnp.sqrt(fresh)
        copies.send(answer_ref.at[part, :], answer_hbm.at[part, :])
        extra_ref[part, :] = jnp.broadcast_to(extra, (LANES, LANES))
        copies.send(extra_ref.at[part, :], extra_hbm.at[part, :])
    copies.finish()


def gather_rows(z, t, flat_ref, table_ref, out_ref):
    def step(g, carry):
        base = pl.multiple_of(g * 32, 32)
        for k in range(32):
            row = flat_ref[t * z.places + base + k]
            out_ref[pl.ds(base + k, 1), :] = table_ref[pl.ds(row, 1), :]
        return carry

    lax.fori_loop(0, z.places // 32, step, 0)


def put_rows(z, t, flat_ref, answer_ref, table_ref):
    def step(g, carry):
        base = pl.multiple_of(g * 32, 32)
        for k in range(32):
            row = flat_ref[t * z.places + base + k]
            table_ref[pl.ds(row, 1), :] = answer_ref[pl.ds(base + k, 1), :]
        return carry

    lax.fori_loop(0, z.places // 32, step, 0)


def high_low(z, row):
    col = column(row)
    high = col >> 7 == iota((LANES, z.row_tiles), 1) if z.row_tiles == LANES else (
        col[:, : z.row_tiles] >> 7 == iota((LANES, z.row_tiles), 1)
    )
    return one(high), col & 127 == iota((LANES, LANES), 1)


def gather_accum(z, t, index_ref, accum, out_ref):
    parts = split3(accum)
    for c in range(z.chunks):
        now = t * z.chunks + c
        high, low = high_low(z, index_ref[now : now + 1, :])
        value = jnp.sum(jnp.where(low, fold(dot(high, parts), 3), 0.0), axis=1, keepdims=True)
        out_ref[c : c + 1, :] = jnp.transpose(jnp.broadcast_to(value, (LANES, LANES)))[0:1, :]


def put_accum(z, t, index_ref, accum, extra_ref):
    rows = [index_ref[t * z.chunks + c : t * z.chunks + c + 1, :] for c in range(z.chunks)]
    for i in range(z.chunks):
        col = column(rows[i])
        seen = jnp.where((col == rows[i]) & (iota((LANES, LANES), 1) < iota((LANES, LANES), 0)), 1.0, 0.0)
        for j in range(i):
            seen = jnp.where(col == rows[j], 1.0, seen)
        again = jnp.max(seen, axis=1, keepdims=True)
        high, low = high_low(z, rows[i])
        add = jnp.where(low & (again < 0.5), extra_ref[lane_part(i), :], 0.0)
        accum = accum + fold(dot_tn(high, split3(add)), 3)
    return accum


def start_kernel(z, flat_ref, index_ref, accum_ref, table_hbm, old_accum_ref, old_hbm, table_ref, old_ref, sems):
    copies = Copies(sems)
    table_in = copies.start(table_hbm, table_ref)
    gather_accum(z, 0, index_ref, accum_ref[...], old_accum_ref)
    table_in.wait()
    gather_rows(z, 0, flat_ref, table_ref, old_ref)
    copies.send(old_ref, old_hbm)
    copies.finish()


def update_kernel(z, t, owner_ref, flat_ref, index_ref, accum_ref, place_ref, back_ref,
                  table_hbm, answer_hbm, extra_hbm, cache_hbm,
                  new_accum_ref, old_accum_ref, table_out, old_hbm, cache_out,
                  table_ref, answer_ref, extra_ref, cache_ref, order_ref, old_ref, sems):
    copies = Copies(sems)
    answer_in = copies.start(answer_hbm, answer_ref)
    table_in = copies.start(table_hbm, table_ref)
    cache_in = copies.start(cache_hbm, cache_ref)
    extra_in = copies.start(extra_hbm, extra_ref)
    answer_in.wait()
    table_in.wait()
    put_rows(z, t, flat_ref, answer_ref, table_ref)
    copies.send(table_ref, table_out)
    gather_rows(z, t + 1, flat_ref, table_ref, old_ref)
    copies.send(old_ref, old_hbm)
    extra_in.wait()
    accum = put_accum(z, t, index_ref, accum_ref[...], extra_ref)
    new_accum_ref[...] = accum
    gather_accum(z, t + 1, index_ref, accum, old_accum_ref)
    from_owners(z, back_ref, owner_ref, order_ref)
    cache_in.wait()
    for c in range(z.chunks):
        pick = pick_of(z, place_ref, t, c)
        value = cache_ref[z.part(c), :]
        if t == 0:
            value = value * keep_of(z, pick)
        value = value + fold(dot_tn(pick, split3(order_ref[lane_part(c), :])), 3)
        cache_ref[z.part(c), :] = value * keep_of(z, pick_of(z, place_ref, t + 1, c))
    copies.send(cache_ref, cache_out)
    copies.finish()


def last_update_kernel(z, flat_ref, index_ref, accum_ref, place_ref, grad_ref,
                       table_hbm, answer_hbm, extra_hbm, pending_hbm, count_hbm,
                       new_accum_ref, table_out, pending_out,
                       table_ref, answer_ref, extra_ref, pending_ref, count_ref, sems):
    t = z.steps - 1
    copies = Copies(sems)
    answer_in = copies.start(answer_hbm, answer_ref)
    table_in = copies.start(table_hbm, table_ref)
    extra_in = copies.start(extra_hbm, extra_ref)
    count_in = copies.start(count_hbm, count_ref)
    pending_in = copies.start(pending_hbm, pending_ref)
    answer_in.wait()
    table_in.wait()
    put_rows(z, t, flat_ref, answer_ref, table_ref)
    copies.send(table_ref, table_out)
    extra_in.wait()
    new_accum_ref[...] = put_accum(z, t, index_ref, accum_ref[...], extra_ref)
    count_in.wait()
    pending_in.wait()
    add_pending(z, t, place_ref, grad_ref, count_ref, pending_ref, None)
    copies.send(pending_ref, pending_out)
    copies.finish()


def last_cache_kernel(z, owner_ref, back_ref, place_ref, cache_hbm, cache_out, order_ref, cache_ref, sems):
    t = z.steps - 1
    copies = Copies(sems)
    cache_in = copies.start(cache_hbm, cache_ref)
    from_owners(z, back_ref, owner_ref, order_ref)
    cache_in.wait()
    for c in range(z.chunks):
        pick = pick_of(z, place_ref, t, c)
        cache_ref[z.part(c), :] = cache_ref[z.part(c), :] + fold(
            dot_tn(pick, split3(order_ref[lane_part(c), :])), 3
        )
        copies.send(cache_ref.at[z.part(c), :], cache_out.at[z.part(c), :])
    copies.finish()


def body(table, accum, cache, cache_rows, pending, batch_slots, targets, dirty):
    z = Sizes(
        lax.axis_size(AXES), table.shape[0], cache.shape[0], cache.shape[1],
        batch_slots.shape[0], batch_slots.shape[1], batch_slots.shape[2], dirty.shape[1],
    )
    ids = batch_slots.transpose(0, 2, 1)
    wide, slots = z.wide, (z.slots, z.width)
    count, grads = ((z.bags, z.slots), BF16), ((z.bags, 2 * z.width), BF16)
    accums = ((z.row_tiles, LANES), F32)
    big = 2 * z.bags * z.slots * 2 * z.width

    def buf(shape, dtype=F32):
        return pltpu.VMEM(shape, dtype)

    def exchange(values):
        values = values.reshape(z.devices, z.cap, z.width)
        return lax.all_to_all(values, AXES, split_axis=0, concat_axis=0, tiled=True).reshape(wide)

    owner, place, grad, counts, outgoing = call(
        functools.partial(first_kernel, z),
        [SMEM, VMEM, VMEM, VMEM, ANY, ANY],
        [((z.devices,), I32, SMEM), ((z.steps * z.chunks, z.chunk), F32, VMEM), (*grads, VMEM), (*count, ANY),
         (wide, F32, ANY)],
        scratch=count_scratch(z) + [buf(slots), buf(slots), buf(*count), buf(wide)],
        copies=3 + z.devices, flops=6 * big, nbytes=2**24, name="first",
    )(cache_rows, dirty, ids, targets, cache, pending)

    outgoing, place = lax.optimization_barrier((outgoing, place))
    got = exchange(outgoing)
    index = call(
        functools.partial(index_kernel, z), [VMEM, VMEM], [((z.steps * z.chunks, LANES), I32, VMEM)],
        flops=10**9, nbytes=2**20, name="index",
    )(cache_rows.reshape(z.chunks, z.chunk), place)[0]
    index = index.reshape(z.steps, z.devices, z.cap).transpose(1, 0, 2).reshape(z.devices, -1)
    to = owner[None, :] == jnp.arange(z.devices, dtype=I32)[:, None]
    index = jnp.sum(jnp.where(to[:, :, None], index[None], 0), axis=1)
    index = lax.all_to_all(index.reshape(z.devices, 1, -1), AXES, split_axis=0, concat_axis=0, tiled=True)
    index = index.reshape(z.devices, z.steps, z.cap).transpose(1, 0, 2)
    flat = index.reshape(-1)
    index = index.reshape(z.steps * z.chunks, LANES)
    accum = accum.reshape(accums[0])

    old_accum, old = call(
        functools.partial(start_kernel, z), [SMEM, VMEM, VMEM, ANY],
        [((z.chunks, LANES), F32, VMEM), (wide, F32, ANY)],
        scratch=[buf(table.shape), buf(wide)], copies=2, flops=10**9, nbytes=2**23, name="start",
    )(flat, index, accum, table)

    for t in range(z.steps):
        answer, extra = call(
            functools.partial(owner_kernel, z, t), [VMEM, VMEM, VMEM, ANY], [(wide, F32, ANY), (wide, F32, ANY)],
            scratch=[buf(wide), buf(wide), buf(wide)], copies=1 + 2 * z.chunks, flops=10**9, nbytes=2**21,
            vmem=24, name="owner",
        )(got, index, old_accum, old)
        answer, extra, grad = lax.optimization_barrier((answer, extra, grad))
        back = exchange(answer)
        if t == z.steps - 1:
            break
        pending, waiting, counts, back_counts, flush_counts, base = call(
            functools.partial(next_kernel, z, t), [VMEM, VMEM, VMEM, VMEM, ANY, ANY, ANY],
            [(slots, F32, ANY), (wide, F32, ANY), (*count, ANY), ((z.bags, z.places), BF16, ANY),
             ((z.places, z.bags), BF16, ANY), ((z.bags, z.width), F32, ANY)],
            scratch=count_scratch(z) + [
                buf(slots), buf(slots), buf(*count), buf(*count), buf(wide), buf((z.bags, z.places), BF16),
                buf((z.places, z.bags), BF16), buf((z.bags, z.width))],
            copies=9, flops=8 * big, nbytes=2**24, name="next",
        )(place, grad, ids, targets, cache, pending, counts)
        grad, outgoing = call(
            functools.partial(step_kernel, z), [SMEM, VMEM, ANY, ANY, ANY, ANY], [(*grads, VMEM), (wide, F32, ANY)],
            scratch=[buf(wide), buf((z.bags, z.places), BF16), buf((z.bags, z.width)), buf((z.places, z.bags), BF16),
                     buf(wide)],
            copies=4 + z.devices, flops=10**9, nbytes=2**22, vmem=24, name="step",
        )(owner, back, back_counts, base, flush_counts, waiting)
        outgoing, back, answer = lax.optimization_barrier((outgoing, back, answer))
        got = exchange(outgoing)
        accum, old_accum, table, old, cache = call(
            functools.partial(update_kernel, z, t), [SMEM, SMEM, VMEM, VMEM, VMEM, VMEM, ANY, ANY, ANY, ANY],
            [(*accums, VMEM), ((z.chunks, LANES), F32, VMEM), (table.shape, F32, ANY), (wide, F32, ANY),
             (slots, F32, ANY)],
            scratch=[buf(table.shape), buf(wide), buf(wide), buf(slots), buf(wide), buf(wide)],
            copies=7, flops=3 * big, nbytes=2**24, name="update",
        )(owner, flat, index, accum, place, back, table, answer, extra, cache)
    accum, table, pending = call(
        functools.partial(last_update_kernel, z), [SMEM, VMEM, VMEM, VMEM, VMEM, ANY, ANY, ANY, ANY, ANY],
        [(*accums, VMEM), (table.shape, F32, ANY), (slots, F32, ANY)],
        scratch=[buf(table.shape), buf(wide), buf(wide), buf(slots), buf(*count)],
        copies=7, flops=3 * big, nbytes=2**24, name="last_update",
    )(flat, index, accum, place, grad, table, answer, extra, pending, counts)
    cache = call(
        functools.partial(last_cache_kernel, z), [SMEM, VMEM, VMEM, ANY], [(slots, F32, ANY)],
        scratch=[buf(wide), buf(slots)], copies=1 + z.chunks, flops=big, nbytes=2**22, vmem=24, name="last_cache",
    )(owner, back, place, cache)[0]
    return (table, accum.reshape(-1), cache, pending)


def solution(mesh):
    in_specs = (
        P(AXES, None),
        P(AXES),
        P(AXES, None),
        P(AXES),
        P(AXES, None),
        P(None, AXES, None),
        P(None, AXES, None),
        P(None, AXES),
    )
    out_specs = (P(AXES, None), P(AXES), P(AXES, None), P(AXES, None))
    return jax.shard_map(body, mesh=mesh, in_specs=in_specs, out_specs=out_specs, check_vma=False)
```

```python
import functools

import jax
import jax.numpy as jnp
from jax import lax
from jax.experimental import pallas as pl
from jax.experimental.pallas import tpu as pltpu
from jax.sharding import PartitionSpec as P

LEARN_RATE = 0.3
AXES = ("gx", "gy")
F32, BF16, I32 = jnp.float32, jnp.bfloat16, jnp.int32
LANES = 128
VMEM = pl.BlockSpec(memory_space=pltpu.VMEM)
SMEM = pl.BlockSpec(memory_space=pltpu.SMEM)
ANY = pl.BlockSpec(memory_space=pl.ANY)


def call(body, ins, outs, scratch=(), copies=0, flops=0, nbytes=0, vmem=40, name=None):
    kernel = pl.pallas_call(
        body,
        out_shape=tuple(pltpu.HBM(shape, dtype) if memory is ANY else jax.ShapeDtypeStruct(shape, dtype) for shape, dtype, memory in outs),
        in_specs=list(ins),
        out_specs=tuple(memory for _, _, memory in outs),
        scratch_shapes=list(scratch) + ([pltpu.SemaphoreType.DMA((copies,))] if copies else []),
        compiler_params=pltpu.CompilerParams(vmem_limit_bytes=vmem * 2**20),
        cost_estimate=pl.CostEstimate(flops=flops, bytes_accessed=nbytes, transcendentals=0),
        name=name,
    )

    def run(*operands):
        return kernel(*(
            pltpu.with_memory_space_constraint(x, pltpu.HBM) if memory is ANY else x
            for x, memory in zip(operands, ins)
        ))

    return run


def log2(value):
    assert value & (value - 1) == 0
    return value.bit_length() - 1


def iota(shape, dim):
    return lax.broadcasted_iota(I32, shape, dim)


def one(mask):
    return jnp.where(mask, 1.0, 0.0).astype(BF16)


def split2(x):
    top = x.astype(BF16)
    rest = (x - top.astype(F32)).astype(BF16)
    return jnp.concatenate([top, rest], axis=-1)


def split3(x):
    top = x.astype(BF16)
    rest = x - top.astype(F32)
    middle = rest.astype(BF16)
    last = (rest - middle.astype(F32)).astype(BF16)
    return jnp.concatenate([top, middle, last], axis=-1)


def dot(a, b):
    return lax.dot_general(a, b, (((1,), (0,)), ((), ())), preferred_element_type=F32)


def dot_nt(a, b):
    return lax.dot_general(a, b, (((1,), (1,)), ((), ())), preferred_element_type=F32)


def dot_tn(a, b):
    return lax.dot_general(a, b, (((0,), (0,)), ((), ())), preferred_element_type=F32)


def fold(x, parts):
    width = x.shape[-1] // parts
    total = x[..., (parts - 1) * width :]
    for part in reversed(range(parts - 1)):
        total = total + x[..., part * width : (part + 1) * width]
    return total


class Sizes:
    def __init__(self, devices, rows, slots, width, steps, bags, lookups, listed):
        self.devices, self.rows, self.slots, self.width = devices, rows, slots, width
        self.steps, self.bags, self.lookups, self.listed = steps, bags, lookups, listed
        self.cap = 2 * listed // devices
        self.places = devices * self.cap
        self.block = slots // devices
        self.chunks = self.places // LANES
        self.chunk = slots // self.chunks
        self.chunk_blocks = devices // self.chunks
        self.group = 256 // lookups
        self.groups = bags // self.group
        self.row_tiles = rows // LANES
        self.wide = (self.places, width)
        assert width == LANES and self.cap % 8 == 0 and self.chunk % self.block == 0
        assert self.groups * self.group == bags and self.group % 16 == 0
        assert slots // 256 * self.group <= 256 and self.row_tiles <= LANES

    def part(self, c):
        return slice(c * self.chunk, (c + 1) * self.chunk)


def lane_part(c):
    return slice(c * LANES, (c + 1) * LANES)


class Copies:
    def __init__(self, sems):
        self.sems, self.used, self.open = sems, 0, []

    def start(self, source, target):
        copy = pltpu.make_async_copy(source, target, self.sems.at[self.used])
        self.used += 1
        copy.start()
        return copy

    def send(self, source, target):
        self.open.append(self.start(source, target))

    def finish(self):
        for copy in self.open:
            copy.wait()


def place_of(z, dirty_ref, place_ref):
    earlier = iota((z.chunk, z.chunk), 0)
    later = iota((z.chunk, z.chunk), 1)
    shift = log2(z.block)
    before = one((earlier < later) & ((earlier >> shift) == (later >> shift)))
    base = ((iota((z.chunks, z.chunk), 1) >> shift) * z.cap).astype(F32)
    for t in range(z.steps):
        listed = dirty_ref[t : t + 1, :]
        high, low = listed >> log2(z.chunk), listed & (z.chunk - 1)
        chosen_high = one(iota((z.chunks, z.listed), 0) == high)
        chosen_low = one(iota((z.chunk, z.listed), 0) == low)
        chosen = dot_nt(chosen_high, chosen_low)
        rank = dot(chosen.astype(BF16), before)
        place_ref[t * z.chunks : (t + 1) * z.chunks, :] = jnp.where(chosen > 0.5, base + rank, -1.0)


def pick_of(z, place_ref, t, c):
    row = t * z.chunks + c
    return one(iota((LANES, z.chunk), 0).astype(F32) == place_ref[row : row + 1, :])


def keep_of(z, pick):
    return 1.0 - dot_tn(pick, jnp.ones((LANES, LANES), BF16))


def count_into(z, ids, count_ref, key_ref, low_ref):
    lanes = z.group * z.lookups
    spread = one((iota((z.lookups, lanes), 1) & (z.lookups - 1)) == iota((z.lookups, lanes), 0))
    bag_of_lane = iota((z.bags, lanes), 1) >> log2(z.lookups)
    mine = bag_of_lane == (iota((z.bags, lanes), 0) & (z.group - 1))
    high = dot_tn((ids >> 8).astype(F32).astype(BF16), spread)
    low = dot_tn((ids & 255).astype(F32).astype(BF16), spread)
    key = high * z.group + bag_of_lane.astype(F32)
    key_ref[...] = jnp.sum(jnp.where(mine, key, 0.0).reshape(z.groups, z.group, lanes), axis=1)
    low_ref[...] = jnp.sum(jnp.where(mine, low, 0.0).reshape(z.groups, z.group, lanes), axis=1)
    tiles = z.slots // 256
    for g in range(z.groups):
        key_row = key_ref[g : g + 1, :].astype(I32)
        low_row = low_ref[g : g + 1, :].astype(I32)
        left = one(iota((tiles * z.group, lanes), 0) == key_row)
        right = one(iota((256, lanes), 0) == low_row)
        counts = dot_nt(left, right).astype(BF16)
        for h in range(tiles):
            count_ref[g * z.group : (g + 1) * z.group, h * 256 : (h + 1) * 256] = counts[
                h * z.group : (h + 1) * z.group, :
            ]


def count_scratch(z):
    lanes = z.group * z.lookups
    return [pltpu.VMEM((z.groups, lanes), F32), pltpu.VMEM((z.groups, lanes), F32)]


def send_chunk(z, c, copies, owner, values_ref, out_ref):
    for b in range(c * z.chunk_blocks, (c + 1) * z.chunk_blocks):
        start = pl.multiple_of(owner(b) * z.cap, z.cap)
        copies.send(values_ref.at[b * z.cap : (b + 1) * z.cap, :], out_ref.at[pl.ds(start, z.cap), :])


def from_owners(z, back_ref, owner_ref, out_ref):
    for b in range(z.devices):
        start = pl.multiple_of(owner_ref[b] * z.cap, z.cap)
        out_ref[b * z.cap : (b + 1) * z.cap, :] = back_ref[pl.ds(start, z.cap), :]


def place_kernel(z, rows_hbm, tiled_hbm, dirty_hbm, owner_ref, place_ref, index_ref, rows_ref, tiled_ref, dirty_ref, sems):
    copies = Copies(sems)
    dirty_in = copies.start(dirty_hbm, dirty_ref)
    tiled_in = copies.start(tiled_hbm, tiled_ref)
    rows_in = copies.start(rows_hbm, rows_ref)
    dirty_in.wait()
    place_of(z, dirty_ref, place_ref)
    tiled_in.wait()
    local = tiled_ref[...] & (z.rows - 1)
    pieces = z.chunk // LANES
    for c in range(z.chunks):
        row = jnp.concatenate([local[c * pieces + k : c * pieces + k + 1, :] for k in range(pieces)], axis=1)
        parts = jnp.where(iota((8, z.chunk), 0) == 0, row >> 7, row & 127).astype(F32).astype(BF16)
        for t in range(z.steps):
            found = dot_nt(parts, pick_of(z, place_ref, t, c))
            index = found[0:1, :] * 128.0 + found[1:2, :]
            index_ref[t * z.chunks + c : t * z.chunks + c + 1, :] = index.astype(I32)
    rows_in.wait()
    for b in range(z.devices):
        owner_ref[b] = rows_ref[b * z.block] >> log2(z.rows)


def first_kernel(z, owner_ref, place_ref, ids_hbm, targets_hbm, cache_hbm, pending_hbm,
                 grad_hbm, count_hbm, out_hbm,
                 grad_ref, key_ref, low_ref, ids_ref, targets_ref, cache_ref, pending_ref, count_ref,
                 flush_ref, sems):
    copies = Copies(sems)
    ids_in = copies.start(ids_hbm.at[0], ids_ref)
    cache_in = copies.start(cache_hbm, cache_ref)
    targets_in = copies.start(targets_hbm.at[0], targets_ref)
    pending_in = copies.start(pending_hbm, pending_ref)
    ids_in.wait()
    count_into(z, ids_ref[...], count_ref, key_ref, low_ref)
    copies.send(count_ref, count_hbm)
    targets_in.wait()
    cache_in.wait()
    total = jnp.zeros((z.bags, 2 * z.width), F32)
    for c in range(z.chunks):
        total = total + dot(count_ref[:, z.part(c)], split2(cache_ref[z.part(c), :]))
    pooled = fold(total, 2) * (1.0 / z.lookups)
    grad = split2((pooled - targets_ref[...]) * (1.0 / z.lookups))
    grad_ref[...] = grad
    copies.send(grad_ref, grad_hbm)
    pending_in.wait()
    for c in range(z.chunks):
        pick = pick_of(z, place_ref, 0, c)
        lookups = dot_nt(pick, count_ref[:, z.part(c)]).astype(BF16)
        flush_ref[lane_part(c), :] = fold(dot(pick, split3(pending_ref[z.part(c), :])), 3) + fold(
            dot(lookups, grad), 2
        )
        send_chunk(z, c, copies, lambda b: owner_ref[b], flush_ref, out_hbm)
    copies.finish()


def next_kernel(z, t, place_ref, grad_hbm, ids_hbm, targets_hbm, cache_hbm, pending_hbm, count_hbm,
                pending_out, waiting_ref, new_count_hbm, back_ref, flush_ref, base_hbm,
                grad_ref, base_ref, key_ref, low_ref, ids_ref, targets_ref, cache_ref, pending_ref, count_ref, new_ref, sems):
    copies = Copies(sems)
    ids_in = copies.start(ids_hbm.at[t + 1], ids_ref)
    cache_in = copies.start(cache_hbm, cache_ref)
    targets_in = copies.start(targets_hbm.at[t + 1], targets_ref)
    pending_in = copies.start(pending_hbm, pending_ref)
    count_in = copies.start(count_hbm, count_ref)
    grad_in = copies.start(grad_hbm, grad_ref)
    ids_in.wait()
    count_into(z, ids_ref[...], new_ref, key_ref, low_ref)
    copies.send(new_ref, new_count_hbm)
    cache_in.wait()
    total = jnp.zeros((z.bags, 2 * z.width), F32)
    for c in range(z.chunks):
        counts = new_ref[:, z.part(c)]
        pick = pick_of(z, place_ref, t, c)
        value = cache_ref[z.part(c), :]
        if t == 0:
            value = value * keep_of(z, pick)
        total = total + dot(counts, split2(value))
        back_ref[:, lane_part(c)] = dot_nt(counts, pick).astype(BF16)
        flush_ref[lane_part(c), :] = dot_nt(pick_of(z, place_ref, t + 1, c), counts).astype(BF16)
    targets_in.wait()
    base_ref[...] = fold(total, 2) * (1.0 / z.lookups) - targets_ref[...]
    copies.send(base_ref, base_hbm)
    grad_in.wait()
    pending_in.wait()
    count_in.wait()
    add_pending(z, t, place_ref, grad_ref, count_ref, pending_ref, waiting_ref)
    copies.send(pending_ref, pending_out)
    copies.finish()


def add_pending(z, t, place_ref, grad_ref, count_ref, pending_ref, waiting_ref):
    for c in range(z.chunks):
        added = fold(dot_tn(count_ref[:, z.part(c)], grad_ref[...]), 2)
        value = (pending_ref[z.part(c), :] + added) * keep_of(z, pick_of(z, place_ref, t, c))
        pending_ref[z.part(c), :] = value
        if waiting_ref is not None:
            waiting_ref[lane_part(c), :] = fold(dot(pick_of(z, place_ref, t + 1, c), split3(value)), 3)


def step_kernel(z, owner_ref, back_ref, counts_ref, base_hbm, flush_counts_ref, waiting_ref,
                grad_hbm, out_hbm, grad_ref, base_ref, order_ref, flush_ref, sems):
    copies = Copies(sems)
    base_in = copies.start(base_hbm, base_ref)
    from_owners(z, back_ref, owner_ref, order_ref)
    total = fold(dot(counts_ref[...], split2(order_ref[...])), 2)
    base_in.wait()
    grad = split2((base_ref[...] + total * (1.0 / z.lookups)) * (1.0 / z.lookups))
    grad_ref[...] = grad
    copies.send(grad_ref, grad_hbm)
    for c in range(z.chunks):
        part = lane_part(c)
        flush_ref[part, :] = waiting_ref[part, :] + fold(dot(flush_counts_ref[part, :], grad), 2)
        send_chunk(z, c, copies, lambda b: owner_ref[b], flush_ref, out_hbm)
    copies.finish()


def column(row):
    return jnp.transpose(jnp.broadcast_to(row, (LANES, LANES)))


def owner_kernel(z, t, got_ref, index_ref, accum_ref, old_ref, answer_hbm, extra_hbm,
                 answer_ref, extra_ref, sems):
    copies = Copies(sems)
    got = split2(got_ref[...])
    rows = [index_ref[t * z.chunks + c : t * z.chunks + c + 1, :].astype(F32) for c in range(z.chunks)]
    for c in range(z.chunks):
        part = lane_part(c)
        col = column(rows[c])
        same = jnp.concatenate([one(col == row) for row in rows], axis=1)
        grad = fold(dot(same, got), 2)
        extra = jnp.mean(grad * grad, axis=1, keepdims=True)
        fresh = column(accum_ref[c : c + 1, :]) + extra
        answer_ref[part, :] = old_ref[part, :] - LEARN_RATE * grad / jnp.sqrt(fresh)
        copies.send(answer_ref.at[part, :], answer_hbm.at[part, :])
        extra_ref[part, :] = jnp.broadcast_to(extra, (LANES, LANES))
        copies.send(extra_ref.at[part, :], extra_hbm.at[part, :])
    copies.finish()


def gather_rows(z, t, flat_ref, table_ref, out_ref):
    def step(g, carry):
        base = pl.multiple_of(g * 32, 32)
        for k in range(32):
            row = flat_ref[t * z.places + base + k]
            out_ref[pl.ds(base + k, 1), :] = table_ref[pl.ds(row, 1), :]
        return carry

    lax.fori_loop(0, z.places // 32, step, 0)


def put_rows(z, t, flat_ref, answer_ref, table_ref):
    def step(g, carry):
        base = pl.multiple_of(g * 32, 32)
        for k in range(32):
            row = flat_ref[t * z.places + base + k]
            table_ref[pl.ds(row, 1), :] = answer_ref[pl.ds(base + k, 1), :]
        return carry

    lax.fori_loop(0, z.places // 32, step, 0)


def high_low(z, row):
    col = column(row)
    high = col >> 7 == iota((LANES, z.row_tiles), 1) if z.row_tiles == LANES else (
        col[:, : z.row_tiles] >> 7 == iota((LANES, z.row_tiles), 1)
    )
    return one(high), col & 127 == iota((LANES, LANES), 1)


def gather_accum(z, t, index_ref, accum, out_ref):
    parts = split3(accum)
    for c in range(z.chunks):
        now = t * z.chunks + c
        high, low = high_low(z, index_ref[now : now + 1, :])
        value = jnp.sum(jnp.where(low, fold(dot(high, parts), 3), 0.0), axis=1, keepdims=True)
        out_ref[c : c + 1, :] = jnp.transpose(jnp.broadcast_to(value, (LANES, LANES)))[0:1, :]


def put_accum(z, t, index_ref, accum, extra_ref):
    rows = [index_ref[t * z.chunks + c : t * z.chunks + c + 1, :] for c in range(z.chunks)]
    for i in range(z.chunks):
        col = column(rows[i])
        seen = jnp.where((col == rows[i]) & (iota((LANES, LANES), 1) < iota((LANES, LANES), 0)), 1.0, 0.0)
        for j in range(i):
            seen = jnp.where(col == rows[j], 1.0, seen)
        again = jnp.max(seen, axis=1, keepdims=True)
        high, low = high_low(z, rows[i])
        add = jnp.where(low & (again < 0.5), extra_ref[lane_part(i), :], 0.0)
        accum = accum + fold(dot_tn(high, split3(add)), 3)
    return accum


def start_kernel(z, flat_ref, index_ref, accum_ref, table_hbm, old_accum_ref, old_ref, table_ref, sems):
    copies = Copies(sems)
    table_in = copies.start(table_hbm, table_ref)
    gather_accum(z, 0, index_ref, accum_ref[...], old_accum_ref)
    table_in.wait()
    gather_rows(z, 0, flat_ref, table_ref, old_ref)


def update_kernel(z, t, owner_ref, flat_ref, index_ref, accum_ref, place_ref, back_ref,
                  table_hbm, answer_hbm, extra_hbm, cache_hbm,
                  new_accum_ref, old_accum_ref, table_out, old_ref, cache_out,
                  table_ref, answer_ref, extra_ref, cache_ref, order_ref, sems):
    copies = Copies(sems)
    answer_in = copies.start(answer_hbm, answer_ref)
    table_in = copies.start(table_hbm, table_ref)
    cache_in = copies.start(cache_hbm, cache_ref)
    extra_in = copies.start(extra_hbm, extra_ref)
    answer_in.wait()
    table_in.wait()
    put_rows(z, t, flat_ref, answer_ref, table_ref)
    copies.send(table_ref, table_out)
    gather_rows(z, t + 1, flat_ref, table_ref, old_ref)
    extra_in.wait()
    accum = put_accum(z, t, index_ref, accum_ref[...], extra_ref)
    new_accum_ref[...] = accum
    gather_accum(z, t + 1, index_ref, accum, old_accum_ref)
    from_owners(z, back_ref, owner_ref, order_ref)
    cache_in.wait()
    for c in range(z.chunks):
        pick = pick_of(z, place_ref, t, c)
        value = cache_ref[z.part(c), :]
        if t == 0:
            value = value * keep_of(z, pick)
        value = value + fold(dot_tn(pick, split3(order_ref[lane_part(c), :])), 3)
        cache_ref[z.part(c), :] = value * keep_of(z, pick_of(z, place_ref, t + 1, c))
    copies.send(cache_ref, cache_out)
    copies.finish()


def last_update_kernel(z, flat_ref, index_ref, accum_ref, place_ref, grad_hbm,
                       table_hbm, answer_hbm, extra_hbm, pending_hbm, count_hbm,
                       new_accum_ref, table_out, pending_out,
                       grad_ref, table_ref, answer_ref, extra_ref, pending_ref, count_ref, sems):
    t = z.steps - 1
    copies = Copies(sems)
    answer_in = copies.start(answer_hbm, answer_ref)
    table_in = copies.start(table_hbm, table_ref)
    extra_in = copies.start(extra_hbm, extra_ref)
    count_in = copies.start(count_hbm, count_ref)
    pending_in = copies.start(pending_hbm, pending_ref)
    grad_in = copies.start(grad_hbm, grad_ref)
    answer_in.wait()
    table_in.wait()
    put_rows(z, t, flat_ref, answer_ref, table_ref)
    copies.send(table_ref, table_out)
    extra_in.wait()
    new_accum_ref[...] = put_accum(z, t, index_ref, accum_ref[...], extra_ref)
    grad_in.wait()
    count_in.wait()
    pending_in.wait()
    add_pending(z, t, place_ref, grad_ref, count_ref, pending_ref, None)
    copies.send(pending_ref, pending_out)
    copies.finish()


def last_cache_kernel(z, owner_ref, back_ref, place_ref, cache_hbm, cache_out, order_ref, cache_ref, sems):
    t = z.steps - 1
    copies = Copies(sems)
    cache_in = copies.start(cache_hbm, cache_ref)
    from_owners(z, back_ref, owner_ref, order_ref)
    cache_in.wait()
    for c in range(z.chunks):
        pick = pick_of(z, place_ref, t, c)
        cache_ref[z.part(c), :] = cache_ref[z.part(c), :] + fold(
            dot_tn(pick, split3(order_ref[lane_part(c), :])), 3
        )
        copies.send(cache_ref.at[z.part(c), :], cache_out.at[z.part(c), :])
    copies.finish()


def body(table, accum, cache, cache_rows, pending, batch_slots, targets, dirty):
    z = Sizes(
        lax.axis_size(AXES), table.shape[0], cache.shape[0], cache.shape[1],
        batch_slots.shape[0], batch_slots.shape[1], batch_slots.shape[2], dirty.shape[1],
    )
    ids = batch_slots.transpose(0, 2, 1)
    wide, slots = z.wide, (z.slots, z.width)
    count, grads = ((z.bags, z.slots), BF16), ((z.bags, 2 * z.width), BF16)
    accums = ((z.row_tiles, LANES), F32)
    big = 2 * z.bags * z.slots * 2 * z.width

    def buf(shape, dtype=F32):
        return pltpu.VMEM(shape, dtype)

    def exchange(values):
        values = values.reshape(z.devices, z.cap, z.width)
        return lax.all_to_all(values, AXES, split_axis=0, concat_axis=0, tiled=True).reshape(wide)

    owner, place, index = call(
        functools.partial(place_kernel, z), [ANY] * 3,
        [((z.devices,), I32, SMEM), ((z.steps * z.chunks, z.chunk), F32, VMEM),
         ((z.steps * z.chunks, LANES), I32, VMEM)],
        scratch=[pltpu.SMEM((z.slots,), I32), buf((z.slots // LANES, LANES), I32), buf(dirty.shape, I32)],
        copies=3, flops=10**9, nbytes=2**20, name="place",
    )(cache_rows, cache_rows.reshape(-1, LANES), dirty)

    index = index.reshape(z.steps, z.devices, z.cap).transpose(1, 0, 2).reshape(z.devices, -1)
    to = owner[None, :] == jnp.arange(z.devices, dtype=I32)[:, None]
    index = jnp.sum(jnp.where(to[:, :, None], index[None], 0), axis=1)
    index = lax.all_to_all(index.reshape(z.devices, 1, -1), AXES, split_axis=0, concat_axis=0, tiled=True)
    grad, counts, outgoing = call(
        functools.partial(first_kernel, z), [SMEM, VMEM] + [ANY] * 4, [(*grads, ANY), (*count, ANY), (wide, F32, ANY)],
        scratch=[buf(*grads)] + count_scratch(z) + [
            buf(ids.shape[1:], I32), buf(targets.shape[1:]), buf(slots), buf(slots), buf(*count), buf(wide)],
        copies=6 + z.devices, flops=6 * big, nbytes=2**24, name="first",
    )(owner, place, ids, targets, cache, pending)
    got = exchange(outgoing)
    index = index.reshape(z.devices, z.steps, z.cap).transpose(1, 0, 2)
    flat = index.reshape(-1)
    index = index.reshape(z.steps * z.chunks, LANES)
    accum = accum.reshape(accums[0])

    old_accum, old = call(
        functools.partial(start_kernel, z), [SMEM, VMEM, VMEM, ANY],
        [((z.chunks, LANES), F32, VMEM), (wide, F32, VMEM)],
        scratch=[buf(table.shape)], copies=1, flops=10**9, nbytes=2**23, name="start",
    )(flat, index, accum, table)

    for t in range(z.steps):
        answer, extra = call(
            functools.partial(owner_kernel, z, t), [VMEM] * 4, [(wide, F32, ANY), (wide, F32, ANY)],
            scratch=[buf(wide), buf(wide)], copies=2 * z.chunks, flops=10**9, nbytes=2**21,
            vmem=24, name="owner",
        )(got, index, old_accum, old)
        answer, extra, grad = lax.optimization_barrier((answer, extra, grad))
        back = exchange(answer)
        if t == z.steps - 1:
            break
        pending, waiting, counts, back_counts, flush_counts, base = call(
            functools.partial(next_kernel, z, t), [VMEM, ANY, ANY, ANY, ANY, ANY, ANY],
            [(slots, F32, ANY), (wide, F32, VMEM), (*count, ANY), ((z.bags, z.places), BF16, VMEM),
             ((z.places, z.bags), BF16, VMEM), ((z.bags, z.width), F32, ANY)],
            scratch=[buf(*grads), buf((z.bags, z.width))] + count_scratch(z) + [
                buf(ids.shape[1:], I32), buf(targets.shape[1:]), buf(slots), buf(slots), buf(*count), buf(*count)],
            copies=9, flops=8 * big, nbytes=2**24, name="next",
        )(place, grad, ids, targets, cache, pending, counts)
        grad, outgoing = call(
            functools.partial(step_kernel, z), [SMEM, VMEM, VMEM, ANY, VMEM, VMEM],
            [(*grads, ANY), (wide, F32, ANY)],
            scratch=[buf(*grads), buf((z.bags, z.width)), buf(wide), buf(wide)], copies=2 + z.devices, flops=10**9, nbytes=2**22, vmem=24, name="step",
        )(owner, back, back_counts, base, flush_counts, waiting)
        outgoing, back, answer = lax.optimization_barrier((outgoing, back, answer))
        got = exchange(outgoing)
        accum, old_accum, table, old, cache = call(
            functools.partial(update_kernel, z, t), [SMEM, SMEM, VMEM, VMEM, VMEM, VMEM, ANY, ANY, ANY, ANY],
            [(*accums, VMEM), ((z.chunks, LANES), F32, VMEM), (table.shape, F32, ANY), (wide, F32, VMEM),
             (slots, F32, ANY)],
            scratch=[buf(table.shape), buf(wide), buf(wide), buf(slots), buf(wide)],
            copies=6, flops=3 * big, nbytes=2**24, name="update",
        )(owner, flat, index, accum, place, back, table, answer, extra, cache)
    accum, table, pending = call(
        functools.partial(last_update_kernel, z), [SMEM, VMEM, VMEM, VMEM] + [ANY] * 6,
        [(*accums, VMEM), (table.shape, F32, ANY), (slots, F32, ANY)],
        scratch=[buf(*grads), buf(table.shape), buf(wide), buf(wide), buf(slots), buf(*count)],
        copies=8, flops=3 * big, nbytes=2**24, name="last_update",
    )(flat, index, accum, place, grad, table, answer, extra, pending, counts)
    cache = call(
        functools.partial(last_cache_kernel, z), [SMEM, VMEM, VMEM, ANY], [(slots, F32, ANY)],
        scratch=[buf(wide), buf(slots)], copies=1 + z.chunks, flops=big, nbytes=2**22, vmem=24, name="last_cache",
    )(owner, back, place, cache)[0]
    return (table, accum.reshape(-1), cache, pending)


def solution(mesh):
    in_specs = (
        P(AXES, None),
        P(AXES),
        P(AXES, None),
        P(AXES),
        P(AXES, None),
        P(None, AXES, None),
        P(None, AXES, None),
        P(None, AXES),
    )
    out_specs = (P(AXES, None), P(AXES), P(AXES, None), P(AXES, None))
    return jax.shard_map(body, mesh=mesh, in_specs=in_specs, out_specs=out_specs, check_vma=False)
```

```python
import functools

import jax
import jax.numpy as jnp
from jax import lax
from jax.experimental import pallas as pl
from jax.experimental.pallas import tpu as pltpu
from jax.sharding import PartitionSpec as P

LEARN_RATE = 0.3
AXES = ("gx", "gy")
F32, BF16, I32 = jnp.float32, jnp.bfloat16, jnp.int32
LANES = 128
VMEM = pl.BlockSpec(memory_space=pltpu.VMEM)
SMEM = pl.BlockSpec(memory_space=pltpu.SMEM)
ANY = pl.BlockSpec(memory_space=pl.ANY)


def call(body, ins, outs, scratch=(), copies=0, flops=0, nbytes=0, vmem=40, name=None):
    kernel = pl.pallas_call(
        body,
        out_shape=tuple(pltpu.HBM(shape, dtype) if memory is ANY else jax.ShapeDtypeStruct(shape, dtype) for shape, dtype, memory in outs),
        in_specs=list(ins),
        out_specs=tuple(memory for _, _, memory in outs),
        scratch_shapes=list(scratch) + ([pltpu.SemaphoreType.DMA((copies,))] if copies else []),
        compiler_params=pltpu.CompilerParams(vmem_limit_bytes=vmem * 2**20),
        cost_estimate=pl.CostEstimate(flops=flops, bytes_accessed=nbytes, transcendentals=0),
        name=name,
    )

    def run(*operands):
        return kernel(*(
            pltpu.with_memory_space_constraint(x, pltpu.HBM) if memory is ANY else x
            for x, memory in zip(operands, ins)
        ))

    return run


def log2(value):
    assert value & (value - 1) == 0
    return value.bit_length() - 1


def iota(shape, dim):
    return lax.broadcasted_iota(I32, shape, dim)


def one(mask):
    return jnp.where(mask, 1.0, 0.0).astype(BF16)


def split2(x):
    top = x.astype(BF16)
    rest = (x - top.astype(F32)).astype(BF16)
    return jnp.concatenate([top, rest], axis=-1)


def split3(x):
    top = x.astype(BF16)
    rest = x - top.astype(F32)
    middle = rest.astype(BF16)
    last = (rest - middle.astype(F32)).astype(BF16)
    return jnp.concatenate([top, middle, last], axis=-1)


def dot(a, b):
    return lax.dot_general(a, b, (((1,), (0,)), ((), ())), preferred_element_type=F32)


def dot_nt(a, b):
    return lax.dot_general(a, b, (((1,), (1,)), ((), ())), preferred_element_type=F32)


def dot_tn(a, b):
    return lax.dot_general(a, b, (((0,), (0,)), ((), ())), preferred_element_type=F32)


def fold(x, parts):
    width = x.shape[-1] // parts
    total = x[..., (parts - 1) * width :]
    for part in reversed(range(parts - 1)):
        total = total + x[..., part * width : (part + 1) * width]
    return total


class Sizes:
    def __init__(self, devices, rows, slots, width, steps, bags, lookups, listed):
        self.devices, self.rows, self.slots, self.width = devices, rows, slots, width
        self.steps, self.bags, self.lookups, self.listed = steps, bags, lookups, listed
        self.cap = 2 * listed // devices
        self.places = devices * self.cap
        self.block = slots // devices
        self.chunks = self.places // LANES
        self.chunk = slots // self.chunks
        self.chunk_blocks = devices // self.chunks
        self.group = 256 // lookups
        self.groups = bags // self.group
        self.row_tiles = rows // LANES
        self.wide = (self.places, width)
        assert width == LANES and self.cap % 8 == 0 and self.chunk % self.block == 0
        assert self.groups * self.group == bags and self.group % 16 == 0
        assert slots // 256 * self.group <= 256 and self.row_tiles <= LANES

    def part(self, c):
        return slice(c * self.chunk, (c + 1) * self.chunk)


def lane_part(c):
    return slice(c * LANES, (c + 1) * LANES)


class Copies:
    def __init__(self, sems):
        self.sems, self.used, self.open = sems, 0, []

    def start(self, source, target):
        copy = pltpu.make_async_copy(source, target, self.sems.at[self.used])
        self.used += 1
        copy.start()
        return copy

    def send(self, source, target):
        self.open.append(self.start(source, target))

    def finish(self):
        for copy in self.open:
            copy.wait()


def place_of(z, dirty_ref, place_ref):
    earlier = iota((z.chunk, z.chunk), 0)
    later = iota((z.chunk, z.chunk), 1)
    shift = log2(z.block)
    before = one((earlier < later) & ((earlier >> shift) == (later >> shift)))
    base = ((iota((z.chunks, z.chunk), 1) >> shift) * z.cap).astype(F32)
    for t in range(z.steps):
        listed = dirty_ref[t : t + 1, :]
        high, low = listed >> log2(z.chunk), listed & (z.chunk - 1)
        chosen_high = one(iota((z.chunks, z.listed), 0) == high)
        chosen_low = one(iota((z.chunk, z.listed), 0) == low)
        chosen = dot_nt(chosen_high, chosen_low)
        rank = dot(chosen.astype(BF16), before)
        place_ref[t * z.chunks : (t + 1) * z.chunks, :] = jnp.where(chosen > 0.5, base + rank, -1.0)


def pick_of(z, place_ref, t, c):
    row = t * z.chunks + c
    return one(iota((LANES, z.chunk), 0).astype(F32) == place_ref[row : row + 1, :])


def keep_of(z, pick):
    return 1.0 - dot_tn(pick, jnp.ones((LANES, LANES), BF16))


def count_into(z, ids, count_ref, key_ref, low_ref):
    lanes = z.group * z.lookups
    spread = one((iota((z.lookups, lanes), 1) & (z.lookups - 1)) == iota((z.lookups, lanes), 0))
    bag_of_lane = iota((z.bags, lanes), 1) >> log2(z.lookups)
    mine = bag_of_lane == (iota((z.bags, lanes), 0) & (z.group - 1))
    high = dot_tn((ids >> 8).astype(F32).astype(BF16), spread)
    low = dot_tn((ids & 255).astype(F32).astype(BF16), spread)
    key = high * z.group + bag_of_lane.astype(F32)
    key_ref[...] = jnp.sum(jnp.where(mine, key, 0.0).reshape(z.groups, z.group, lanes), axis=1)
    low_ref[...] = jnp.sum(jnp.where(mine, low, 0.0).reshape(z.groups, z.group, lanes), axis=1)
    tiles = z.slots // 256
    for g in range(z.groups):
        key_row = key_ref[g : g + 1, :].astype(I32)
        low_row = low_ref[g : g + 1, :].astype(I32)
        left = one(iota((tiles * z.group, lanes), 0) == key_row)
        right = one(iota((256, lanes), 0) == low_row)
        counts = dot_nt(left, right).astype(BF16)
        for h in range(tiles):
            count_ref[g * z.group : (g + 1) * z.group, h * 256 : (h + 1) * 256] = counts[
                h * z.group : (h + 1) * z.group, :
            ]


def count_scratch(z):
    lanes = z.group * z.lookups
    return [pltpu.VMEM((z.groups, lanes), F32), pltpu.VMEM((z.groups, lanes), F32)]


def send_chunk(z, c, copies, owner, values_ref, out_ref):
    for b in range(c * z.chunk_blocks, (c + 1) * z.chunk_blocks):
        start = pl.multiple_of(owner(b) * z.cap, z.cap)
        copies.send(values_ref.at[b * z.cap : (b + 1) * z.cap, :], out_ref.at[pl.ds(start, z.cap), :])


def from_owners(z, back_ref, owner_ref, out_ref):
    for b in range(z.devices):
        start = pl.multiple_of(owner_ref[b] * z.cap, z.cap)
        out_ref[b * z.cap : (b + 1) * z.cap, :] = back_ref[pl.ds(start, z.cap), :]


def place_kernel(z, rows_hbm, tiled_hbm, dirty_hbm, owner_ref, place_ref, index_ref, rows_ref, tiled_ref, dirty_ref, sems):
    copies = Copies(sems)
    dirty_in = copies.start(dirty_hbm, dirty_ref)
    tiled_in = copies.start(tiled_hbm, tiled_ref)
    rows_in = copies.start(rows_hbm, rows_ref)
    dirty_in.wait()
    place_of(z, dirty_ref, place_ref)
    tiled_in.wait()
    local = tiled_ref[...] & (z.rows - 1)
    pieces = z.chunk // LANES
    for c in range(z.chunks):
        row = jnp.concatenate([local[c * pieces + k : c * pieces + k + 1, :] for k in range(pieces)], axis=1)
        parts = jnp.where(iota((8, z.chunk), 0) == 0, row >> 7, row & 127).astype(F32).astype(BF16)
        for t in range(z.steps):
            found = dot_nt(parts, pick_of(z, place_ref, t, c))
            index = found[0:1, :] * 128.0 + found[1:2, :]
            index_ref[t * z.chunks + c : t * z.chunks + c + 1, :] = index.astype(I32)
    rows_in.wait()
    for b in range(z.devices):
        owner_ref[b] = rows_ref[b * z.block] >> log2(z.rows)


def first_kernel(z, owner_ref, place_ref, ids_ref, targets_hbm, cache_hbm, pending_hbm,
                 grad_hbm, count_hbm, out_hbm,
                 grad_ref, key_ref, low_ref, targets_ref, cache_ref, pending_ref, count_ref, flush_ref, sems):
    copies = Copies(sems)
    cache_in = copies.start(cache_hbm, cache_ref)
    targets_in = copies.start(targets_hbm.at[0], targets_ref)
    pending_in = copies.start(pending_hbm, pending_ref)
    count_into(z, ids_ref[0], count_ref, key_ref, low_ref)
    copies.send(count_ref, count_hbm)
    targets_in.wait()
    cache_in.wait()
    total = jnp.zeros((z.bags, 2 * z.width), F32)
    for c in range(z.chunks):
        total = total + dot(count_ref[:, z.part(c)], split2(cache_ref[z.part(c), :]))
    pooled = fold(total, 2) * (1.0 / z.lookups)
    grad = split2((pooled - targets_ref[...]) * (1.0 / z.lookups))
    grad_ref[...] = grad
    copies.send(grad_ref, grad_hbm)
    pending_in.wait()
    for c in range(z.chunks):
        pick = pick_of(z, place_ref, 0, c)
        lookups = dot_nt(pick, count_ref[:, z.part(c)]).astype(BF16)
        flush_ref[lane_part(c), :] = fold(dot(pick, split3(pending_ref[z.part(c), :])), 3) + fold(
            dot(lookups, grad), 2
        )
        send_chunk(z, c, copies, lambda b: owner_ref[b], flush_ref, out_hbm)
    copies.finish()


def next_kernel(z, t, place_ref, grad_hbm, ids_hbm, targets_hbm, cache_hbm, pending_hbm, count_hbm,
                pending_out, waiting_out, new_count_hbm, back_ref, flush_out, base_ref,
                grad_ref, sent_ref, key_ref, low_ref, ids_ref, targets_ref, cache_ref, pending_ref, count_ref, new_ref, sems):
    copies = Copies(sems)
    flush_ref, waiting_ref = (sent_ref, waiting_out) if t == 0 else (flush_out, sent_ref)
    ids_in = copies.start(ids_hbm.at[t + 1], ids_ref)
    cache_in = copies.start(cache_hbm, cache_ref)
    targets_in = copies.start(targets_hbm.at[t + 1], targets_ref)
    pending_in = copies.start(pending_hbm, pending_ref)
    count_in = copies.start(count_hbm, count_ref)
    grad_in = copies.start(grad_hbm, grad_ref)
    ids_in.wait()
    count_into(z, ids_ref[...], new_ref, key_ref, low_ref)
    copies.send(new_ref, new_count_hbm)
    cache_in.wait()
    total = jnp.zeros((z.bags, 2 * z.width), F32)
    for c in range(z.chunks):
        counts = new_ref[:, z.part(c)]
        pick = pick_of(z, place_ref, t, c)
        value = cache_ref[z.part(c), :]
        if t == 0:
            value = value * keep_of(z, pick)
        total = total + dot(counts, split2(value))
        back_ref[:, lane_part(c)] = dot_nt(counts, pick).astype(BF16)
        flush_ref[lane_part(c), :] = dot_nt(pick_of(z, place_ref, t + 1, c), counts).astype(BF16)
    targets_in.wait()
    base_ref[...] = fold(total, 2) * (1.0 / z.lookups) - targets_ref[...]
    if t == 0:
        copies.send(flush_ref, flush_out)
    grad_in.wait()
    pending_in.wait()
    count_in.wait()
    add_pending(z, t, place_ref, grad_ref, count_ref, pending_ref, waiting_ref)
    copies.send(pending_ref, pending_out)
    if t > 0:
        copies.send(waiting_ref, waiting_out)
    copies.finish()


def add_pending(z, t, place_ref, grad_ref, count_ref, pending_ref, waiting_ref):
    for c in range(z.chunks):
        added = fold(dot_tn(count_ref[:, z.part(c)], grad_ref[...]), 2)
        value = (pending_ref[z.part(c), :] + added) * keep_of(z, pick_of(z, place_ref, t, c))
        pending_ref[z.part(c), :] = value
        if waiting_ref is not None:
            waiting_ref[lane_part(c), :] = fold(dot(pick_of(z, place_ref, t + 1, c), split3(value)), 3)


def step_kernel(z, t, owner_ref, back_ref, counts_ref, base_ref, flush_counts, waiting,
                grad_hbm, out_hbm, grad_ref, order_ref, flush_ref, loaded_ref, sems):
    copies = Copies(sems)
    load = copies.start(flush_counts if t == 0 else waiting, loaded_ref)
    flush_counts_ref, waiting_ref = (loaded_ref, waiting) if t == 0 else (flush_counts, loaded_ref)
    from_owners(z, back_ref, owner_ref, order_ref)
    total = fold(dot(counts_ref[...], split2(order_ref[...])), 2)
    grad = split2((base_ref[...] + total * (1.0 / z.lookups)) * (1.0 / z.lookups))
    grad_ref[...] = grad
    copies.send(grad_ref, grad_hbm)
    load.wait()
    for c in range(z.chunks):
        part = lane_part(c)
        flush_ref[part, :] = waiting_ref[part, :] + fold(dot(flush_counts_ref[part, :], grad), 2)
        send_chunk(z, c, copies, lambda b: owner_ref[b], flush_ref, out_hbm)
    copies.finish()


def column(row):
    return jnp.transpose(jnp.broadcast_to(row, (LANES, LANES)))


def owner_kernel(z, t, far, got_ref, index_ref, accum_ref, old, answer_hbm, extra_hbm,
                 answer_ref, extra_ref, *rest):
    copies = Copies(rest[-1])
    old_ref = rest[0] if far else old
    if far:
        old_in = copies.start(old, old_ref)
    got = split2(got_ref[...])
    rows = [index_ref[t * z.chunks + c : t * z.chunks + c + 1, :].astype(F32) for c in range(z.chunks)]
    for c in range(z.chunks):
        part = lane_part(c)
        col = column(rows[c])
        same = jnp.concatenate([one(col == row) for row in rows], axis=1)
        grad = fold(dot(same, got), 2)
        extra = jnp.mean(grad * grad, axis=1, keepdims=True)
        fresh = column(accum_ref[c : c + 1, :]) + extra
        change = LEARN_RATE * grad / jnp.sqrt(fresh)
        extra_ref[part, :] = jnp.broadcast_to(extra, (LANES, LANES))
        copies.send(extra_ref.at[part, :], extra_hbm.at[part, :])
        if far:
            answer_ref[part, :] = change
        else:
            answer_ref[part, :] = old_ref[part, :] - change
            copies.send(answer_ref.at[part, :], answer_hbm.at[part, :])
    if far:
        old_in.wait()
        answer_ref[...] = old_ref[...] - answer_ref[...]
        copies.send(answer_ref, answer_hbm)
    copies.finish()


def gather_rows(z, t, flat_ref, table_ref, out_ref):
    def step(g, carry):
        base = pl.multiple_of(g * 32, 32)
        for k in range(32):
            row = flat_ref[t * z.places + base + k]
            out_ref[pl.ds(base + k, 1), :] = table_ref[pl.ds(row, 1), :]
        return carry

    lax.fori_loop(0, z.places // 32, step, 0)


def put_rows(z, t, flat_ref, answer_ref, table_ref):
    def step(g, carry):
        base = pl.multiple_of(g * 32, 32)
        for k in range(32):
            row = flat_ref[t * z.places + base + k]
            table_ref[pl.ds(row, 1), :] = answer_ref[pl.ds(base + k, 1), :]
        return carry

    lax.fori_loop(0, z.places // 32, step, 0)


def high_low(z, row):
    col = column(row)
    high = col >> 7 == iota((LANES, z.row_tiles), 1) if z.row_tiles == LANES else (
        col[:, : z.row_tiles] >> 7 == iota((LANES, z.row_tiles), 1)
    )
    return one(high), col & 127 == iota((LANES, LANES), 1)


def gather_accum(z, t, index_ref, accum, out_ref):
    parts = split3(accum)
    for c in range(z.chunks):
        now = t * z.chunks + c
        high, low = high_low(z, index_ref[now : now + 1, :])
        value = jnp.sum(jnp.where(low, fold(dot(high, parts), 3), 0.0), axis=1, keepdims=True)
        out_ref[c : c + 1, :] = jnp.transpose(jnp.broadcast_to(value, (LANES, LANES)))[0:1, :]


def put_accum(z, t, index_ref, accum, extra_ref):
    rows = [index_ref[t * z.chunks + c : t * z.chunks + c + 1, :] for c in range(z.chunks)]
    for i in range(z.chunks):
        col = column(rows[i])
        seen = jnp.where((col == rows[i]) & (iota((LANES, LANES), 1) < iota((LANES, LANES), 0)), 1.0, 0.0)
        for j in range(i):
            seen = jnp.where(col == rows[j], 1.0, seen)
        again = jnp.max(seen, axis=1, keepdims=True)
        high, low = high_low(z, rows[i])
        add = jnp.where(low & (again < 0.5), extra_ref[lane_part(i), :], 0.0)
        accum = accum + fold(dot_tn(high, split3(add)), 3)
    return accum


def start_kernel(z, flat_ref, index_ref, accum_ref, table_hbm, old_accum_ref, old_ref, table_ref, sems):
    copies = Copies(sems)
    table_in = copies.start(table_hbm, table_ref)
    gather_accum(z, 0, index_ref, accum_ref[...], old_accum_ref)
    table_in.wait()
    gather_rows(z, 0, flat_ref, table_ref, old_ref)


def update_kernel(z, t, owner_ref, flat_ref, index_ref, accum_ref, place_ref, back_ref,
                  table_hbm, answer_hbm, extra_hbm, cache_hbm,
                  new_accum_ref, old_accum_ref, table_out, old, cache_out,
                  table_ref, answer_ref, extra_ref, cache_ref, order_ref, *rest):
    copies = Copies(rest[-1])
    last = t + 2 == z.steps
    old_ref = rest[0] if last else old
    answer_in = copies.start(answer_hbm, answer_ref)
    table_in = copies.start(table_hbm, table_ref)
    cache_in = copies.start(cache_hbm, cache_ref)
    extra_in = copies.start(extra_hbm, extra_ref)
    answer_in.wait()
    table_in.wait()
    put_rows(z, t, flat_ref, answer_ref, table_ref)
    copies.send(table_ref, table_out)
    gather_rows(z, t + 1, flat_ref, table_ref, old_ref)
    if last:
        copies.send(old_ref, old)
    extra_in.wait()
    accum = put_accum(z, t, index_ref, accum_ref[...], extra_ref)
    new_accum_ref[...] = accum
    gather_accum(z, t + 1, index_ref, accum, old_accum_ref)
    from_owners(z, back_ref, owner_ref, order_ref)
    cache_in.wait()
    new_ref = cache_out if last else cache_ref
    for c in range(z.chunks):
        pick = pick_of(z, place_ref, t, c)
        value = cache_ref[z.part(c), :]
        if t == 0:
            value = value * keep_of(z, pick)
        value = value + fold(dot_tn(pick, split3(order_ref[lane_part(c), :])), 3)
        new_ref[z.part(c), :] = value * keep_of(z, pick_of(z, place_ref, t + 1, c))
    if not last:
        copies.send(cache_ref, cache_out)
    copies.finish()


def last_update_kernel(z, flat_ref, index_ref, accum_ref, place_ref, grad_hbm,
                       table_hbm, answer_hbm, extra_hbm, pending_hbm, count_hbm,
                       new_accum_ref, table_out, pending_out,
                       grad_ref, table_ref, answer_ref, extra_ref, pending_ref, count_ref, sems):
    t = z.steps - 1
    copies = Copies(sems)
    answer_in = copies.start(answer_hbm, answer_ref)
    table_in = copies.start(table_hbm, table_ref)
    extra_in = copies.start(extra_hbm, extra_ref)
    count_in = copies.start(count_hbm, count_ref)
    pending_in = copies.start(pending_hbm, pending_ref)
    grad_in = copies.start(grad_hbm, grad_ref)
    answer_in.wait()
    table_in.wait()
    put_rows(z, t, flat_ref, answer_ref, table_ref)
    copies.send(table_ref, table_out)
    extra_in.wait()
    new_accum_ref[...] = put_accum(z, t, index_ref, accum_ref[...], extra_ref)
    grad_in.wait()
    count_in.wait()
    pending_in.wait()
    add_pending(z, t, place_ref, grad_ref, count_ref, pending_ref, None)
    copies.send(pending_ref, pending_out)
    copies.finish()


def last_cache_kernel(z, owner_ref, back_ref, place_ref, cache_ref, cache_out, order_ref, new_ref, sems):
    t = z.steps - 1
    copies = Copies(sems)
    from_owners(z, back_ref, owner_ref, order_ref)
    for c in range(z.chunks):
        pick = pick_of(z, place_ref, t, c)
        new_ref[z.part(c), :] = cache_ref[z.part(c), :] + fold(
            dot_tn(pick, split3(order_ref[lane_part(c), :])), 3
        )
        copies.send(new_ref.at[z.part(c), :], cache_out.at[z.part(c), :])
    copies.finish()


def body(table, accum, cache, cache_rows, pending, batch_slots, targets, dirty):
    z = Sizes(
        lax.axis_size(AXES), table.shape[0], cache.shape[0], cache.shape[1],
        batch_slots.shape[0], batch_slots.shape[1], batch_slots.shape[2], dirty.shape[1],
    )
    ids = batch_slots.transpose(0, 2, 1)
    wide, slots = z.wide, (z.slots, z.width)
    count, grads = ((z.bags, z.slots), BF16), ((z.bags, 2 * z.width), BF16)
    accums = ((z.row_tiles, LANES), F32)
    big = 2 * z.bags * z.slots * 2 * z.width

    def buf(shape, dtype=F32):
        return pltpu.VMEM(shape, dtype)

    def exchange(values):
        values = values.reshape(z.devices, z.cap, z.width)
        return lax.all_to_all(values, AXES, split_axis=0, concat_axis=0, tiled=True).reshape(wide)

    owner, place, index = call(
        functools.partial(place_kernel, z), [ANY] * 3,
        [((z.devices,), I32, SMEM), ((z.steps * z.chunks, z.chunk), F32, VMEM),
         ((z.steps * z.chunks, LANES), I32, VMEM)],
        scratch=[pltpu.SMEM((z.slots,), I32), buf((z.slots // LANES, LANES), I32), buf(dirty.shape, I32)],
        copies=3, flops=10**9, nbytes=2**20, name="place",
    )(cache_rows, cache_rows.reshape(-1, LANES), dirty)

    index = index.reshape(z.steps, z.devices, z.cap).transpose(1, 0, 2).reshape(z.devices, -1)
    to = owner[None, :] == jnp.arange(z.devices, dtype=I32)[:, None]
    index = jnp.sum(jnp.where(to[:, :, None], index[None], 0), axis=1)
    index = lax.all_to_all(index.reshape(z.devices, 1, -1), AXES, split_axis=0, concat_axis=0, tiled=True)
    grad, counts, outgoing = call(
        functools.partial(first_kernel, z), [SMEM, VMEM, VMEM] + [ANY] * 3, [(*grads, ANY), (*count, ANY), (wide, F32, ANY)],
        scratch=[buf(*grads)] + count_scratch(z) + [
            buf(targets.shape[1:]), buf(slots), buf(slots), buf(*count), buf(wide)],
        copies=5 + z.devices, flops=6 * big, nbytes=2**24, name="first",
    )(owner, place, ids, targets, cache, pending)
    got = exchange(outgoing)
    index = index.reshape(z.devices, z.steps, z.cap).transpose(1, 0, 2)
    flat = index.reshape(-1)
    index = index.reshape(z.steps * z.chunks, LANES)
    accum = accum.reshape(accums[0])

    old_accum, old = call(
        functools.partial(start_kernel, z), [SMEM, VMEM, VMEM, ANY],
        [((z.chunks, LANES), F32, VMEM), (wide, F32, VMEM)],
        scratch=[buf(table.shape)], copies=1, flops=10**9, nbytes=2**23, name="start",
    )(flat, index, accum, table)

    for t in range(z.steps):
        far = t == z.steps - 1
        answer, extra = call(
            functools.partial(owner_kernel, z, t, far), [VMEM] * 3 + [ANY if far else VMEM],
            [(wide, F32, ANY), (wide, F32, ANY)],
            scratch=[buf(wide)] * (3 if far else 2), copies=2 + 2 * z.chunks, flops=10**9, nbytes=2**21,
            vmem=24, name="owner",
        )(got, index, old_accum, old)
        answer, extra, grad = lax.optimization_barrier((answer, extra, grad))
        back = exchange(answer)
        if t == z.steps - 1:
            break
        early, late = (VMEM, ANY) if t == 0 else (ANY, VMEM)
        sent = buf((z.places, z.bags), BF16) if t == 0 else buf(wide)
        pending, waiting, counts, back_counts, flush_counts, base = call(
            functools.partial(next_kernel, z, t), [VMEM, ANY, ANY, ANY, ANY, ANY, ANY],
            [(slots, F32, ANY), (wide, F32, early), (*count, ANY), ((z.bags, z.places), BF16, VMEM),
             ((z.places, z.bags), BF16, late), ((z.bags, z.width), F32, VMEM)],
            scratch=[buf(*grads), sent] + count_scratch(z) + [
                buf(ids.shape[1:], I32), buf(targets.shape[1:]), buf(slots), buf(slots), buf(*count), buf(*count)],
            copies=9, flops=8 * big, nbytes=2**24, name="next",
        )(place, grad, ids, targets, cache, pending, counts)
        grad, outgoing = call(
            functools.partial(step_kernel, z, t), [SMEM, VMEM, VMEM, VMEM, late, early],
            [(*grads, ANY), (wide, F32, ANY)],
            scratch=[buf(*grads), buf(wide), buf(wide), sent], copies=2 + z.devices, flops=10**9, nbytes=2**22, vmem=24, name="step",
        )(owner, back, back_counts, base, flush_counts, waiting)
        outgoing, back, answer = lax.optimization_barrier((outgoing, back, answer))
        got = exchange(outgoing)
        accum, old_accum, table, old, cache = call(
            functools.partial(update_kernel, z, t), [SMEM, SMEM, VMEM, VMEM, VMEM, VMEM, ANY, ANY, ANY, ANY],
            [(*accums, VMEM), ((z.chunks, LANES), F32, VMEM), (table.shape, F32, ANY), (wide, F32, ANY if t + 2 == z.steps else VMEM),
             (slots, F32, VMEM if t + 2 == z.steps else ANY)],
            scratch=[buf(table.shape), buf(wide), buf(wide), buf(slots), buf(wide)]
            + ([buf(wide)] if t + 2 == z.steps else []),
            copies=7, flops=3 * big, nbytes=2**24, name="update",
        )(owner, flat, index, accum, place, back, table, answer, extra, cache)
    accum, table, pending = call(
        functools.partial(last_update_kernel, z), [SMEM, VMEM, VMEM, VMEM] + [ANY] * 6,
        [(*accums, VMEM), (table.shape, F32, ANY), (slots, F32, ANY)],
        scratch=[buf(*grads), buf(table.shape), buf(wide), buf(wide), buf(slots), buf(*count)],
        copies=8, flops=3 * big, nbytes=2**24, name="last_update",
    )(flat, index, accum, place, grad, table, answer, extra, pending, counts)
    cache = call(
        functools.partial(last_cache_kernel, z), [SMEM, VMEM, VMEM, VMEM], [(slots, F32, ANY)],
        scratch=[buf(wide), buf(slots)], copies=z.chunks, flops=big, nbytes=2**22, vmem=24, name="last_cache",
    )(owner, back, place, cache)[0]
    return (table, accum.reshape(-1), cache, pending)


def solution(mesh):
    in_specs = (
        P(AXES, None),
        P(AXES),
        P(AXES, None),
        P(AXES),
        P(AXES, None),
        P(None, AXES, None),
        P(None, AXES, None),
        P(None, AXES),
    )
    out_specs = (P(AXES, None), P(AXES), P(AXES, None), P(AXES, None))
    return jax.shard_map(body, mesh=mesh, in_specs=in_specs, out_specs=out_specs, check_vma=False)
```

```python
import functools

import jax
import jax.numpy as jnp
from jax import lax
from jax.experimental import pallas as pl
from jax.experimental.pallas import tpu as pltpu
from jax.sharding import PartitionSpec as P

LEARN_RATE = 0.3
AXES = ("gx", "gy")
F32, BF16, I32 = jnp.float32, jnp.bfloat16, jnp.int32
LANES = 128
VMEM = pl.BlockSpec(memory_space=pltpu.VMEM)
SMEM = pl.BlockSpec(memory_space=pltpu.SMEM)
ANY = pl.BlockSpec(memory_space=pl.ANY)


def call(body, ins, outs, scratch=(), copies=0, flops=0, nbytes=0, vmem=40, name=None):
    kernel = pl.pallas_call(
        body,
        out_shape=tuple(pltpu.HBM(shape, dtype) if memory is ANY else jax.ShapeDtypeStruct(shape, dtype) for shape, dtype, memory in outs),
        in_specs=list(ins),
        out_specs=tuple(memory for _, _, memory in outs),
        scratch_shapes=list(scratch) + ([pltpu.SemaphoreType.DMA((copies,))] if copies else []),
        compiler_params=pltpu.CompilerParams(vmem_limit_bytes=vmem * 2**20),
        cost_estimate=pl.CostEstimate(flops=flops, bytes_accessed=nbytes, transcendentals=0),
        name=name,
    )

    def run(*operands):
        return kernel(*(
            pltpu.with_memory_space_constraint(x, pltpu.HBM) if memory is ANY else x
            for x, memory in zip(operands, ins)
        ))

    return run


def log2(value):
    assert value & (value - 1) == 0
    return value.bit_length() - 1


def iota(shape, dim):
    return lax.broadcasted_iota(I32, shape, dim)


def one(mask):
    return jnp.where(mask, 1.0, 0.0).astype(BF16)


def split2(x):
    top = x.astype(BF16)
    rest = (x - top.astype(F32)).astype(BF16)
    return jnp.concatenate([top, rest], axis=-1)


def split3(x):
    top = x.astype(BF16)
    rest = x - top.astype(F32)
    middle = rest.astype(BF16)
    last = (rest - middle.astype(F32)).astype(BF16)
    return jnp.concatenate([top, middle, last], axis=-1)


def dot(a, b):
    return lax.dot_general(a, b, (((1,), (0,)), ((), ())), preferred_element_type=F32)


def dot_nt(a, b):
    return lax.dot_general(a, b, (((1,), (1,)), ((), ())), preferred_element_type=F32)


def dot_tn(a, b):
    return lax.dot_general(a, b, (((0,), (0,)), ((), ())), preferred_element_type=F32)


def fold(x, parts):
    width = x.shape[-1] // parts
    total = x[..., (parts - 1) * width :]
    for part in reversed(range(parts - 1)):
        total = total + x[..., part * width : (part + 1) * width]
    return total


class Sizes:
    def __init__(self, devices, rows, slots, width, steps, bags, lookups, listed):
        self.devices, self.rows, self.slots, self.width = devices, rows, slots, width
        self.steps, self.bags, self.lookups, self.listed = steps, bags, lookups, listed
        self.cap = 2 * listed // devices
        self.places = devices * self.cap
        self.block = slots // devices
        self.chunks = self.places // LANES
        self.chunk = slots // self.chunks
        self.chunk_blocks = devices // self.chunks
        self.group = 256 // lookups
        self.groups = bags // self.group
        self.row_tiles = rows // LANES
        self.wide = (self.places, width)
        assert LANES % self.cap == 0 and self.steps <= 8
        assert width == LANES and self.cap % 8 == 0 and self.chunk % self.block == 0
        assert self.groups * self.group == bags and self.group % 16 == 0
        assert slots // 256 * self.group <= 256 and self.row_tiles <= LANES

    def part(self, c):
        return slice(c * self.chunk, (c + 1) * self.chunk)


def lane_part(c):
    return slice(c * LANES, (c + 1) * LANES)


class Copies:
    def __init__(self, sems):
        self.sems, self.used, self.open = sems, 0, []

    def start(self, source, target):
        copy = pltpu.make_async_copy(source, target, self.sems.at[self.used])
        self.used += 1
        copy.start()
        return copy

    def send(self, source, target):
        self.open.append(self.start(source, target))

    def finish(self):
        for copy in self.open:
            copy.wait()


def place_of(z, dirty_ref, place_ref):
    earlier = iota((z.chunk, z.chunk), 0)
    later = iota((z.chunk, z.chunk), 1)
    shift = log2(z.block)
    before = one((earlier < later) & ((earlier >> shift) == (later >> shift)))
    base = ((iota((z.chunks, z.chunk), 1) >> shift) * z.cap).astype(F32)
    for t in range(z.steps):
        listed = dirty_ref[t : t + 1, :]
        high, low = listed >> log2(z.chunk), listed & (z.chunk - 1)
        chosen_high = one(iota((z.chunks, z.listed), 0) == high)
        chosen_low = one(iota((z.chunk, z.listed), 0) == low)
        chosen = dot_nt(chosen_high, chosen_low)
        rank = dot(chosen.astype(BF16), before)
        place_ref[t * z.chunks : (t + 1) * z.chunks, :] = jnp.where(chosen > 0.5, base + rank, -1.0)


def pick_of(z, place_ref, t, c):
    row = t * z.chunks + c
    return one(iota((LANES, z.chunk), 0).astype(F32) == place_ref[row : row + 1, :])


def keep_of(z, pick):
    return 1.0 - dot_tn(pick, jnp.ones((LANES, LANES), BF16))


def count_into(z, ids, count_ref, key_ref, low_ref):
    lanes = z.group * z.lookups
    spread = one((iota((z.lookups, lanes), 1) & (z.lookups - 1)) == iota((z.lookups, lanes), 0))
    bag_of_lane = iota((z.bags, lanes), 1) >> log2(z.lookups)
    mine = bag_of_lane == (iota((z.bags, lanes), 0) & (z.group - 1))
    high = dot_tn((ids >> 8).astype(F32).astype(BF16), spread)
    low = dot_tn((ids & 255).astype(F32).astype(BF16), spread)
    key = high * z.group + bag_of_lane.astype(F32)
    key_ref[...] = jnp.sum(jnp.where(mine, key, 0.0).reshape(z.groups, z.group, lanes), axis=1)
    low_ref[...] = jnp.sum(jnp.where(mine, low, 0.0).reshape(z.groups, z.group, lanes), axis=1)
    tiles = z.slots // 256
    for g in range(z.groups):
        key_row = key_ref[g : g + 1, :].astype(I32)
        low_row = low_ref[g : g + 1, :].astype(I32)
        left = one(iota((tiles * z.group, lanes), 0) == key_row)
        right = one(iota((256, lanes), 0) == low_row)
        counts = dot_nt(left, right).astype(BF16)
        for h in range(tiles):
            count_ref[g * z.group : (g + 1) * z.group, h * 256 : (h + 1) * 256] = counts[
                h * z.group : (h + 1) * z.group, :
            ]


def count_scratch(z):
    lanes = z.group * z.lookups
    return [pltpu.VMEM((z.groups, lanes), F32), pltpu.VMEM((z.groups, lanes), F32)]


def send_chunk(z, c, copies, owner, values_ref, out_ref):
    for b in range(c * z.chunk_blocks, (c + 1) * z.chunk_blocks):
        start = pl.multiple_of(owner(b) * z.cap, z.cap)
        copies.send(values_ref.at[b * z.cap : (b + 1) * z.cap, :], out_ref.at[pl.ds(start, z.cap), :])


def from_owners(z, back_ref, owner_ref, out_ref):
    for b in range(z.devices):
        start = pl.multiple_of(owner_ref[b] * z.cap, z.cap)
        out_ref[b * z.cap : (b + 1) * z.cap, :] = back_ref[pl.ds(start, z.cap), :]


def place_kernel(z, rows_hbm, tiled_hbm, dirty_hbm, owner_ref, place_ref, tiles_hbm,
                 rows_ref, tiled_ref, dirty_ref, tiles_ref, sems):
    copies = Copies(sems)
    dirty_in = copies.start(dirty_hbm, dirty_ref)
    tiled_in = copies.start(tiled_hbm, tiled_ref)
    rows_in = copies.start(rows_hbm, rows_ref)
    dirty_in.wait()
    place_of(z, dirty_ref, place_ref)
    tiled_in.wait()
    rows_in.wait()
    tiles_ref[...] = jnp.zeros_like(tiles_ref)
    local = tiled_ref[...] & (z.rows - 1)
    pieces = z.chunk // LANES
    step = iota((8, LANES), 0)
    block = iota((8, LANES), 1) >> log2(z.cap)
    for c in range(z.chunks):
        row = jnp.concatenate([local[c * pieces + k : c * pieces + k + 1, :] for k in range(pieces)], axis=1)
        parts = jnp.where(iota((8, z.chunk), 0) == 0, row >> 7, row & 127).astype(F32).astype(BF16)
        index = jnp.zeros((8, LANES), F32)
        for t in range(z.steps):
            found = dot_nt(parts, pick_of(z, place_ref, t, c))
            index = jnp.where(step == t, found[0:1, :] * 128.0 + found[1:2, :], index)
        for j in range(z.chunk_blocks):
            tile = jnp.where(block == j, index, 0.0)
            shift = z.cap
            while shift < LANES:
                tile = tile + pltpu.roll(tile, shift, 1)
                shift *= 2
            b = c * z.chunk_blocks + j
            owner = rows_ref[b * z.block] >> log2(z.rows)
            owner_ref[b] = owner
            tiles_ref[pl.ds(pl.multiple_of(owner * 8, 8), 8), :] = tile.astype(I32)
    copies.send(tiles_ref, tiles_hbm)
    copies.finish()


def first_kernel(z, owner_ref, place_ref, ids_ref, targets_hbm, cache_hbm, pending_hbm,
                 grad_hbm, count_hbm, out_hbm,
                 grad_ref, key_ref, low_ref, targets_ref, cache_ref, pending_ref, count_ref, flush_ref, sems):
    copies = Copies(sems)
    cache_in = copies.start(cache_hbm, cache_ref)
    targets_in = copies.start(targets_hbm.at[0], targets_ref)
    pending_in = copies.start(pending_hbm, pending_ref)
    count_into(z, ids_ref[0], count_ref, key_ref, low_ref)
    copies.send(count_ref, count_hbm)
    targets_in.wait()
    cache_in.wait()
    total = jnp.zeros((z.bags, 2 * z.width), F32)
    for c in range(z.chunks):
        total = total + dot(count_ref[:, z.part(c)], split2(cache_ref[z.part(c), :]))
    pooled = fold(total, 2) * (1.0 / z.lookups)
    grad = split2((pooled - targets_ref[...]) * (1.0 / z.lookups))
    grad_ref[...] = grad
    copies.send(grad_ref, grad_hbm)
    pending_in.wait()
    for c in range(z.chunks):
        pick = pick_of(z, place_ref, 0, c)
        lookups = dot_nt(pick, count_ref[:, z.part(c)]).astype(BF16)
        flush_ref[lane_part(c), :] = fold(dot(pick, split2(pending_ref[z.part(c), :])), 2) + fold(
            dot(lookups, grad), 2
        )
        send_chunk(z, c, copies, lambda b: owner_ref[b], flush_ref, out_hbm)
    copies.finish()


def next_kernel(z, t, place_ref, grad_hbm, ids_hbm, targets_hbm, cache_hbm, pending_hbm, count_hbm,
                pending_out, waiting_out, new_count_hbm, back_ref, flush_out, base_ref,
                grad_ref, sent_ref, key_ref, low_ref, ids_ref, targets_ref, cache_ref, pending_ref, count_ref, new_ref, sems):
    copies = Copies(sems)
    flush_ref, waiting_ref = (sent_ref, waiting_out) if t == 0 else (flush_out, sent_ref)
    ids_in = copies.start(ids_hbm.at[t + 1], ids_ref)
    cache_in = copies.start(cache_hbm, cache_ref)
    targets_in = copies.start(targets_hbm.at[t + 1], targets_ref)
    pending_in = copies.start(pending_hbm, pending_ref)
    count_in = copies.start(count_hbm, count_ref)
    grad_in = copies.start(grad_hbm, grad_ref)
    ids_in.wait()
    count_into(z, ids_ref[...], new_ref, key_ref, low_ref)
    copies.send(new_ref, new_count_hbm)
    cache_in.wait()
    total = jnp.zeros((z.bags, 2 * z.width), F32)
    for c in range(z.chunks):
        counts = new_ref[:, z.part(c)]
        pick = pick_of(z, place_ref, t, c)
        value = cache_ref[z.part(c), :]
        if t == 0:
            value = value * keep_of(z, pick)
        total = total + dot(counts, split2(value))
        back_ref[:, lane_part(c)] = dot_nt(counts, pick).astype(BF16)
        flush_ref[lane_part(c), :] = dot_nt(pick_of(z, place_ref, t + 1, c), counts).astype(BF16)
    targets_in.wait()
    base_ref[...] = fold(total, 2) * (1.0 / z.lookups) - targets_ref[...]
    if t == 0:
        copies.send(flush_ref, flush_out)
    grad_in.wait()
    pending_in.wait()
    count_in.wait()
    add_pending(z, t, place_ref, grad_ref, count_ref, pending_ref, waiting_ref)
    copies.send(pending_ref, pending_out)
    if t > 0:
        copies.send(waiting_ref, waiting_out)
    copies.finish()


def add_pending(z, t, place_ref, grad_ref, count_ref, pending_ref, waiting_ref):
    for c in range(z.chunks):
        added = fold(dot_tn(count_ref[:, z.part(c)], grad_ref[...]), 2)
        value = (pending_ref[z.part(c), :] + added) * keep_of(z, pick_of(z, place_ref, t, c))
        pending_ref[z.part(c), :] = value
        if waiting_ref is not None:
            waiting_ref[lane_part(c), :] = fold(dot(pick_of(z, place_ref, t + 1, c), split3(value)), 3)


def step_kernel(z, t, owner_ref, back_ref, counts_ref, base_ref, flush_counts, waiting,
                grad_hbm, out_hbm, grad_ref, order_ref, flush_ref, loaded_ref, sems):
    copies = Copies(sems)
    load = copies.start(flush_counts if t == 0 else waiting, loaded_ref)
    flush_counts_ref, waiting_ref = (loaded_ref, waiting) if t == 0 else (flush_counts, loaded_ref)
    from_owners(z, back_ref, owner_ref, order_ref)
    total = fold(dot(counts_ref[...], split2(order_ref[...])), 2)
    grad = split2((base_ref[...] + total * (1.0 / z.lookups)) * (1.0 / z.lookups))
    grad_ref[...] = grad
    copies.send(grad_ref, grad_hbm)
    load.wait()
    for c in range(z.chunks):
        part = lane_part(c)
        flush_ref[part, :] = waiting_ref[part, :] + fold(dot(flush_counts_ref[part, :], grad), 2)
        send_chunk(z, c, copies, lambda b: owner_ref[b], flush_ref, out_hbm)
    copies.finish()


def column(row):
    return jnp.transpose(jnp.broadcast_to(row, (LANES, LANES)))


def owner_kernel(z, t, far, got_ref, index_ref, accum_ref, old, answer_hbm, extra_hbm,
                 answer_ref, extra_ref, *rest):
    copies = Copies(rest[-1])
    old_ref = rest[0] if far else old
    if far:
        old_in = copies.start(old, old_ref)
    got = split2(got_ref[...])
    rows = [index_ref[t * z.chunks + c : t * z.chunks + c + 1, :].astype(F32) for c in range(z.chunks)]
    for c in range(z.chunks):
        part = lane_part(c)
        col = column(rows[c])
        same = jnp.concatenate([one(col == row) for row in rows], axis=1)
        grad = fold(dot(same, got), 2)
        extra = jnp.mean(grad * grad, axis=1, keepdims=True)
        fresh = column(accum_ref[c : c + 1, :]) + extra
        change = LEARN_RATE * grad / jnp.sqrt(fresh)
        extra_ref[part, :] = jnp.broadcast_to(extra, (LANES, LANES))
        copies.send(extra_ref.at[part, :], extra_hbm.at[part, :])
        if far:
            answer_ref[part, :] = change
        else:
            answer_ref[part, :] = old_ref[part, :] - change
            copies.send(answer_ref.at[part, :], answer_hbm.at[part, :])
    if far:
        old_in.wait()
        answer_ref[...] = old_ref[...] - answer_ref[...]
        copies.send(answer_ref, answer_hbm)
    copies.finish()


def gather_rows(z, t, flat_ref, table_ref, out_ref):
    def step(g, carry):
        base = pl.multiple_of(g * 32, 32)
        for k in range(32):
            row = flat_ref[t * z.chunks + (g >> 2), (g & 3) * 32 + k]
            out_ref[pl.ds(base + k, 1), :] = table_ref[pl.ds(row, 1), :]
        return carry

    lax.fori_loop(0, z.places // 32, step, 0)


def put_rows(z, t, flat_ref, answer_ref, table_ref):
    def step(g, carry):
        base = pl.multiple_of(g * 32, 32)
        for k in range(32):
            row = flat_ref[t * z.chunks + (g >> 2), (g & 3) * 32 + k]
            table_ref[pl.ds(row, 1), :] = answer_ref[pl.ds(base + k, 1), :]
        return carry

    lax.fori_loop(0, z.places // 32, step, 0)


def high_low(z, row):
    col = column(row)
    high = col >> 7 == iota((LANES, z.row_tiles), 1) if z.row_tiles == LANES else (
        col[:, : z.row_tiles] >> 7 == iota((LANES, z.row_tiles), 1)
    )
    return one(high), col & 127 == iota((LANES, LANES), 1)


def gather_accum(z, t, index_ref, accum, out_ref):
    parts = split3(accum)
    for c in range(z.chunks):
        now = t * z.chunks + c
        high, low = high_low(z, index_ref[now : now + 1, :])
        value = jnp.sum(jnp.where(low, fold(dot(high, parts), 3), 0.0), axis=1, keepdims=True)
        out_ref[c : c + 1, :] = jnp.transpose(jnp.broadcast_to(value, (LANES, LANES)))[0:1, :]


def put_accum(z, t, index_ref, accum, extra_ref):
    rows = [index_ref[t * z.chunks + c : t * z.chunks + c + 1, :] for c in range(z.chunks)]
    for i in range(z.chunks):
        col = column(rows[i])
        seen = jnp.where((col == rows[i]) & (iota((LANES, LANES), 1) < iota((LANES, LANES), 0)), 1.0, 0.0)
        for j in range(i):
            seen = jnp.where(col == rows[j], 1.0, seen)
        again = jnp.max(seen, axis=1, keepdims=True)
        high, low = high_low(z, rows[i])
        add = jnp.where(low & (again < 0.5), extra_ref[lane_part(i), :], 0.0)
        accum = accum + fold(dot_tn(high, split3(add)), 3)
    return accum


def start_kernel(z, tiles_ref, accum_ref, table_hbm, index_ref, old_accum_ref, old_ref, flat_ref, table_ref, sems):
    copies = Copies(sems)
    table_in = copies.start(table_hbm, table_ref)
    block = iota((8, LANES), 1) >> log2(z.cap)
    for c in range(z.chunks):
        index = jnp.zeros((8, LANES), I32)
        for j in range(z.chunk_blocks):
            b = c * z.chunk_blocks + j
            index = jnp.where(block == j, tiles_ref[b * 8 : (b + 1) * 8, :], index)
        for t in range(z.steps):
            index_ref[t * z.chunks + c : t * z.chunks + c + 1, :] = index[t : t + 1, :]
    flat_in = copies.start(index_ref, flat_ref)
    gather_accum(z, 0, index_ref, accum_ref[...], old_accum_ref)
    flat_in.wait()
    table_in.wait()
    gather_rows(z, 0, flat_ref, table_ref, old_ref)


def update_kernel(z, t, owner_ref, flat_ref, index_ref, accum_ref, place_ref, back_ref,
                  table_hbm, answer_hbm, extra_hbm, cache_hbm,
                  new_accum_ref, old_accum_ref, table_out, old, cache_out,
                  table_ref, answer_ref, extra_ref, cache_ref, order_ref, *rest):
    copies = Copies(rest[-1])
    last = t + 2 == z.steps
    old_ref = rest[0] if last else old
    answer_in = copies.start(answer_hbm, answer_ref)
    table_in = copies.start(table_hbm, table_ref)
    cache_in = copies.start(cache_hbm, cache_ref)
    extra_in = copies.start(extra_hbm, extra_ref)
    answer_in.wait()
    table_in.wait()
    put_rows(z, t, flat_ref, answer_ref, table_ref)
    copies.send(table_ref, table_out)
    gather_rows(z, t + 1, flat_ref, table_ref, old_ref)
    if last:
        copies.send(old_ref, old)
    extra_in.wait()
    accum = put_accum(z, t, index_ref, accum_ref[...], extra_ref)
    new_accum_ref[...] = accum
    gather_accum(z, t + 1, index_ref, accum, old_accum_ref)
    from_owners(z, back_ref, owner_ref, order_ref)
    cache_in.wait()
    new_ref = cache_out if last else cache_ref
    for c in range(z.chunks):
        pick = pick_of(z, place_ref, t, c)
        value = cache_ref[z.part(c), :]
        if t == 0:
            value = value * keep_of(z, pick)
        value = value + fold(dot_tn(pick, split3(order_ref[lane_part(c), :])), 3)
        new_ref[z.part(c), :] = value * keep_of(z, pick_of(z, place_ref, t + 1, c))
    if not last:
        copies.send(cache_ref, cache_out)
    copies.finish()


def last_update_kernel(z, flat_ref, index_ref, accum_ref, place_ref, grad_hbm,
                       table_hbm, answer_hbm, extra_hbm, pending_hbm, count_hbm,
                       new_accum_ref, table_out, pending_out,
                       grad_ref, table_ref, answer_ref, extra_ref, pending_ref, count_ref, sems):
    t = z.steps - 1
    copies = Copies(sems)
    answer_in = copies.start(answer_hbm, answer_ref)
    table_in = copies.start(table_hbm, table_ref)
    extra_in = copies.start(extra_hbm, extra_ref)
    count_in = copies.start(count_hbm, count_ref)
    pending_in = copies.start(pending_hbm, pending_ref)
    grad_in = copies.start(grad_hbm, grad_ref)
    answer_in.wait()
    table_in.wait()
    put_rows(z, t, flat_ref, answer_ref, table_ref)
    copies.send(table_ref, table_out)
    extra_in.wait()
    new_accum_ref[...] = put_accum(z, t, index_ref, accum_ref[...], extra_ref)
    grad_in.wait()
    count_in.wait()
    pending_in.wait()
    add_pending(z, t, place_ref, grad_ref, count_ref, pending_ref, None)
    copies.send(pending_ref, pending_out)
    copies.finish()


def last_cache_kernel(z, owner_ref, back_ref, place_ref, cache_ref, cache_out, order_ref, new_ref, sems):
    t = z.steps - 1
    copies = Copies(sems)
    from_owners(z, back_ref, owner_ref, order_ref)
    for c in range(z.chunks):
        pick = pick_of(z, place_ref, t, c)
        new_ref[z.part(c), :] = cache_ref[z.part(c), :] + fold(
            dot_tn(pick, split2(order_ref[lane_part(c), :])), 2
        )
        copies.send(new_ref.at[z.part(c), :], cache_out.at[z.part(c), :])
    copies.finish()


def body(table, accum, cache, cache_rows, pending, batch_slots, targets, dirty):
    z = Sizes(
        lax.axis_size(AXES), table.shape[0], cache.shape[0], cache.shape[1],
        batch_slots.shape[0], batch_slots.shape[1], batch_slots.shape[2], dirty.shape[1],
    )
    ids = batch_slots.transpose(0, 2, 1)
    wide, slots = z.wide, (z.slots, z.width)
    count, grads = ((z.bags, z.slots), BF16), ((z.bags, 2 * z.width), BF16)
    accums = ((z.row_tiles, LANES), F32)
    big = 2 * z.bags * z.slots * 2 * z.width

    def buf(shape, dtype=F32):
        return pltpu.VMEM(shape, dtype)

    def exchange(values):
        values = values.reshape(z.devices, z.cap, z.width)
        return lax.all_to_all(values, AXES, split_axis=0, concat_axis=0, tiled=True).reshape(wide)

    owner, place, tiles = call(
        functools.partial(place_kernel, z), [ANY] * 3,
        [((z.devices,), I32, SMEM), ((z.steps * z.chunks, z.chunk), F32, VMEM), ((z.devices * 8, LANES), I32, ANY)],
        scratch=[pltpu.SMEM((z.slots,), I32), buf((z.slots // LANES, LANES), I32), buf(dirty.shape, I32),
                 buf((z.devices * 8, LANES), I32)],
        copies=4, flops=10**9, nbytes=2**20, name="place",
    )(cache_rows, cache_rows.reshape(-1, LANES), dirty)

    tiles = lax.all_to_all(tiles.reshape(z.devices, 8, LANES), AXES, split_axis=0, concat_axis=0, tiled=True)
    tiles = tiles.reshape(-1, LANES)
    grad, counts, outgoing = call(
        functools.partial(first_kernel, z), [SMEM, VMEM, VMEM] + [ANY] * 3, [(*grads, ANY), (*count, ANY), (wide, F32, ANY)],
        scratch=[buf(*grads)] + count_scratch(z) + [
            buf(targets.shape[1:]), buf(slots), buf(slots), buf(*count), buf(wide)],
        copies=5 + z.devices, flops=6 * big, nbytes=2**24, name="first",
    )(owner, place, ids, targets, cache, pending)
    got = exchange(outgoing)
    accum = accum.reshape(accums[0])

    index, old_accum, old = call(
        functools.partial(start_kernel, z), [VMEM, VMEM, ANY],
        [((z.steps * z.chunks, LANES), I32, VMEM), ((z.chunks, LANES), F32, VMEM), (wide, F32, VMEM)],
        scratch=[pltpu.SMEM((z.steps * z.chunks, LANES), I32), buf(table.shape)], copies=2, flops=10**9,
        nbytes=2**23, name="start",
    )(tiles, accum, table)
    flat = index

    for t in range(z.steps):
        far = t == z.steps - 1
        answer, extra = call(
            functools.partial(owner_kernel, z, t, far), [VMEM] * 3 + [ANY if far else VMEM],
            [(wide, F32, ANY), (wide, F32, ANY)],
            scratch=[buf(wide)] * (3 if far else 2), copies=2 + 2 * z.chunks, flops=10**9, nbytes=2**21,
            vmem=24, name="owner",
        )(got, index, old_accum, old)
        answer, extra, grad = lax.optimization_barrier((answer, extra, grad))
        back = exchange(answer)
        if t == z.steps - 1:
            break
        early, late = (VMEM, ANY) if t == 0 else (ANY, VMEM)
        sent = buf((z.places, z.bags), BF16) if t == 0 else buf(wide)
        pending, waiting, counts, back_counts, flush_counts, base = call(
            functools.partial(next_kernel, z, t), [VMEM, ANY, ANY, ANY, ANY, ANY, ANY],
            [(slots, F32, ANY), (wide, F32, early), (*count, ANY), ((z.bags, z.places), BF16, VMEM),
             ((z.places, z.bags), BF16, late), ((z.bags, z.width), F32, VMEM)],
            scratch=[buf(*grads), sent] + count_scratch(z) + [
                buf(ids.shape[1:], I32), buf(targets.shape[1:]), buf(slots), buf(slots), buf(*count), buf(*count)],
            copies=9, flops=8 * big, nbytes=2**24, name="next",
        )(place, grad, ids, targets, cache, pending, counts)
        grad, outgoing = call(
            functools.partial(step_kernel, z, t), [SMEM, VMEM, VMEM, VMEM, late, early],
            [(*grads, ANY), (wide, F32, ANY)],
            scratch=[buf(*grads), buf(wide), buf(wide), sent], copies=2 + z.devices, flops=10**9, nbytes=2**22, vmem=24, name="step",
        )(owner, back, back_counts, base, flush_counts, waiting)
        outgoing, back, answer = lax.optimization_barrier((outgoing, back, answer))
        got = exchange(outgoing)
        accum, old_accum, table, old, cache = call(
            functools.partial(update_kernel, z, t), [SMEM, SMEM, VMEM, VMEM, VMEM, VMEM, ANY, ANY, ANY, ANY],
            [(*accums, VMEM), ((z.chunks, LANES), F32, VMEM), (table.shape, F32, ANY), (wide, F32, ANY if t + 2 == z.steps else VMEM),
             (slots, F32, VMEM if t + 2 == z.steps else ANY)],
            scratch=[buf(table.shape), buf(wide), buf(wide), buf(slots), buf(wide)]
            + ([buf(wide)] if t + 2 == z.steps else []),
            copies=7, flops=3 * big, nbytes=2**24, name="update",
        )(owner, flat, index, accum, place, back, table, answer, extra, cache)
    accum, table, pending = call(
        functools.partial(last_update_kernel, z), [SMEM, VMEM, VMEM, VMEM] + [ANY] * 6,
        [(*accums, VMEM), (table.shape, F32, ANY), (slots, F32, ANY)],
        scratch=[buf(*grads), buf(table.shape), buf(wide), buf(wide), buf(slots), buf(*count)],
        copies=8, flops=3 * big, nbytes=2**24, name="last_update",
    )(flat, index, accum, place, grad, table, answer, extra, pending, counts)
    cache = call(
        functools.partial(last_cache_kernel, z), [SMEM, VMEM, VMEM, VMEM], [(slots, F32, ANY)],
        scratch=[buf(wide), buf(slots)], copies=z.chunks, flops=big, nbytes=2**22, vmem=24, name="last_cache",
    )(owner, back, place, cache)[0]
    return (table, accum.reshape(-1), cache, pending)


def solution(mesh):
    in_specs = (
        P(AXES, None),
        P(AXES),
        P(AXES, None),
        P(AXES),
        P(AXES, None),
        P(None, AXES, None),
        P(None, AXES, None),
        P(None, AXES),
    )
    out_specs = (P(AXES, None), P(AXES), P(AXES, None), P(AXES, None))
    return jax.shard_map(body, mesh=mesh, in_specs=in_specs, out_specs=out_specs, check_vma=False)
```

```python
import functools

import jax
import jax.numpy as jnp
from jax import lax
from jax.experimental import pallas as pl
from jax.experimental.pallas import tpu as pltpu
from jax.sharding import PartitionSpec as P

LEARN_RATE = 0.3
AXES = ("gx", "gy")
F32, BF16, I32 = jnp.float32, jnp.bfloat16, jnp.int32
LANES = 128
VMEM = pl.BlockSpec(memory_space=pltpu.VMEM)
SMEM = pl.BlockSpec(memory_space=pltpu.SMEM)
ANY = pl.BlockSpec(memory_space=pl.ANY)


def call(body, ins, outs, scratch=(), copies=0, flops=0, nbytes=0, vmem=40, name=None):
    kernel = pl.pallas_call(
        body,
        out_shape=tuple(pltpu.HBM(shape, dtype) if memory is ANY else jax.ShapeDtypeStruct(shape, dtype) for shape, dtype, memory in outs),
        in_specs=list(ins),
        out_specs=tuple(memory for _, _, memory in outs),
        scratch_shapes=list(scratch) + ([pltpu.SemaphoreType.DMA((copies,))] if copies else []),
        compiler_params=pltpu.CompilerParams(vmem_limit_bytes=vmem * 2**20),
        cost_estimate=pl.CostEstimate(flops=flops, bytes_accessed=nbytes, transcendentals=0),
        name=name,
    )

    def run(*operands):
        return kernel(*(
            pltpu.with_memory_space_constraint(x, pltpu.HBM) if memory is ANY else x
            for x, memory in zip(operands, ins)
        ))

    return run


def log2(value):
    assert value & (value - 1) == 0
    return value.bit_length() - 1


def iota(shape, dim):
    return lax.broadcasted_iota(I32, shape, dim)


def one(mask):
    return jnp.where(mask, 1.0, 0.0).astype(BF16)


def split2(x):
    top = x.astype(BF16)
    rest = (x - top.astype(F32)).astype(BF16)
    return jnp.concatenate([top, rest], axis=-1)


def split3(x):
    top = x.astype(BF16)
    rest = x - top.astype(F32)
    middle = rest.astype(BF16)
    last = (rest - middle.astype(F32)).astype(BF16)
    return jnp.concatenate([top, middle, last], axis=-1)


def dot(a, b):
    return lax.dot_general(a, b, (((1,), (0,)), ((), ())), preferred_element_type=F32)


def dot_nt(a, b):
    return lax.dot_general(a, b, (((1,), (1,)), ((), ())), preferred_element_type=F32)


def dot_tn(a, b):
    return lax.dot_general(a, b, (((0,), (0,)), ((), ())), preferred_element_type=F32)


def fold(x, parts):
    width = x.shape[-1] // parts
    total = x[..., (parts - 1) * width :]
    for part in reversed(range(parts - 1)):
        total = total + x[..., part * width : (part + 1) * width]
    return total


class Sizes:
    def __init__(self, devices, rows, slots, width, steps, bags, lookups, listed):
        self.devices, self.rows, self.slots, self.width = devices, rows, slots, width
        self.steps, self.bags, self.lookups, self.listed = steps, bags, lookups, listed
        self.cap = 2 * listed // devices
        self.places = devices * self.cap
        self.block = slots // devices
        self.chunks = self.places // LANES
        self.chunk = slots // self.chunks
        self.chunk_blocks = devices // self.chunks
        self.group = 256 // lookups
        self.groups = bags // self.group
        self.row_tiles = rows // LANES
        self.wide = (self.places, width)
        assert LANES % self.cap == 0 and self.steps * self.cap < LANES
        assert width == LANES and self.cap % 8 == 0 and self.chunk % self.block == 0
        assert self.groups * self.group == bags and self.group % 16 == 0
        assert slots // 256 * self.group <= 256 and self.row_tiles <= LANES

    def part(self, c):
        return slice(c * self.chunk, (c + 1) * self.chunk)


def lane_part(c):
    return slice(c * LANES, (c + 1) * LANES)


class Copies:
    def __init__(self, sems):
        self.sems, self.used, self.open = sems, 0, []

    def start(self, source, target):
        copy = pltpu.make_async_copy(source, target, self.sems.at[self.used])
        self.used += 1
        copy.start()
        return copy

    def send(self, source, target):
        self.open.append(self.start(source, target))

    def finish(self):
        for copy in self.open:
            copy.wait()


def place_of(z, dirty_ref, place_ref):
    earlier = iota((z.chunk, z.chunk), 0)
    later = iota((z.chunk, z.chunk), 1)
    shift = log2(z.block)
    before = one((earlier < later) & ((earlier >> shift) == (later >> shift)))
    base = ((iota((z.chunks, z.chunk), 1) >> shift) * z.cap).astype(F32)
    for t in range(z.steps):
        listed = dirty_ref[t : t + 1, :]
        high, low = listed >> log2(z.chunk), listed & (z.chunk - 1)
        chosen_high = one(iota((z.chunks, z.listed), 0) == high)
        chosen_low = one(iota((z.chunk, z.listed), 0) == low)
        chosen = dot_nt(chosen_high, chosen_low)
        rank = dot(chosen.astype(BF16), before)
        place_ref[t * z.chunks : (t + 1) * z.chunks, :] = jnp.where(chosen > 0.5, base + rank, -1.0)


def pick_of(z, place_ref, t, c):
    row = t * z.chunks + c
    return one(iota((LANES, z.chunk), 0).astype(F32) == place_ref[row : row + 1, :])


def keep_of(z, pick):
    return 1.0 - dot_tn(pick, jnp.ones((LANES, LANES), BF16))


def count_into(z, ids, count_ref, key_ref, low_ref):
    lanes = z.group * z.lookups
    spread = one((iota((z.lookups, lanes), 1) & (z.lookups - 1)) == iota((z.lookups, lanes), 0))
    bag_of_lane = iota((z.bags, lanes), 1) >> log2(z.lookups)
    mine = bag_of_lane == (iota((z.bags, lanes), 0) & (z.group - 1))
    high = dot_tn((ids >> 8).astype(F32).astype(BF16), spread)
    low = dot_tn((ids & 255).astype(F32).astype(BF16), spread)
    key = high * z.group + bag_of_lane.astype(F32)
    key_ref[...] = jnp.sum(jnp.where(mine, key, 0.0).reshape(z.groups, z.group, lanes), axis=1)
    low_ref[...] = jnp.sum(jnp.where(mine, low, 0.0).reshape(z.groups, z.group, lanes), axis=1)
    tiles = z.slots // 256
    for g in range(z.groups):
        key_row = key_ref[g : g + 1, :].astype(I32)
        low_row = low_ref[g : g + 1, :].astype(I32)
        left = one(iota((tiles * z.group, lanes), 0) == key_row)
        right = one(iota((256, lanes), 0) == low_row)
        counts = dot_nt(left, right).astype(BF16)
        for h in range(tiles):
            count_ref[g * z.group : (g + 1) * z.group, h * 256 : (h + 1) * 256] = counts[
                h * z.group : (h + 1) * z.group, :
            ]


def count_scratch(z):
    lanes = z.group * z.lookups
    return [pltpu.VMEM((z.groups, lanes), F32), pltpu.VMEM((z.groups, lanes), F32)]


def send_chunk(z, c, copies, owner, values_ref, out_ref):
    for b in range(c * z.chunk_blocks, (c + 1) * z.chunk_blocks):
        start = pl.multiple_of(owner(b) * z.cap, z.cap)
        copies.send(values_ref.at[b * z.cap : (b + 1) * z.cap, :], out_ref.at[pl.ds(start, z.cap), :])


def from_owners(z, back_ref, owner_ref, out_ref):
    for b in range(z.devices):
        start = pl.multiple_of(owner_ref[b] * z.cap, z.cap)
        out_ref[b * z.cap : (b + 1) * z.cap, :] = back_ref[pl.ds(start, z.cap), :]


def place_kernel(z, rows_hbm, tiled_hbm, dirty_hbm, owner_ref, place_ref, tiles_hbm,
                 rows_ref, tiled_ref, dirty_ref, tiles_ref, sems):
    copies = Copies(sems)
    dirty_in = copies.start(dirty_hbm, dirty_ref)
    tiled_in = copies.start(tiled_hbm, tiled_ref)
    rows_in = copies.start(rows_hbm, rows_ref)
    dirty_in.wait()
    place_of(z, dirty_ref, place_ref)
    tiled_in.wait()
    rows_in.wait()
    tiles_ref[...] = jnp.zeros_like(tiles_ref)
    local = tiled_ref[...] & (z.rows - 1)
    pieces = z.chunk // LANES
    blocks = z.chunk_blocks
    block = iota((1, z.chunk), 1) >> log2(z.block)
    start = (block * z.cap).astype(F32)
    which = iota((2 * blocks, z.chunk), 0)
    own = (which & (blocks - 1)) == block
    place_in_block = iota((z.cap, z.chunk), 0).astype(F32)
    spare = jnp.zeros((LANES - z.steps * z.cap, z.chunk), F32)
    for c in range(z.chunks):
        row = jnp.concatenate([local[c * pieces + k : c * pieces + k + 1, :] for k in range(pieces)], axis=1)
        parts = jnp.where(own, jnp.where(which < blocks, row >> 7, row & 127), 0).astype(F32).astype(BF16)
        picks = []
        for t in range(z.steps):
            place = place_ref[t * z.chunks + c : t * z.chunks + c + 1, :]
            picks.append(jnp.where(place_in_block == place - start, jnp.where(place >= 0.0, 1.0, 0.0), 0.0))
        found = dot_nt(parts, jnp.concatenate(picks + [spare], axis=0).astype(BF16))
        index = (found[:blocks, :] * 128.0 + found[blocks:, :]).astype(I32)
        for j in range(blocks):
            b = c * blocks + j
            owner = rows_ref[b * z.block] >> log2(z.rows)
            owner_ref[b] = owner
            tiles_ref[pl.ds(pl.multiple_of(owner * 8, 8), 1), :] = index[j : j + 1, :]
    copies.send(tiles_ref, tiles_hbm)
    copies.finish()


def first_kernel(z, owner_ref, place_ref, ids_ref, targets_hbm, cache_hbm, pending_hbm,
                 grad_hbm, count_hbm, out_hbm,
                 grad_ref, key_ref, low_ref, targets_ref, cache_ref, pending_ref, count_ref, flush_ref, sems):
    copies = Copies(sems)
    cache_in = copies.start(cache_hbm, cache_ref)
    targets_in = copies.start(targets_hbm.at[0], targets_ref)
    pending_in = copies.start(pending_hbm, pending_ref)
    count_into(z, ids_ref[0], count_ref, key_ref, low_ref)
    copies.send(count_ref, count_hbm)
    targets_in.wait()
    cache_in.wait()
    total = jnp.zeros((z.bags, 2 * z.width), F32)
    for c in range(z.chunks):
        total = total + dot(count_ref[:, z.part(c)], split2(cache_ref[z.part(c), :]))
    pooled = fold(total, 2) * (1.0 / z.lookups)
    grad = split2((pooled - targets_ref[...]) * (1.0 / z.lookups))
    grad_ref[...] = grad
    copies.send(grad_ref, grad_hbm)
    pending_in.wait()
    for c in range(z.chunks):
        pick = pick_of(z, place_ref, 0, c)
        lookups = dot_nt(pick, count_ref[:, z.part(c)]).astype(BF16)
        flush_ref[lane_part(c), :] = fold(dot(pick, split2(pending_ref[z.part(c), :])), 2) + fold(
            dot(lookups, grad), 2
        )
        send_chunk(z, c, copies, lambda b: owner_ref[b], flush_ref, out_hbm)
    copies.finish()


def next_kernel(z, t, place_ref, grad_hbm, ids_hbm, targets_hbm, cache_hbm, pending_hbm, count_hbm,
                pending_out, waiting_out, new_count_hbm, back_ref, flush_out, base_ref,
                grad_ref, sent_ref, key_ref, low_ref, ids_ref, targets_ref, cache_ref, pending_ref, count_ref, new_ref, sems):
    copies = Copies(sems)
    flush_ref, waiting_ref = (sent_ref, waiting_out) if t == 0 else (flush_out, sent_ref)
    ids_in = copies.start(ids_hbm.at[t + 1], ids_ref)
    cache_in = copies.start(cache_hbm, cache_ref)
    targets_in = copies.start(targets_hbm.at[t + 1], targets_ref)
    pending_in = copies.start(pending_hbm, pending_ref)
    count_in = copies.start(count_hbm, count_ref)
    grad_in = copies.start(grad_hbm, grad_ref)
    ids_in.wait()
    count_into(z, ids_ref[...], new_ref, key_ref, low_ref)
    copies.send(new_ref, new_count_hbm)
    cache_in.wait()
    total = jnp.zeros((z.bags, 2 * z.width), F32)
    for c in range(z.chunks):
        counts = new_ref[:, z.part(c)]
        pick = pick_of(z, place_ref, t, c)
        value = cache_ref[z.part(c), :]
        if t == 0:
            value = value * keep_of(z, pick)
        total = total + dot(counts, split2(value))
        back_ref[:, lane_part(c)] = dot_nt(counts, pick).astype(BF16)
        flush_ref[lane_part(c), :] = dot_nt(pick_of(z, place_ref, t + 1, c), counts).astype(BF16)
    targets_in.wait()
    base_ref[...] = fold(total, 2) * (1.0 / z.lookups) - targets_ref[...]
    if t == 0:
        copies.send(flush_ref, flush_out)
    grad_in.wait()
    pending_in.wait()
    count_in.wait()
    add_pending(z, t, place_ref, grad_ref, count_ref, pending_ref, waiting_ref)
    copies.send(pending_ref, pending_out)
    if t > 0:
        copies.send(waiting_ref, waiting_out)
    copies.finish()


def add_pending(z, t, place_ref, grad_ref, count_ref, pending_ref, waiting_ref):
    for c in range(z.chunks):
        added = fold(dot_tn(count_ref[:, z.part(c)], grad_ref[...]), 2)
        value = (pending_ref[z.part(c), :] + added) * keep_of(z, pick_of(z, place_ref, t, c))
        pending_ref[z.part(c), :] = value
        if waiting_ref is not None:
            waiting_ref[lane_part(c), :] = fold(dot(pick_of(z, place_ref, t + 1, c), split3(value)), 3)


def step_kernel(z, t, owner_ref, back_ref, counts_ref, base_ref, flush_counts, waiting,
                grad_hbm, out_hbm, grad_ref, order_ref, flush_ref, loaded_ref, sems):
    copies = Copies(sems)
    load = copies.start(flush_counts if t == 0 else waiting, loaded_ref)
    flush_counts_ref, waiting_ref = (loaded_ref, waiting) if t == 0 else (flush_counts, loaded_ref)
    from_owners(z, back_ref, owner_ref, order_ref)
    total = fold(dot(counts_ref[...], split2(order_ref[...])), 2)
    grad = split2((base_ref[...] + total * (1.0 / z.lookups)) * (1.0 / z.lookups))
    grad_ref[...] = grad
    copies.send(grad_ref, grad_hbm)
    load.wait()
    for c in range(z.chunks):
        part = lane_part(c)
        flush_ref[part, :] = waiting_ref[part, :] + fold(dot(flush_counts_ref[part, :], grad), 2)
        send_chunk(z, c, copies, lambda b: owner_ref[b], flush_ref, out_hbm)
    copies.finish()


def column(row):
    return jnp.transpose(jnp.broadcast_to(row, (LANES, LANES)))


def owner_kernel(z, t, far, got_ref, index_ref, accum_ref, old, answer_hbm, extra_hbm,
                 answer_ref, extra_ref, *rest):
    copies = Copies(rest[-1])
    old_ref = rest[0] if far else old
    if far:
        old_in = copies.start(old, old_ref)
    got = split2(got_ref[...])
    rows = [index_ref[t * z.chunks + c : t * z.chunks + c + 1, :].astype(F32) for c in range(z.chunks)]
    for c in range(z.chunks):
        part = lane_part(c)
        col = column(rows[c])
        same = jnp.concatenate([one(col == row) for row in rows], axis=1)
        grad = fold(dot(same, got), 2)
        extra = jnp.mean(grad * grad, axis=1, keepdims=True)
        fresh = column(accum_ref[c : c + 1, :]) + extra
        change = LEARN_RATE * grad / jnp.sqrt(fresh)
        extra_ref[part, :] = jnp.broadcast_to(extra, (LANES, LANES))
        copies.send(extra_ref.at[part, :], extra_hbm.at[part, :])
        if far:
            answer_ref[part, :] = change
        else:
            answer_ref[part, :] = old_ref[part, :] - change
            copies.send(answer_ref.at[part, :], answer_hbm.at[part, :])
    if far:
        old_in.wait()
        answer_ref[...] = old_ref[...] - answer_ref[...]
        copies.send(answer_ref, answer_hbm)
    copies.finish()


def gather_rows(z, t, flat_ref, table_ref, out_ref):
    def step(g, carry):
        base = pl.multiple_of(g * 32, 32)
        for k in range(32):
            row = flat_ref[t * z.chunks + (g >> 2), (g & 3) * 32 + k]
            out_ref[pl.ds(base + k, 1), :] = table_ref[pl.ds(row, 1), :]
        return carry

    lax.fori_loop(0, z.places // 32, step, 0)


def put_rows(z, t, flat_ref, answer_ref, table_ref):
    def step(g, carry):
        base = pl.multiple_of(g * 32, 32)
        for k in range(32):
            row = flat_ref[t * z.chunks + (g >> 2), (g & 3) * 32 + k]
            table_ref[pl.ds(row, 1), :] = answer_ref[pl.ds(base + k, 1), :]
        return carry

    lax.fori_loop(0, z.places // 32, step, 0)


def high_low(z, row):
    col = column(row)
    high = col >> 7 == iota((LANES, z.row_tiles), 1) if z.row_tiles == LANES else (
        col[:, : z.row_tiles] >> 7 == iota((LANES, z.row_tiles), 1)
    )
    return one(high), col & 127 == iota((LANES, LANES), 1)


def gather_accum(z, t, index_ref, accum, out_ref):
    parts = split3(accum)
    for c in range(z.chunks):
        now = t * z.chunks + c
        high, low = high_low(z, index_ref[now : now + 1, :])
        value = jnp.sum(jnp.where(low, fold(dot(high, parts), 3), 0.0), axis=1, keepdims=True)
        out_ref[c : c + 1, :] = jnp.transpose(jnp.broadcast_to(value, (LANES, LANES)))[0:1, :]


def put_accum(z, t, index_ref, accum, extra_ref):
    rows = [index_ref[t * z.chunks + c : t * z.chunks + c + 1, :] for c in range(z.chunks)]
    for i in range(z.chunks):
        col = column(rows[i])
        seen = jnp.where((col == rows[i]) & (iota((LANES, LANES), 1) < iota((LANES, LANES), 0)), 1.0, 0.0)
        for j in range(i):
            seen = jnp.where(col == rows[j], 1.0, seen)
        again = jnp.max(seen, axis=1, keepdims=True)
        high, low = high_low(z, rows[i])
        add = jnp.where(low & (again < 0.5), extra_ref[lane_part(i), :], 0.0)
        accum = accum + fold(dot_tn(high, split3(add)), 3)
    return accum


def start_kernel(z, tiles_ref, accum_ref, table_hbm, index_ref, old_accum_ref, old_ref, flat_ref, table_ref, sems):
    copies = Copies(sems)
    table_in = copies.start(table_hbm, table_ref)
    block = iota((8, LANES), 1) >> log2(z.cap)
    for c in range(z.chunks):
        for t in range(z.steps):
            index = jnp.zeros((1, LANES), I32)
            for j in range(z.chunk_blocks):
                b = c * z.chunk_blocks + j
                moved = pltpu.roll(tiles_ref[b * 8 : b * 8 + 1, :], (j - t) * z.cap % LANES, 1)
                index = jnp.where(block[0:1, :] == j, moved, index)
            index_ref[t * z.chunks + c : t * z.chunks + c + 1, :] = index
    flat_in = copies.start(index_ref, flat_ref)
    gather_accum(z, 0, index_ref, accum_ref[...], old_accum_ref)
    flat_in.wait()
    table_in.wait()
    gather_rows(z, 0, flat_ref, table_ref, old_ref)


def update_kernel(z, t, owner_ref, flat_ref, index_ref, accum_ref, place_ref, back_ref,
                  table_hbm, answer_hbm, extra_hbm, cache_hbm,
                  new_accum_ref, old_accum_ref, table_out, old, cache_out,
                  table_ref, answer_ref, extra_ref, cache_ref, order_ref, *rest):
    copies = Copies(rest[-1])
    last = t + 2 == z.steps
    old_ref = rest[0] if last else old
    answer_in = copies.start(answer_hbm, answer_ref)
    table_in = copies.start(table_hbm, table_ref)
    cache_in = copies.start(cache_hbm, cache_ref)
    extra_in = copies.start(extra_hbm, extra_ref)
    answer_in.wait()
    table_in.wait()
    put_rows(z, t, flat_ref, answer_ref, table_ref)
    copies.send(table_ref, table_out)
    gather_rows(z, t + 1, flat_ref, table_ref, old_ref)
    if last:
        copies.send(old_ref, old)
    extra_in.wait()
    accum = put_accum(z, t, index_ref, accum_ref[...], extra_ref)
    new_accum_ref[...] = accum
    gather_accum(z, t + 1, index_ref, accum, old_accum_ref)
    from_owners(z, back_ref, owner_ref, order_ref)
    cache_in.wait()
    new_ref = cache_out if last else cache_ref
    for c in range(z.chunks):
        pick = pick_of(z, place_ref, t, c)
        value = cache_ref[z.part(c), :]
        if t == 0:
            value = value * keep_of(z, pick)
        value = value + fold(dot_tn(pick, split3(order_ref[lane_part(c), :])), 3)
        new_ref[z.part(c), :] = value * keep_of(z, pick_of(z, place_ref, t + 1, c))
    if not last:
        copies.send(cache_ref, cache_out)
    copies.finish()


def last_update_kernel(z, flat_ref, index_ref, accum_ref, place_ref, grad_hbm,
                       table_hbm, answer_hbm, extra_hbm, pending_hbm, count_hbm,
                       new_accum_ref, table_out, pending_out,
                       grad_ref, table_ref, answer_ref, extra_ref, pending_ref, count_ref, sems):
    t = z.steps - 1
    copies = Copies(sems)
    answer_in = copies.start(answer_hbm, answer_ref)
    table_in = copies.start(table_hbm, table_ref)
    extra_in = copies.start(extra_hbm, extra_ref)
    count_in = copies.start(count_hbm, count_ref)
    pending_in = copies.start(pending_hbm, pending_ref)
    grad_in = copies.start(grad_hbm, grad_ref)
    answer_in.wait()
    table_in.wait()
    put_rows(z, t, flat_ref, answer_ref, table_ref)
    copies.send(table_ref, table_out)
    extra_in.wait()
    new_accum_ref[...] = put_accum(z, t, index_ref, accum_ref[...], extra_ref)
    grad_in.wait()
    count_in.wait()
    pending_in.wait()
    add_pending(z, t, place_ref, grad_ref, count_ref, pending_ref, None)
    copies.send(pending_ref, pending_out)
    copies.finish()


def last_cache_kernel(z, owner_ref, back_ref, place_ref, cache_ref, cache_out, order_ref, new_ref, sems):
    t = z.steps - 1
    copies = Copies(sems)
    from_owners(z, back_ref, owner_ref, order_ref)
    for c in range(z.chunks):
        pick = pick_of(z, place_ref, t, c)
        new_ref[z.part(c), :] = cache_ref[z.part(c), :] + fold(
            dot_tn(pick, split2(order_ref[lane_part(c), :])), 2
        )
        copies.send(new_ref.at[z.part(c), :], cache_out.at[z.part(c), :])
    copies.finish()


def body(table, accum, cache, cache_rows, pending, batch_slots, targets, dirty):
    z = Sizes(
        lax.axis_size(AXES), table.shape[0], cache.shape[0], cache.shape[1],
        batch_slots.shape[0], batch_slots.shape[1], batch_slots.shape[2], dirty.shape[1],
    )
    ids = batch_slots.transpose(0, 2, 1)
    wide, slots = z.wide, (z.slots, z.width)
    count, grads = ((z.bags, z.slots), BF16), ((z.bags, 2 * z.width), BF16)
    accums = ((z.row_tiles, LANES), F32)
    big = 2 * z.bags * z.slots * 2 * z.width

    def buf(shape, dtype=F32):
        return pltpu.VMEM(shape, dtype)

    def exchange(values):
        values = values.reshape(z.devices, z.cap, z.width)
        return lax.all_to_all(values, AXES, split_axis=0, concat_axis=0, tiled=True).reshape(wide)

    owner, place, tiles = call(
        functools.partial(place_kernel, z), [ANY] * 3,
        [((z.devices,), I32, SMEM), ((z.steps * z.chunks, z.chunk), F32, VMEM), ((z.devices * 8, LANES), I32, ANY)],
        scratch=[pltpu.SMEM((z.slots,), I32), buf((z.slots // LANES, LANES), I32), buf(dirty.shape, I32),
                 buf((z.devices * 8, LANES), I32)],
        copies=4, flops=10**9, nbytes=2**20, name="place",
    )(cache_rows, cache_rows.reshape(-1, LANES), dirty)

    tiles = lax.all_to_all(tiles.reshape(z.devices, 8, LANES), AXES, split_axis=0, concat_axis=0, tiled=True)
    tiles = tiles.reshape(-1, LANES)
    grad, counts, outgoing = call(
        functools.partial(first_kernel, z), [SMEM, VMEM, VMEM] + [ANY] * 3, [(*grads, ANY), (*count, ANY), (wide, F32, ANY)],
        scratch=[buf(*grads)] + count_scratch(z) + [
            buf(targets.shape[1:]), buf(slots), buf(slots), buf(*count), buf(wide)],
        copies=5 + z.devices, flops=6 * big, nbytes=2**24, name="first",
    )(owner, place, ids, targets, cache, pending)
    got = exchange(outgoing)
    accum = accum.reshape(accums[0])

    index, old_accum, old = call(
        functools.partial(start_kernel, z), [VMEM, VMEM, ANY],
        [((z.steps * z.chunks, LANES), I32, VMEM), ((z.chunks, LANES), F32, VMEM), (wide, F32, VMEM)],
        scratch=[pltpu.SMEM((z.steps * z.chunks, LANES), I32), buf(table.shape)], copies=2, flops=10**9,
        nbytes=2**23, name="start",
    )(tiles, accum, table)
    flat = index

    for t in range(z.steps):
        far = t == z.steps - 1
        answer, extra = call(
            functools.partial(owner_kernel, z, t, far), [VMEM] * 3 + [ANY if far else VMEM],
            [(wide, F32, ANY), (wide, F32, ANY)],
            scratch=[buf(wide)] * (3 if far else 2), copies=2 + 2 * z.chunks, flops=10**9, nbytes=2**21,
            vmem=24, name="owner",
        )(got, index, old_accum, old)
        answer, extra, grad = lax.optimization_barrier((answer, extra, grad))
        back = exchange(answer)
        if t == z.steps - 1:
            break
        early, late = (VMEM, ANY) if t == 0 else (ANY, VMEM)
        sent = buf((z.places, z.bags), BF16) if t == 0 else buf(wide)
        pending, waiting, counts, back_counts, flush_counts, base = call(
            functools.partial(next_kernel, z, t), [VMEM, ANY, ANY, ANY, ANY, ANY, ANY],
            [(slots, F32, ANY), (wide, F32, early), (*count, ANY), ((z.bags, z.places), BF16, VMEM),
             ((z.places, z.bags), BF16, late), ((z.bags, z.width), F32, VMEM)],
            scratch=[buf(*grads), sent] + count_scratch(z) + [
                buf(ids.shape[1:], I32), buf(targets.shape[1:]), buf(slots), buf(slots), buf(*count), buf(*count)],
            copies=9, flops=8 * big, nbytes=2**24, name="next",
        )(place, grad, ids, targets, cache, pending, counts)
        grad, outgoing = call(
            functools.partial(step_kernel, z, t), [SMEM, VMEM, VMEM, VMEM, late, early],
            [(*grads, ANY), (wide, F32, ANY)],
            scratch=[buf(*grads), buf(wide), buf(wide), sent], copies=2 + z.devices, flops=10**9, nbytes=2**22, vmem=24, name="step",
        )(owner, back, back_counts, base, flush_counts, waiting)
        outgoing, back, answer = lax.optimization_barrier((outgoing, back, answer))
        got = exchange(outgoing)
        accum, old_accum, table, old, cache = call(
            functools.partial(update_kernel, z, t), [SMEM, SMEM, VMEM, VMEM, VMEM, VMEM, ANY, ANY, ANY, ANY],
            [(*accums, VMEM), ((z.chunks, LANES), F32, VMEM), (table.shape, F32, ANY), (wide, F32, ANY if t + 2 == z.steps else VMEM),
             (slots, F32, VMEM if t + 2 == z.steps else ANY)],
            scratch=[buf(table.shape), buf(wide), buf(wide), buf(slots), buf(wide)]
            + ([buf(wide)] if t + 2 == z.steps else []),
            copies=7, flops=3 * big, nbytes=2**24, name="update",
        )(owner, flat, index, accum, place, back, table, answer, extra, cache)
    accum, table, pending = call(
        functools.partial(last_update_kernel, z), [SMEM, VMEM, VMEM, VMEM] + [ANY] * 6,
        [(*accums, VMEM), (table.shape, F32, ANY), (slots, F32, ANY)],
        scratch=[buf(*grads), buf(table.shape), buf(wide), buf(wide), buf(slots), buf(*count)],
        copies=8, flops=3 * big, nbytes=2**24, name="last_update",
    )(flat, index, accum, place, grad, table, answer, extra, pending, counts)
    cache = call(
        functools.partial(last_cache_kernel, z), [SMEM, VMEM, VMEM, VMEM], [(slots, F32, ANY)],
        scratch=[buf(wide), buf(slots)], copies=z.chunks, flops=big, nbytes=2**22, vmem=24, name="last_cache",
    )(owner, back, place, cache)[0]
    return (table, accum.reshape(-1), cache, pending)


def solution(mesh):
    in_specs = (
        P(AXES, None),
        P(AXES),
        P(AXES, None),
        P(AXES),
        P(AXES, None),
        P(None, AXES, None),
        P(None, AXES, None),
        P(None, AXES),
    )
    out_specs = (P(AXES, None), P(AXES), P(AXES, None), P(AXES, None))
    return jax.shard_map(body, mesh=mesh, in_specs=in_specs, out_specs=out_specs, check_vma=False)
```

```python
import functools

import jax
import jax.numpy as jnp
from jax import lax
from jax.experimental import pallas as pl
from jax.experimental.pallas import tpu as pltpu
from jax.sharding import PartitionSpec as P

LEARN_RATE = 0.3
AXES = ("gx", "gy")
F32, BF16, I32 = jnp.float32, jnp.bfloat16, jnp.int32
LANES = 128
VMEM = pl.BlockSpec(memory_space=pltpu.VMEM)
SMEM = pl.BlockSpec(memory_space=pltpu.SMEM)
ANY = pl.BlockSpec(memory_space=pl.ANY)


def call(body, ins, outs, scratch=(), copies=0, flops=0, nbytes=0, vmem=40, name=None):
    kernel = pl.pallas_call(
        body,
        out_shape=tuple(pltpu.HBM(shape, dtype) if memory is ANY else jax.ShapeDtypeStruct(shape, dtype) for shape, dtype, memory in outs),
        in_specs=list(ins),
        out_specs=tuple(memory for _, _, memory in outs),
        scratch_shapes=list(scratch) + ([pltpu.SemaphoreType.DMA((copies,))] if copies else []),
        compiler_params=pltpu.CompilerParams(vmem_limit_bytes=vmem * 2**20),
        cost_estimate=pl.CostEstimate(flops=flops, bytes_accessed=nbytes, transcendentals=0),
        name=name,
    )

    def run(*operands):
        return kernel(*(
            pltpu.with_memory_space_constraint(x, pltpu.HBM) if memory is ANY else x
            for x, memory in zip(operands, ins)
        ))

    return run


def log2(value):
    assert value & (value - 1) == 0
    return value.bit_length() - 1


def iota(shape, dim):
    return lax.broadcasted_iota(I32, shape, dim)


def one(mask):
    return jnp.where(mask, 1.0, 0.0).astype(BF16)


def split2(x):
    top = x.astype(BF16)
    rest = (x - top.astype(F32)).astype(BF16)
    return jnp.concatenate([top, rest], axis=-1)


def split3(x):
    top = x.astype(BF16)
    rest = x - top.astype(F32)
    middle = rest.astype(BF16)
    last = (rest - middle.astype(F32)).astype(BF16)
    return jnp.concatenate([top, middle, last], axis=-1)


def dot(a, b):
    return lax.dot_general(a, b, (((1,), (0,)), ((), ())), preferred_element_type=F32)


def dot_nt(a, b):
    return lax.dot_general(a, b, (((1,), (1,)), ((), ())), preferred_element_type=F32)


def dot_tn(a, b):
    return lax.dot_general(a, b, (((0,), (0,)), ((), ())), preferred_element_type=F32)


def fold(x, parts):
    width = x.shape[-1] // parts
    total = x[..., (parts - 1) * width :]
    for part in reversed(range(parts - 1)):
        total = total + x[..., part * width : (part + 1) * width]
    return total


class Sizes:
    def __init__(self, devices, rows, slots, width, steps, bags, lookups, listed):
        self.devices, self.rows, self.slots, self.width = devices, rows, slots, width
        self.steps, self.bags, self.lookups, self.listed = steps, bags, lookups, listed
        self.cap = 2 * listed // devices
        self.places = devices * self.cap
        self.block = slots // devices
        self.chunks = self.places // LANES
        self.chunk = slots // self.chunks
        self.chunk_blocks = devices // self.chunks
        self.group = 256 // lookups
        self.groups = bags // self.group
        self.row_tiles = rows // LANES
        self.wide = (self.places, width)
        assert LANES % self.cap == 0 and self.steps * self.cap < LANES
        assert width == LANES and self.cap % 8 == 0 and self.chunk % self.block == 0
        assert self.groups * self.group == bags and self.group % 16 == 0
        assert slots // 256 * self.group <= 256 and self.row_tiles <= LANES

    def part(self, c):
        return slice(c * self.chunk, (c + 1) * self.chunk)


def lane_part(c):
    return slice(c * LANES, (c + 1) * LANES)


class Copies:
    def __init__(self, sems):
        self.sems, self.used, self.open = sems, 0, []

    def start(self, source, target):
        copy = pltpu.make_async_copy(source, target, self.sems.at[self.used])
        self.used += 1
        copy.start()
        return copy

    def send(self, source, target):
        self.open.append(self.start(source, target))

    def finish(self):
        for copy in self.open:
            copy.wait()


def place_of(z, dirty_ref, place_ref):
    earlier = iota((z.chunk, z.chunk), 0)
    later = iota((z.chunk, z.chunk), 1)
    shift = log2(z.block)
    before = one((earlier < later) & ((earlier >> shift) == (later >> shift)))
    base = ((iota((z.chunks, z.chunk), 1) >> shift) * z.cap).astype(F32)
    for t in range(z.steps):
        listed = dirty_ref[t : t + 1, :]
        high, low = listed >> log2(z.chunk), listed & (z.chunk - 1)
        chosen_high = one(iota((z.chunks, z.listed), 0) == high)
        chosen_low = one(iota((z.chunk, z.listed), 0) == low)
        chosen = dot_nt(chosen_high, chosen_low)
        rank = dot(chosen.astype(BF16), before)
        place_ref[t * z.chunks : (t + 1) * z.chunks, :] = jnp.where(chosen > 0.5, base + rank, -1.0)


def pick_of(z, place_ref, t, c):
    row = t * z.chunks + c
    return one(iota((LANES, z.chunk), 0).astype(F32) == place_ref[row : row + 1, :])


def keep_of(z, pick):
    return 1.0 - dot_tn(pick, jnp.ones((LANES, LANES), BF16))


def count_into(z, ids, count_ref, key_ref, low_ref):
    lanes = z.group * z.lookups
    spread = one((iota((z.lookups, lanes), 1) & (z.lookups - 1)) == iota((z.lookups, lanes), 0))
    bag_of_lane = iota((z.bags, lanes), 1) >> log2(z.lookups)
    mine = bag_of_lane == (iota((z.bags, lanes), 0) & (z.group - 1))
    high = dot_tn((ids >> 8).astype(F32).astype(BF16), spread)
    low = dot_tn((ids & 255).astype(F32).astype(BF16), spread)
    key = high * z.group + bag_of_lane.astype(F32)
    key_ref[...] = jnp.sum(jnp.where(mine, key, 0.0).reshape(z.groups, z.group, lanes), axis=1)
    low_ref[...] = jnp.sum(jnp.where(mine, low, 0.0).reshape(z.groups, z.group, lanes), axis=1)
    tiles = z.slots // 256
    for g in range(z.groups):
        key_row = key_ref[g : g + 1, :].astype(I32)
        low_row = low_ref[g : g + 1, :].astype(I32)
        left = one(iota((tiles * z.group, lanes), 0) == key_row)
        right = one(iota((256, lanes), 0) == low_row)
        counts = dot_nt(left, right).astype(BF16)
        for h in range(tiles):
            count_ref[g * z.group : (g + 1) * z.group, h * 256 : (h + 1) * 256] = counts[
                h * z.group : (h + 1) * z.group, :
            ]


def count_scratch(z):
    lanes = z.group * z.lookups
    return [pltpu.VMEM((z.groups, lanes), F32), pltpu.VMEM((z.groups, lanes), F32)]


def send_chunk(z, c, copies, owner, values_ref, out_ref):
    for b in range(c * z.chunk_blocks, (c + 1) * z.chunk_blocks):
        start = pl.multiple_of(owner(b) * z.cap, z.cap)
        copies.send(values_ref.at[b * z.cap : (b + 1) * z.cap, :], out_ref.at[pl.ds(start, z.cap), :])


def from_owners(z, back_ref, owner_ref, out_ref):
    for b in range(z.devices):
        start = pl.multiple_of(owner_ref[b] * z.cap, z.cap)
        out_ref[b * z.cap : (b + 1) * z.cap, :] = back_ref[pl.ds(start, z.cap), :]


def place_kernel(z, rows_hbm, tiled_hbm, dirty_hbm, owner_ref, place_ref, tiles_hbm,
                 rows_ref, tiled_ref, dirty_ref, tiles_ref, sems):
    copies = Copies(sems)
    dirty_in = copies.start(dirty_hbm, dirty_ref)
    tiled_in = copies.start(tiled_hbm, tiled_ref)
    rows_in = copies.start(rows_hbm, rows_ref)
    dirty_in.wait()
    place_of(z, dirty_ref, place_ref)
    tiled_in.wait()
    rows_in.wait()
    tiles_ref[...] = jnp.zeros_like(tiles_ref)
    local = tiled_ref[...] & (z.rows - 1)
    pieces = z.chunk // LANES
    blocks = z.chunk_blocks
    block = iota((1, z.chunk), 1) >> log2(z.block)
    start = (block * z.cap).astype(F32)
    which = iota((2 * blocks, z.chunk), 0)
    own = (which & (blocks - 1)) == block
    place_in_block = iota((z.cap, z.chunk), 0).astype(F32)
    spare = jnp.zeros((LANES - z.steps * z.cap, z.chunk), F32)
    for c in range(z.chunks):
        row = jnp.concatenate([local[c * pieces + k : c * pieces + k + 1, :] for k in range(pieces)], axis=1)
        parts = jnp.where(own, jnp.where(which < blocks, row >> 7, row & 127), 0).astype(F32).astype(BF16)
        picks = []
        for t in range(z.steps):
            place = place_ref[t * z.chunks + c : t * z.chunks + c + 1, :]
            picks.append(jnp.where(place_in_block == place - start, jnp.where(place >= 0.0, 1.0, 0.0), 0.0))
        found = dot_nt(parts, jnp.concatenate(picks + [spare], axis=0).astype(BF16))
        index = (found[:blocks, :] * 128.0 + found[blocks:, :]).astype(I32)
        for j in range(blocks):
            b = c * blocks + j
            owner = rows_ref[b * z.block] >> log2(z.rows)
            owner_ref[b] = owner
            tiles_ref[pl.ds(pl.multiple_of(owner * 8, 8), 1), :] = index[j : j + 1, :]
    copies.send(tiles_ref, tiles_hbm)
    copies.finish()


def first_kernel(z, owner_ref, place_ref, ids_ref, targets_hbm, cache_hbm, pending_hbm,
                 grad_hbm, count_hbm, out_hbm,
                 grad_ref, key_ref, low_ref, targets_ref, cache_ref, pending_ref, count_ref, flush_ref, sems):
    copies = Copies(sems)
    cache_in = copies.start(cache_hbm, cache_ref)
    targets_in = copies.start(targets_hbm.at[0], targets_ref)
    pending_in = copies.start(pending_hbm, pending_ref)
    count_into(z, ids_ref[0], count_ref, key_ref, low_ref)
    copies.send(count_ref, count_hbm)
    targets_in.wait()
    cache_in.wait()
    total = jnp.zeros((z.bags, 2 * z.width), F32)
    for c in range(z.chunks):
        total = total + dot(count_ref[:, z.part(c)], split2(cache_ref[z.part(c), :]))
    pooled = fold(total, 2) * (1.0 / z.lookups)
    grad = split2((pooled - targets_ref[...]) * (1.0 / z.lookups))
    grad_ref[...] = grad
    copies.send(grad_ref, grad_hbm)
    pending_in.wait()
    for c in range(z.chunks):
        pick = pick_of(z, place_ref, 0, c)
        lookups = dot_nt(pick, count_ref[:, z.part(c)]).astype(BF16)
        flush_ref[lane_part(c), :] = fold(dot(pick, split2(pending_ref[z.part(c), :])), 2) + fold(
            dot(lookups, grad), 2
        )
        send_chunk(z, c, copies, lambda b: owner_ref[b], flush_ref, out_hbm)
    copies.finish()


def next_kernel(z, t, place_ref, grad_hbm, ids_hbm, targets_hbm, cache_hbm, pending_hbm, count_hbm,
                pending_out, waiting_out, new_count_hbm, back_ref, flush_out, base_ref,
                grad_ref, sent_ref, key_ref, low_ref, ids_ref, targets_ref, cache_ref, pending_ref, count_ref, new_ref, sems):
    copies = Copies(sems)
    flush_ref, waiting_ref = (sent_ref, waiting_out) if t == 0 else (flush_out, sent_ref)
    ids_in = copies.start(ids_hbm.at[t + 1], ids_ref)
    cache_in = copies.start(cache_hbm, cache_ref)
    targets_in = copies.start(targets_hbm.at[t + 1], targets_ref)
    pending_in = copies.start(pending_hbm, pending_ref)
    count_in = copies.start(count_hbm, count_ref)
    grad_in = copies.start(grad_hbm, grad_ref)
    ids_in.wait()
    count_into(z, ids_ref[...], new_ref, key_ref, low_ref)
    copies.send(new_ref, new_count_hbm)
    cache_in.wait()
    total = jnp.zeros((z.bags, 2 * z.width), F32)
    for c in range(z.chunks):
        counts = new_ref[:, z.part(c)]
        pick = pick_of(z, place_ref, t, c)
        value = cache_ref[z.part(c), :]
        if t == 0:
            value = value * keep_of(z, pick)
        total = total + dot(counts, split2(value))
        back_ref[:, lane_part(c)] = dot_nt(counts, pick).astype(BF16)
        flush_ref[lane_part(c), :] = dot_nt(pick_of(z, place_ref, t + 1, c), counts).astype(BF16)
    targets_in.wait()
    base_ref[...] = fold(total, 2) * (1.0 / z.lookups) - targets_ref[...]
    if t == 0:
        copies.send(flush_ref, flush_out)
    grad_in.wait()
    pending_in.wait()
    count_in.wait()
    add_pending(z, t, place_ref, grad_ref, count_ref, pending_ref, waiting_ref)
    copies.send(pending_ref, pending_out)
    if t > 0:
        copies.send(waiting_ref, waiting_out)
    copies.finish()


def add_pending(z, t, place_ref, grad_ref, count_ref, pending_ref, waiting_ref):
    for c in range(z.chunks):
        added = fold(dot_tn(count_ref[:, z.part(c)], grad_ref[...]), 2)
        value = (pending_ref[z.part(c), :] + added) * keep_of(z, pick_of(z, place_ref, t, c))
        pending_ref[z.part(c), :] = value
        if waiting_ref is not None:
            waiting_ref[lane_part(c), :] = fold(dot(pick_of(z, place_ref, t + 1, c), split3(value)), 3)


def step_kernel(z, t, owner_ref, back_ref, counts_ref, base_ref, flush_counts, waiting,
                grad_hbm, out_hbm, grad_ref, order_ref, flush_ref, loaded_ref, sems):
    copies = Copies(sems)
    load = copies.start(flush_counts if t == 0 else waiting, loaded_ref)
    flush_counts_ref, waiting_ref = (loaded_ref, waiting) if t == 0 else (flush_counts, loaded_ref)
    from_owners(z, back_ref, owner_ref, order_ref)
    total = fold(dot(counts_ref[...], split2(order_ref[...])), 2)
    grad = split2((base_ref[...] + total * (1.0 / z.lookups)) * (1.0 / z.lookups))
    grad_ref[...] = grad
    copies.send(grad_ref, grad_hbm)
    load.wait()
    for c in range(z.chunks):
        part = lane_part(c)
        flush_ref[part, :] = waiting_ref[part, :] + fold(dot(flush_counts_ref[part, :], grad), 2)
        send_chunk(z, c, copies, lambda b: owner_ref[b], flush_ref, out_hbm)
    copies.finish()


def column(row):
    return jnp.transpose(jnp.broadcast_to(row, (LANES, LANES)))


def owner_kernel(z, t, far, got_ref, index_ref, accum_ref, old, answer_hbm, extra_hbm,
                 answer_ref, extra_ref, *rest):
    copies = Copies(rest[-1])
    old_ref = rest[0] if far else old
    if far:
        old_in = copies.start(old, old_ref)
    got = split2(got_ref[...])
    rows = [index_ref[t * z.chunks + c : t * z.chunks + c + 1, :].astype(F32) for c in range(z.chunks)]
    for c in range(z.chunks):
        part = lane_part(c)
        col = column(rows[c])
        same = jnp.concatenate([one(col == row) for row in rows], axis=1)
        grad = fold(dot(same, got), 2)
        extra = jnp.mean(grad * grad, axis=1, keepdims=True)
        fresh = column(accum_ref[c : c + 1, :]) + extra
        change = LEARN_RATE * grad / jnp.sqrt(fresh)
        extra_ref[part, :] = jnp.broadcast_to(extra, (LANES, LANES))
        copies.send(extra_ref.at[part, :], extra_hbm.at[part, :])
        if far:
            answer_ref[part, :] = change
        else:
            answer_ref[part, :] = old_ref[part, :] - change
            copies.send(answer_ref.at[part, :], answer_hbm.at[part, :])
    if far:
        old_in.wait()
        for c in range(z.chunks):
            part = lane_part(c)
            answer_ref[part, :] = old_ref[part, :] - answer_ref[part, :]
            copies.send(answer_ref.at[part, :], answer_hbm.at[part, :])
    copies.finish()


def gather_rows(z, t, flat_ref, table_ref, out_ref):
    def step(g, carry):
        base = pl.multiple_of(g * 32, 32)
        for k in range(32):
            row = flat_ref[t * z.chunks + (g >> 2), (g & 3) * 32 + k]
            out_ref[pl.ds(base + k, 1), :] = table_ref[pl.ds(row, 1), :]
        return carry

    lax.fori_loop(0, z.places // 32, step, 0)


def put_rows(z, t, flat_ref, answer_ref, table_ref):
    def step(g, carry):
        base = pl.multiple_of(g * 32, 32)
        for k in range(32):
            row = flat_ref[t * z.chunks + (g >> 2), (g & 3) * 32 + k]
            table_ref[pl.ds(row, 1), :] = answer_ref[pl.ds(base + k, 1), :]
        return carry

    lax.fori_loop(0, z.places // 32, step, 0)


def high_low(z, row):
    col = column(row)
    high = col >> 7 == iota((LANES, z.row_tiles), 1) if z.row_tiles == LANES else (
        col[:, : z.row_tiles] >> 7 == iota((LANES, z.row_tiles), 1)
    )
    return one(high), col & 127 == iota((LANES, LANES), 1)


def gather_accum(z, t, index_ref, accum, out_ref):
    parts = split3(accum)
    for c in range(z.chunks):
        now = t * z.chunks + c
        high, low = high_low(z, index_ref[now : now + 1, :])
        value = jnp.sum(jnp.where(low, fold(dot(high, parts), 3), 0.0), axis=1, keepdims=True)
        out_ref[c : c + 1, :] = jnp.transpose(jnp.broadcast_to(value, (LANES, LANES)))[0:1, :]


def put_accum(z, t, index_ref, accum, extra_ref):
    rows = [index_ref[t * z.chunks + c : t * z.chunks + c + 1, :] for c in range(z.chunks)]
    for i in range(z.chunks):
        col = column(rows[i])
        seen = jnp.where((col == rows[i]) & (iota((LANES, LANES), 1) < iota((LANES, LANES), 0)), 1.0, 0.0)
        for j in range(i):
            seen = jnp.where(col == rows[j], 1.0, seen)
        again = jnp.max(seen, axis=1, keepdims=True)
        high, low = high_low(z, rows[i])
        add = jnp.where(low & (again < 0.5), extra_ref[lane_part(i), :], 0.0)
        accum = accum + fold(dot_tn(high, split3(add)), 3)
    return accum


def start_kernel(z, tiles_ref, accum_ref, table_hbm, index_ref, old_accum_ref, old_ref, flat_ref, table_ref, sems):
    copies = Copies(sems)
    table_in = copies.start(table_hbm, table_ref)
    block = iota((8, LANES), 1) >> log2(z.cap)
    for c in range(z.chunks):
        for t in range(z.steps):
            index = jnp.zeros((1, LANES), I32)
            for j in range(z.chunk_blocks):
                b = c * z.chunk_blocks + j
                moved = pltpu.roll(tiles_ref[b * 8 : b * 8 + 1, :], (j - t) * z.cap % LANES, 1)
                index = jnp.where(block[0:1, :] == j, moved, index)
            index_ref[t * z.chunks + c : t * z.chunks + c + 1, :] = index
    flat_in = copies.start(index_ref, flat_ref)
    gather_accum(z, 0, index_ref, accum_ref[...], old_accum_ref)
    flat_in.wait()
    table_in.wait()
    gather_rows(z, 0, flat_ref, table_ref, old_ref)


def update_kernel(z, t, owner_ref, flat_ref, index_ref, accum_ref, place_ref, back_ref,
                  table_hbm, answer_hbm, extra_hbm, cache_hbm,
                  new_accum_ref, old_accum_ref, table_out, old, cache_out,
                  table_ref, answer_ref, extra_ref, cache_ref, order_ref, *rest):
    copies = Copies(rest[-1])
    last = t + 2 == z.steps
    old_ref = rest[0] if last else old
    answer_in = copies.start(answer_hbm, answer_ref)
    table_in = copies.start(table_hbm, table_ref)
    cache_in = copies.start(cache_hbm, cache_ref)
    extra_in = copies.start(extra_hbm, extra_ref)
    answer_in.wait()
    table_in.wait()
    put_rows(z, t, flat_ref, answer_ref, table_ref)
    copies.send(table_ref, table_out)
    gather_rows(z, t + 1, flat_ref, table_ref, old_ref)
    if last:
        copies.send(old_ref, old)
    extra_in.wait()
    accum = put_accum(z, t, index_ref, accum_ref[...], extra_ref)
    new_accum_ref[...] = accum
    gather_accum(z, t + 1, index_ref, accum, old_accum_ref)
    from_owners(z, back_ref, owner_ref, order_ref)
    cache_in.wait()
    new_ref = cache_out if last else cache_ref
    for c in range(z.chunks):
        pick = pick_of(z, place_ref, t, c)
        value = cache_ref[z.part(c), :]
        if t == 0:
            value = value * keep_of(z, pick)
        value = value + fold(dot_tn(pick, split3(order_ref[lane_part(c), :])), 3)
        new_ref[z.part(c), :] = value * keep_of(z, pick_of(z, place_ref, t + 1, c))
    if not last:
        copies.send(cache_ref, cache_out)
    copies.finish()


def last_update_kernel(z, flat_ref, index_ref, accum_ref, place_ref, grad_hbm,
                       table_hbm, answer_hbm, extra_hbm, pending_hbm, count_hbm,
                       new_accum_ref, table_out, pending_out,
                       grad_ref, table_ref, answer_ref, extra_ref, pending_ref, count_ref, sems):
    t = z.steps - 1
    copies = Copies(sems)
    answer_in = copies.start(answer_hbm, answer_ref)
    table_in = copies.start(table_hbm, table_ref)
    extra_in = copies.start(extra_hbm, extra_ref)
    count_in = copies.start(count_hbm, count_ref)
    pending_in = copies.start(pending_hbm, pending_ref)
    grad_in = copies.start(grad_hbm, grad_ref)
    answer_in.wait()
    table_in.wait()
    put_rows(z, t, flat_ref, answer_ref, table_ref)
    copies.send(table_ref, table_out)
    extra_in.wait()
    new_accum_ref[...] = put_accum(z, t, index_ref, accum_ref[...], extra_ref)
    grad_in.wait()
    count_in.wait()
    pending_in.wait()
    add_pending(z, t, place_ref, grad_ref, count_ref, pending_ref, None)
    copies.send(pending_ref, pending_out)
    copies.finish()


def last_cache_kernel(z, owner_ref, back_ref, place_ref, cache_ref, cache_out, order_ref, new_ref, sems):
    t = z.steps - 1
    copies = Copies(sems)
    from_owners(z, back_ref, owner_ref, order_ref)
    for c in range(z.chunks):
        pick = pick_of(z, place_ref, t, c)
        new_ref[z.part(c), :] = cache_ref[z.part(c), :] + fold(
            dot_tn(pick, split2(order_ref[lane_part(c), :])), 2
        )
        copies.send(new_ref.at[z.part(c), :], cache_out.at[z.part(c), :])
    copies.finish()


def body(table, accum, cache, cache_rows, pending, batch_slots, targets, dirty):
    z = Sizes(
        lax.axis_size(AXES), table.shape[0], cache.shape[0], cache.shape[1],
        batch_slots.shape[0], batch_slots.shape[1], batch_slots.shape[2], dirty.shape[1],
    )
    ids = batch_slots.transpose(0, 2, 1)
    wide, slots = z.wide, (z.slots, z.width)
    count, grads = ((z.bags, z.slots), BF16), ((z.bags, 2 * z.width), BF16)
    accums = ((z.row_tiles, LANES), F32)
    big = 2 * z.bags * z.slots * 2 * z.width

    def buf(shape, dtype=F32):
        return pltpu.VMEM(shape, dtype)

    def exchange(values):
        values = values.reshape(z.devices, z.cap, z.width)
        return lax.all_to_all(values, AXES, split_axis=0, concat_axis=0, tiled=True).reshape(wide)

    owner, place, tiles = call(
        functools.partial(place_kernel, z), [ANY] * 3,
        [((z.devices,), I32, SMEM), ((z.steps * z.chunks, z.chunk), F32, VMEM), ((z.devices * 8, LANES), I32, ANY)],
        scratch=[pltpu.SMEM((z.slots,), I32), buf((z.slots // LANES, LANES), I32), buf(dirty.shape, I32),
                 buf((z.devices * 8, LANES), I32)],
        copies=4, flops=10**9, nbytes=2**20, name="place",
    )(cache_rows, cache_rows.reshape(-1, LANES), dirty)

    tiles = lax.all_to_all(tiles.reshape(z.devices, 8, LANES), AXES, split_axis=0, concat_axis=0, tiled=True)
    tiles = tiles.reshape(-1, LANES)
    grad, counts, outgoing = call(
        functools.partial(first_kernel, z), [SMEM, VMEM, VMEM] + [ANY] * 3, [(*grads, ANY), (*count, ANY), (wide, F32, ANY)],
        scratch=[buf(*grads)] + count_scratch(z) + [
            buf(targets.shape[1:]), buf(slots), buf(slots), buf(*count), buf(wide)],
        copies=5 + z.devices, flops=6 * big, nbytes=2**24, name="first",
    )(owner, place, ids, targets, cache, pending)
    got = exchange(outgoing)
    accum = accum.reshape(accums[0])

    index, old_accum, old = call(
        functools.partial(start_kernel, z), [VMEM, VMEM, ANY],
        [((z.steps * z.chunks, LANES), I32, VMEM), ((z.chunks, LANES), F32, VMEM), (wide, F32, VMEM)],
        scratch=[pltpu.SMEM((z.steps * z.chunks, LANES), I32), buf(table.shape)], copies=2, flops=10**9,
        nbytes=2**23, name="start",
    )(tiles, accum, table)
    flat = index

    for t in range(z.steps):
        far = t == z.steps - 1
        answer, extra = call(
            functools.partial(owner_kernel, z, t, far), [VMEM] * 3 + [ANY if far else VMEM],
            [(wide, F32, ANY), (wide, F32, ANY)],
            scratch=[buf(wide)] * (3 if far else 2), copies=2 + 2 * z.chunks, flops=10**9, nbytes=2**21,
            vmem=24, name="owner",
        )(got, index, old_accum, old)
        answer, extra, grad = lax.optimization_barrier((answer, extra, grad))
        back = exchange(answer)
        if t == z.steps - 1:
            break
        early, late = (VMEM, ANY) if t == 0 else (ANY, VMEM)
        sent = buf((z.places, z.bags), BF16) if t == 0 else buf(wide)
        pending, waiting, counts, back_counts, flush_counts, base = call(
            functools.partial(next_kernel, z, t), [VMEM, ANY, ANY, ANY, ANY, ANY, ANY],
            [(slots, F32, ANY), (wide, F32, early), (*count, ANY), ((z.bags, z.places), BF16, VMEM),
             ((z.places, z.bags), BF16, late), ((z.bags, z.width), F32, VMEM)],
            scratch=[buf(*grads), sent] + count_scratch(z) + [
                buf(ids.shape[1:], I32), buf(targets.shape[1:]), buf(slots), buf(slots), buf(*count), buf(*count)],
            copies=9, flops=8 * big, nbytes=2**24, name="next",
        )(place, grad, ids, targets, cache, pending, counts)
        grad, outgoing = call(
            functools.partial(step_kernel, z, t), [SMEM, VMEM, VMEM, VMEM, late, early],
            [(*grads, ANY), (wide, F32, ANY)],
            scratch=[buf(*grads), buf(wide), buf(wide), sent], copies=2 + z.devices, flops=10**9, nbytes=2**22, vmem=24, name="step",
        )(owner, back, back_counts, base, flush_counts, waiting)
        outgoing, back, answer = lax.optimization_barrier((outgoing, back, answer))
        got = exchange(outgoing)
        accum, old_accum, table, old, cache = call(
            functools.partial(update_kernel, z, t), [SMEM, SMEM, VMEM, VMEM, VMEM, VMEM, ANY, ANY, ANY, ANY],
            [(*accums, VMEM), ((z.chunks, LANES), F32, VMEM), (table.shape, F32, ANY), (wide, F32, ANY if t + 2 == z.steps else VMEM),
             (slots, F32, VMEM if t + 2 == z.steps else ANY)],
            scratch=[buf(table.shape), buf(wide), buf(wide), buf(slots), buf(wide)]
            + ([buf(wide)] if t + 2 == z.steps else []),
            copies=7, flops=3 * big, nbytes=2**24, name="update",
        )(owner, flat, index, accum, place, back, table, answer, extra, cache)
    accum, table, pending = call(
        functools.partial(last_update_kernel, z), [SMEM, VMEM, VMEM, VMEM] + [ANY] * 6,
        [(*accums, VMEM), (table.shape, F32, ANY), (slots, F32, ANY)],
        scratch=[buf(*grads), buf(table.shape), buf(wide), buf(wide), buf(slots), buf(*count)],
        copies=8, flops=3 * big, nbytes=2**24, name="last_update",
    )(flat, index, accum, place, grad, table, answer, extra, pending, counts)
    cache = call(
        functools.partial(last_cache_kernel, z), [SMEM, VMEM, VMEM, VMEM], [(slots, F32, ANY)],
        scratch=[buf(wide), buf(slots)], copies=z.chunks, flops=big, nbytes=2**22, vmem=24, name="last_cache",
    )(owner, back, place, cache)[0]
    return (table, accum.reshape(-1), cache, pending)


def solution(mesh):
    in_specs = (
        P(AXES, None),
        P(AXES),
        P(AXES, None),
        P(AXES),
        P(AXES, None),
        P(None, AXES, None),
        P(None, AXES, None),
        P(None, AXES),
    )
    out_specs = (P(AXES, None), P(AXES), P(AXES, None), P(AXES, None))
    return jax.shard_map(body, mesh=mesh, in_specs=in_specs, out_specs=out_specs, check_vma=False)
```
